128 devices in a mesh: fsdp: 32 (over z, x_hi, y), tp: 4 (over x_lo, core).
Axes of the slice: x: 4 (x_hi: 2, x_lo: 2; x = x_hi * 2 + x_lo), y: 4, z: 4, core: 2. Of those that a mesh axis runs over, the one named last changes fastest.
Arguments:
- inputs: bfloat16 [16384, 1024], P(('fsdp', 'tp')), may hold values from -24 to 24
- segments: int32 [32, 512], P('fsdp'), may hold values from 0 to 3, never falling along the last dimension, each value on 1 to 400 neighbouring positions
- routes: int32 [16384, 8], P('fsdp'), may hold values from 0 to 31, all different within a row; in each aligned block of 128 rows (0 to 127, 128 to 255, ...) at most 33 rows name the same one
- query_weight: bfloat16 [1024, 1024], P('fsdp', 'tp'), may hold values from -0.25 to 0.25
- key_projection_weight: bfloat16 [1024, 512], P('fsdp', 'tp'), may hold values from -0.1875 to 0.1875
- value_projection_weight: bfloat16 [1024, 512], P('fsdp', 'tp'), may hold values from -0.1875 to 0.1875
- out_weight: bfloat16 [1024, 1024], P('tp', 'fsdp'), may hold values from -1.25 to 1.25
- router_weight: bfloat16 [1024, 32], P('fsdp'), may hold values from -0.09375 to 0.09375
- first_gain: bfloat16 [1024], P('fsdp'), may hold values from 0.5 to 1.5
- second_gain: bfloat16 [1024], P('fsdp'), may hold values from 0.5 to 1.5
- gate_weight: bfloat16 [32, 1024, 512], P(None, 'fsdp', 'tp'), may hold values from -0.1875 to 0.1875
- up_weight: bfloat16 [32, 1024, 512], P(None, 'fsdp', 'tp'), may hold values from -0.1875 to 0.1875
- down_weight: bfloat16 [32, 512, 1024], P(None, 'tp', 'fsdp'), may hold values from -1.25 to 1.25
- cotangent: bfloat16 [16384, 1024], P(('fsdp', 'tp')), may hold values from -24 to 24
Outputs:
- output: bfloat16 [16384, 1024], P(('fsdp', 'tp'))
- grad_inputs: float32 [16384, 1024], P(('fsdp', 'tp'))
- grad_query: float32 [1024, 1024], P('fsdp', 'tp')
- grad_key: float32 [1024, 512], P('fsdp', 'tp')
- grad_value: float32 [1024, 512], P('fsdp', 'tp')
- grad_out: float32 [1024, 1024], P('tp', 'fsdp')
- grad_router: float32 [1024, 32], P('fsdp')
- grad_first: float32 [1024], P('fsdp')
- grad_second: float32 [1024], P('fsdp')
- grad_gate: float32 [32, 1024, 512], P(None, 'fsdp', 'tp')
- grad_up: float32 [32, 1024, 512], P(None, 'fsdp', 'tp')
- grad_down: float32 [32, 512, 1024], P(None, 'tp', 'fsdp')
The draws below stay inside these ranges and needn't reach their ends.
Inputs may be any that keep to these rules, and one draw needn't show every extreme that they name: `segments`: each row is one sequence; its document numbers never fall, each document has 1 to 400 tokens, and one document of each row has exactly 400. `routes`: each row names 8 different experts. In each aligned block of rows held by one device, no expert is named by more than 33 rows, a bound that some block reaches.
All inputs are finite; a program needn't handle non-finite values.
Results may differ from the reference program's by a relative error of at most 0.029.
Values may be sent and summed in bfloat16 or wider, within the bound.
A program may use at most 192 MiB of HBM per device.

```python
import math
from functools import partial
import jax
import jax.numpy as jnp
import numpy as np
from jax import lax

MODEL_DIM = 1024
FF = 512
QUERY_HEAD_COUNT = 16
KEY_VALUE_HEADS = 8
HEAD_SIZE = 64
EXPERTS = 32
TOP = 8
LEN = 512
SEQS = 1
MOST_DOC = 400
CAP_DEV = 33
CAP = 132
SEQUENCES = 32
TOKENS = 16384
N_TP = 4


def with_spikes(values, key, source, target, parts, factor):
    def block_of(dim):
        return (jnp.arange(values.shape[dim]) // (values.shape[dim] // parts)).reshape((-1,) + (1,) * (values.ndim - 1 - dim))

    near = jax.random.permutation(key, parts)[block_of(target)]
    second = (block_of(target) + parts // 2) % parts
    return jnp.where((block_of(source) == near) | (block_of(source) == second), factor * values, values)


def level_of(own_key, extent, shards, low, top_value):
    factor_of, own = 1.0, jax.random.fold_in(own_key, 6)
    for axis_at, parts in shards:
        steps = jnp.exp(jax.random.uniform(jax.random.fold_in(own, axis_at), (parts,), jnp.float32, low / len(shards), top_value / len(shards)))
        factor_of = factor_of * jnp.repeat(steps, extent[axis_at] // parts).reshape([-1 if axis == axis_at else 1 for axis in range(len(extent))])
    return factor_of


def length_profile(count, total, limit, slope):
    loads = [(1 << 20) // math.isqrt(grade ** slope) + 1 for grade in range(2, count + 1)]
    spare, holding = total - limit - (count - 1), [1] * (count - 1)
    while spare > 0:
        free = [i for i in range(count - 1) if holding[i] < limit]
        whole, left = sum([loads[i] for i in free]), spare
        for i in free:
            more = min(limit - holding[i], max(1, left * loads[i] // whole), spare)
            holding[i] = holding[i] + more
            spare = spare - more
    return np.array([limit] + holding)


def ragged_sizes(stream_key, count, total, most, skew):
    if count == 2:
        one = jax.random.randint(stream_key, (), max(1, total - most), min(most, total - 1) + 1)
        return jnp.stack([one, total - one])
    tallies = jnp.asarray(length_profile(count, total, most, skew), jnp.int32)
    twos = (count - 1) // 2
    source_of, receiver = tallies[1:1 + 2 * twos:2], tallies[2:2 + 2 * twos:2]
    slack = jnp.minimum(source_of - 1, most - receiver)
    passed = jax.random.randint(jax.random.fold_in(stream_key, 1), (twos,), 0, 1 << 20) % (slack + 1)
    tallies = tallies.at[1:1 + 2 * twos:2].set(source_of - passed).at[2:2 + 2 * twos:2].set(receiver + passed)
    return tallies[jax.random.permutation(jax.random.fold_in(stream_key, 2), count)]


def deal_out(rng, own, number, rows, count, top, most, lean):
    order = jax.random.permutation(rng, count)
    crowded, common = portions_of(count, rows * top, most, lean, True), portions_of(count, rows * top, most, lean, False)
    places = jnp.arange(count)

    def named(tallies, offset_by):
        used = int((tallies > 0).sum())
        fixed = max(1, used // 4)
        moved = fixed + (places - fixed + offset_by * (used - fixed)) % max(1, count - fixed)
        return jnp.zeros((count,), jnp.int32).at[order[jnp.where(places < fixed, places, moved)]].set(jnp.asarray(tallies, jnp.int32))

    tallies = jnp.where(number % 4 == 0, named(crowded, number // 4), named(common, number - number // 4 - 1))
    mixed = jax.random.permutation(jax.random.fold_in(own, 3), count)
    donor, sink = mixed[0:count // 2 * 2:2], mixed[1:count // 2 * 2:2]
    margin = jnp.minimum(tallies[donor] - 1, most - tallies[sink]) // 2
    margin = jnp.where((donor == order[0]) | (sink == order[0]) | (tallies[sink] == 0), 0, jnp.maximum(margin, 0))
    moved = jax.random.randint(jax.random.fold_in(own, 4), (count // 2,), 0, 1 << 20) % (margin + 1)
    tallies = tallies.at[donor].add(-moved).at[sink].add(moved)
    members = jnp.searchsorted(jnp.cumsum(tallies), jnp.arange(rows * top), side="right").astype(jnp.int32)
    listing = members.reshape(top, rows).T
    listing = listing[jax.random.permutation(jax.random.fold_in(own, 1), rows)]
    offset_by = jax.random.randint(jax.random.fold_in(own, 2), (rows, 1), 0, top)
    return jnp.take_along_axis(listing, (jnp.arange(top)[None, :] + offset_by) % top, axis=1)


def portions_of(number_of, total, limit, slope, full):
    weights = [(1 << 20) // math.isqrt(rank ** slope) + 1 for rank in range(1, number_of + 1)]
    largest = limit if full else min(limit, max(-(-total // number_of), total * weights[0] // sum(weights)))
    least = 1 if total - largest >= number_of - 1 else 0
    given, spare = [largest] + [least] * (number_of - 1), total - largest - least * (number_of - 1)
    while spare > 0:
        free = [i for i in range(1, number_of) if given[i] < largest] or [i for i in range(1, number_of) if given[i] < limit]
        pool, left = sum([weights[i] for i in free]), spare
        for i in free:
            addition = min(limit - given[i], max(1, left * weights[i] // pool), spare)
            given[i] = given[i] + addition
            spare = spare - addition
    return np.array(given)


def bell_draw(own_key, extent, spread, most, cuts=(), kind=jnp.bfloat16):
    values = jax.random.normal(own_key, extent, jnp.float32) * spread
    if len(cuts) > 0:
        values = level_of(own_key, extent, cuts, -0.22, 0.18) * values
    return jnp.clip(values, min=-most, max=most).astype(kind)


def heavy_noise(rng, extent, width, most, split, heavy, kind=jnp.bfloat16):
    array = width * jax.random.normal(rng, extent, jnp.float32)
    if split:
        array = array * level_of(rng, extent, split, -0.22, 0.18)
    return jnp.clip(with_spikes(array, jax.random.fold_in(rng, 3), *heavy), -most, most).astype(kind)


def setup_inputs(seed: int = 0) -> dict:
    key_of = jax.random.split(jax.random.key(seed), 15)
    inputs = heavy_noise(key_of[0], (TOKENS, MODEL_DIM), 1.0, 24.0, ((0, 128),), (0, 1, 128, 5.5))
    segments = jax.vmap(lambda own: jnp.searchsorted(jnp.cumsum(ragged_sizes(own, 4, LEN, MOST_DOC, 0)), jnp.arange(LEN), side="right"))(jax.random.split(key_of[1], SEQUENCES)).reshape((SEQUENCES, LEN)).astype(jnp.int32)
    routes_keys = jax.random.split(jax.random.fold_in(key_of[2], 1), TOKENS // (SEQS * LEN // N_TP))
    routes_turns = jax.random.permutation(jax.random.fold_in(key_of[2], 3), TOKENS // (SEQS * LEN // N_TP))
    routes = jax.vmap(lambda own, number: deal_out(jax.random.fold_in(key_of[2], 2), own, number, SEQS * LEN // N_TP, EXPERTS, TOP, CAP_DEV, 0))(routes_keys, routes_turns).reshape((TOKENS, TOP))
    query_weight = bell_draw(key_of[3], (MODEL_DIM, QUERY_HEAD_COUNT * HEAD_SIZE), (MODEL_DIM * 4 // 9) ** -0.5, 0.25, ((0, 32), (1, 4)))
    key_projection_weight = bell_draw(key_of[4], (MODEL_DIM, KEY_VALUE_HEADS * HEAD_SIZE), MODEL_DIM ** -0.5, 0.1875, ((0, 32), (1, 4)))
    value_projection_weight = bell_draw(key_of[5], (MODEL_DIM, KEY_VALUE_HEADS * HEAD_SIZE), MODEL_DIM ** -0.5, 0.1875, ((0, 32), (1, 4)))
    out_weight = bell_draw(key_of[6], (QUERY_HEAD_COUNT * HEAD_SIZE, MODEL_DIM), (QUERY_HEAD_COUNT * HEAD_SIZE // 48) ** -0.5, 1.25, ((0, 4), (1, 32)))
    router_weight = bell_draw(key_of[7], (MODEL_DIM, EXPERTS), (MODEL_DIM * 4) ** -0.5, 0.09375, ((0, 32),))
    first_gain = jnp.clip(1.0 + 0.1 * jax.random.normal(key_of[8], (MODEL_DIM,), jnp.float32), 0.5, 1.5).astype(jnp.bfloat16)
    second_gain = jnp.clip(1.0 + 0.1 * jax.random.normal(key_of[9], (MODEL_DIM,), jnp.float32), 0.5, 1.5).astype(jnp.bfloat16)
    gate_weight = bell_draw(key_of[10], (EXPERTS, MODEL_DIM, FF), MODEL_DIM ** -0.5, 0.1875, ((1, 32), (2, 4)))
    up_weight = bell_draw(key_of[11], (EXPERTS, MODEL_DIM, FF), MODEL_DIM ** -0.5, 0.1875, ((1, 32), (2, 4)))
    down_weight = bell_draw(key_of[12], (EXPERTS, FF, MODEL_DIM), (FF // 20) ** -0.5, 1.25, ((1, 4), (2, 32)))
    cotangent = heavy_noise(key_of[13], (TOKENS, MODEL_DIM), 1.0, 24.0, ((0, 128),), (0, 1, 128, 5.5))
    return dict(inputs=inputs, segments=segments, routes=routes, query_weight=query_weight, key_projection_weight=key_projection_weight, value_projection_weight=value_projection_weight, out_weight=out_weight, router_weight=router_weight, first_gain=first_gain, second_gain=second_gain, gate_weight=gate_weight, up_weight=up_weight, down_weight=down_weight, cotangent=cotangent)


EPSILON = 1e-06
ROPE_BASE = 10000.0
MASKED = -1e+30
BEST_PRECISION = lax.Precision.HIGHEST

@jax.custom_vjp
def lower_precision(v):
    return lax.optimization_barrier(v.astype(jnp.bfloat16)).astype(jnp.float32)

@jax.custom_vjp
def lower_precision_back(v):
    return v

def low_keep(v):
    return (lower_precision(v), None)

def low_pass(kept, grad):
    return (grad,)

def back_keep(v):
    return (v, None)

def back_low(kept, grad):
    return (lower_precision(grad),)
lower_precision.defvjp(low_keep, low_pass)
lower_precision_back.defvjp(back_keep, back_low)

def normalize(values, gain_vec):
    return values * lax.rsqrt(lax.optimization_barrier(jnp.mean(values * values, axis=-1, keepdims=True)) + EPSILON) * gain_vec

def rope_tables(seg_ids):
    length_total = seg_ids.shape[-1]
    places = jnp.arange(length_total, dtype=jnp.int32)
    starts_new = jnp.concatenate([jnp.ones(seg_ids.shape[:-1] + (1,), dtype=jnp.bool_), seg_ids[..., 1:] != seg_ids[..., :-1]], axis=-1)
    doc_start = lax.cummax(jnp.where(starts_new, places, 0).astype(jnp.int32), axis=seg_ids.ndim - 1)
    position = (places - doc_start).astype(jnp.float32)
    halves = jnp.arange(HEAD_SIZE // 2, dtype=jnp.int32).astype(jnp.float32)
    rate_list = jnp.exp(halves * (-2.0 * math.log(ROPE_BASE) / HEAD_SIZE))
    angles = position[..., None] * rate_list
    return (jnp.cos(angles), jnp.sin(angles))

def rotary_apply(values, cosine_lookup, sine_lookup):
    half_dim = values.shape[-1] // 2
    front_half = values[..., :half_dim]
    back_half = values[..., half_dim:]
    cos_wide = cosine_lookup[..., None, :]
    sin_wide = sine_lookup[..., None, :]
    return jnp.concatenate([front_half * cos_wide - back_half * sin_wide, back_half * cos_wide + front_half * sin_wide], axis=-1)

def dispatch(route_ids):
    flat_ids = route_ids.reshape(-1).astype(jnp.int32)
    entry_count = flat_ids.shape[0]
    onehot = (flat_ids[:, None] == jnp.arange(EXPERTS, dtype=jnp.int32)[None, :]).astype(jnp.int32)
    earlier = jnp.cumsum(onehot, axis=0).astype(jnp.int32) - onehot
    slot_of = lax.optimization_barrier(jnp.sum(earlier * onehot, axis=1)).astype(jnp.int32)
    places = flat_ids * CAP + slot_of
    slot_table = jnp.full((EXPERTS * CAP,), entry_count, dtype=jnp.int32)
    slot_table = slot_table.at[places].set(jnp.arange(entry_count, dtype=jnp.int32))
    return slot_table.reshape(EXPERTS, CAP)

def attend_block(pieces, keys_seq, values_seq, seg_keys):
    block_of_queries, seg_query, offset = pieces
    rows_of_queries = block_of_queries.shape[0]
    grouped_heads = block_of_queries.reshape(rows_of_queries, KEY_VALUE_HEADS, QUERY_HEAD_COUNT // KEY_VALUE_HEADS, HEAD_SIZE)
    scores = jnp.einsum('qkgd,tkd->kgqt', grouped_heads, keys_seq, precision=BEST_PRECISION) * HEAD_SIZE ** (-0.5)
    scores = lower_precision_back(scores)
    query_place = offset + jnp.arange(rows_of_queries, dtype=jnp.int32)
    key_place = jnp.arange(keys_seq.shape[0], dtype=jnp.int32)
    allowed = (seg_query[:, None] == seg_keys[None, :]) & (query_place[:, None] >= key_place[None, :])
    scores = jnp.where(allowed, scores, MASKED)
    top_score = lax.optimization_barrier(jnp.max(scores, axis=-1, keepdims=True))
    log_total = top_score + jnp.log(lax.optimization_barrier(jnp.sum(jnp.exp(scores - top_score), axis=-1, keepdims=True)))
    shares = lower_precision(jnp.exp(scores - log_total))
    mixed_vals = jnp.einsum('kgqt,tkd->qkgd', shares, values_seq, precision=BEST_PRECISION)
    return mixed_vals.reshape(rows_of_queries, QUERY_HEAD_COUNT, HEAD_SIZE)

def attend_sequence(pieces):
    query_seq, keys_seq, values_seq, seg_seq = pieces
    length_total = seg_seq.shape[0]
    block_len = min(512, length_total)
    block_count = length_total // block_len
    blocks = (query_seq.reshape(block_count, block_len, QUERY_HEAD_COUNT, HEAD_SIZE), seg_seq.reshape(block_count, block_len), jnp.arange(block_count, dtype=jnp.int32) * block_len)
    block_step = jax.checkpoint(partial(attend_block, keys_seq=keys_seq, values_seq=values_seq, seg_keys=seg_seq))
    return lax.map(block_step, blocks).reshape(length_total, QUERY_HEAD_COUNT, HEAD_SIZE)

def layer_group(pieces, params):
    inputs_group, seg_ids, route_ids = pieces
    query_mat, key_matrix, value_matrix, out_mat, router_mat, gain_one, gain_two, gate_mat, up_mat, down_mat = params
    row_count = inputs_group.shape[0]
    sequence_count = seg_ids.shape[0]
    length_total = seg_ids.shape[1]
    cosine_lookup, sine_lookup = rope_tables(seg_ids)
    normalized_input = lower_precision(normalize(inputs_group, gain_one))
    queries = lower_precision(rotary_apply(lower_precision_back(jnp.dot(normalized_input, query_mat, precision=BEST_PRECISION)).reshape(sequence_count, length_total, QUERY_HEAD_COUNT, HEAD_SIZE), cosine_lookup, sine_lookup))
    every_key = lower_precision(rotary_apply(lower_precision_back(jnp.dot(normalized_input, key_matrix, precision=BEST_PRECISION)).reshape(sequence_count, length_total, KEY_VALUE_HEADS, HEAD_SIZE), cosine_lookup, sine_lookup))
    every_value = lower_precision(lower_precision_back(jnp.dot(normalized_input, value_matrix, precision=BEST_PRECISION))).reshape(sequence_count, length_total, KEY_VALUE_HEADS, HEAD_SIZE)
    attended = lax.map(jax.checkpoint(attend_sequence), (queries, every_key, every_value, seg_ids))
    attended = lower_precision(lower_precision_back(attended.reshape(row_count, QUERY_HEAD_COUNT * HEAD_SIZE)))
    middle = inputs_group + lower_precision_back(jnp.dot(attended, out_mat, precision=BEST_PRECISION))
    normed_two = lower_precision(normalize(middle, gain_two))
    logits = lower_precision_back(jnp.dot(normed_two, router_mat, precision=BEST_PRECISION))
    chosen = jnp.take_along_axis(logits, route_ids, axis=1)
    gate_values = lower_precision(jax.nn.softmax(chosen, axis=-1))
    slot_table = dispatch(route_ids)
    token_of = slot_table // TOP
    padded_rows = jnp.concatenate([normed_two, jnp.zeros((1, MODEL_DIM), jnp.float32)], axis=0)
    padded_gates = jnp.concatenate([gate_values.reshape(-1), jnp.zeros((1,), jnp.float32)], axis=0)
    expert_in = padded_rows[token_of]
    gate_sel = padded_gates[slot_table]
    gate_act = lower_precision_back(jnp.einsum('ecd,edf->ecf', expert_in, gate_mat, precision=BEST_PRECISION))
    up_act = lower_precision_back(jnp.einsum('ecd,edf->ecf', expert_in, up_mat, precision=BEST_PRECISION))
    hidden = lower_precision(jax.nn.silu(gate_act) * up_act * gate_sel[..., None])
    expert_out = jnp.einsum('ecf,efd->ecd', hidden, down_mat, precision=BEST_PRECISION)
    combined = jnp.zeros((row_count + 1, MODEL_DIM), jnp.float32).at[token_of.reshape(-1)].add(expert_out.reshape(-1, MODEL_DIM))[:row_count]
    return middle + lower_precision_back(combined)

def reference(inputs, segments, routes, query_weight, key_projection_weight, value_projection_weight, out_weight, router_weight, first_gain, second_gain, gate_weight, up_weight, down_weight, cotangent):
    params = tuple((matrix.astype(jnp.float32) for matrix in (query_weight, key_projection_weight, value_projection_weight, out_weight, router_weight, first_gain, second_gain, gate_weight, up_weight, down_weight)))
    groups = segments.shape[0] // SEQS
    group_rows = SEQS * LEN
    stacked = (segments.reshape(groups, SEQS, LEN), routes.reshape(groups, group_rows, TOP))

    def forward(inputs_wide, params_wide):

        def one_group(pieces):
            return layer_group(pieces, params_wide)
        return lax.map(jax.checkpoint(one_group), (inputs_wide.reshape(groups, group_rows, MODEL_DIM),) + stacked)
    outputs, pullback = jax.vjp(forward, inputs.astype(jnp.float32), params)
    grad_in, grad_list = pullback(cotangent.astype(jnp.float32).reshape(groups, group_rows, MODEL_DIM))
    return (outputs.reshape(-1, MODEL_DIM).astype(jnp.bfloat16), grad_in, grad_list[0], grad_list[1], grad_list[2], grad_list[3], grad_list[4], grad_list[5], grad_list[6], grad_list[7], grad_list[8], grad_list[9])
```

```python
import math

import jax
import jax.numpy as jnp
from jax import lax
from jax.sharding import PartitionSpec as P

HEAD_SIZE = 64
EXPERTS = 32
TOP = 8


EPSILON = 1e-06
ROPE_BASE = 10000.0
MASKED = -1e30


def from_everyone(shard, axis):
    copies = jnp.broadcast_to(shard, (lax.axis_size(axis), *shard.shape))
    return lax.all_to_all(copies, axis, split_axis=0, concat_axis=0, tiled=True)


def swapped(blocks, axis):
    return lax.all_to_all(blocks, axis, split_axis=0, concat_axis=0, tiled=True)


def added_up(blocks, axis):
    return jnp.sum(swapped(blocks, axis).astype(jnp.float32), axis=0)


def dot_right(left_mat, right_mat):
    return lax.dot_general(
        left_mat, right_mat, (((1,), (1,)), ((), ())), preferred_element_type=jnp.float32
    )


def dot_left(left_mat, right_mat):
    return lax.dot_general(
        left_mat, right_mat, (((0,), (0,)), ((), ())), preferred_element_type=jnp.float32
    )


def rope_tables(seg_ids):
    length_total = seg_ids.shape[-1]
    places = jnp.arange(length_total, dtype=jnp.int32)
    starts_new = jnp.concatenate(
        [
            jnp.ones(seg_ids.shape[:-1] + (1,), dtype=jnp.bool_),
            seg_ids[..., 1:] != seg_ids[..., :-1],
        ],
        axis=-1,
    )
    doc_start = lax.cummax(jnp.where(starts_new, places, 0), axis=seg_ids.ndim - 1)
    position = (places - doc_start).astype(jnp.float32)
    halves = jnp.arange(HEAD_SIZE // 2, dtype=jnp.int32).astype(jnp.float32)
    rate_list = jnp.exp(halves * (-2.0 * math.log(ROPE_BASE) / HEAD_SIZE))
    angles = position[..., None] * rate_list
    return (jnp.cos(angles), jnp.sin(angles))


def rotary_apply(values, cosine_lookup, sine_lookup):
    half_dim = values.shape[-1] // 2
    front_half = values[..., :half_dim]
    back_half = values[..., half_dim:]
    cos_wide = cosine_lookup[..., None, :]
    sin_wide = sine_lookup[..., None, :]
    return jnp.concatenate(
        [
            front_half * cos_wide - back_half * sin_wide,
            back_half * cos_wide + front_half * sin_wide,
        ],
        axis=-1,
    )


def rotate_back(values, cosine_lookup, sine_lookup):
    half_dim = values.shape[-1] // 2
    front_half = values[..., :half_dim]
    back_half = values[..., half_dim:]
    cos_wide = cosine_lookup[..., None, :]
    sin_wide = sine_lookup[..., None, :]
    return jnp.concatenate(
        [
            front_half * cos_wide + back_half * sin_wide,
            back_half * cos_wide - front_half * sin_wide,
        ],
        axis=-1,
    )


def norm_back(values, inverse, gain_vec, grad_out):
    scaled = grad_out * gain_vec
    grad_gain = jnp.sum(grad_out * values * inverse, axis=0)
    grad_vals = inverse * scaled - values * inverse * inverse * inverse * jnp.mean(
        scaled * values, axis=-1, keepdims=True
    )
    return (grad_vals, grad_gain)


def head_scores(queries, keys, allowed):
    scores = jnp.einsum(
        "qkgd,tkd->kgqt", queries, keys, preferred_element_type=jnp.float32
    ) * HEAD_SIZE ** (-0.5)
    return jnp.where(allowed, scores, MASKED)


def slot_picker(my_routes, cap_dev):
    rows = my_routes.shape[0]
    named = (my_routes[:, :, None] == jnp.arange(EXPERTS, dtype=jnp.int32)).astype(jnp.float32)
    member = jnp.sum(named, axis=1)
    earlier = jnp.tril(jnp.ones((rows, rows), jnp.bfloat16), -1)
    slot = jnp.dot(earlier, member.astype(jnp.bfloat16), preferred_element_type=jnp.float32)
    slot = jnp.where(member > 0, slot, -1.0)
    picked = slot.T[:, None, :] == jnp.arange(cap_dev + 1, dtype=jnp.float32)[None, :, None]
    return named, picked.astype(jnp.bfloat16)


def per_device(
    inputs,
    segments,
    routes,
    query_weight,
    key_projection_weight,
    value_projection_weight,
    out_weight,
    router_weight,
    first_gain,
    second_gain,
    gate_weight,
    up_weight,
    down_weight,
    cotangent,
):
    row_count, model_width = inputs.shape
    length_total = segments.shape[1]
    my_offset = lax.axis_index("tp") * row_count
    tp_count = lax.axis_size("tp")
    fsdp_count = lax.axis_size("fsdp")
    width_shard = query_weight.shape[0]
    q_cols, k_cols, o_cols = query_weight.shape[1], key_projection_weight.shape[1], out_weight.shape[0]
    expert_count, _, hidden_shard = gate_weight.shape
    full_hidden = tp_count * hidden_shard
    cap_dev = row_count * TOP * 33 // (EXPERTS * 32)
    f32, bf16 = jnp.float32, jnp.bfloat16

    wide = q_cols + 2 * k_cols + o_cols
    packed = jnp.concatenate(
        [
            query_weight,
            key_projection_weight,
            value_projection_weight,
            out_weight.T,
            router_weight,
            first_gain[:, None],
            second_gain[:, None],
            jnp.zeros((width_shard, 128 - EXPERTS - 2), bf16),
        ],
        axis=1,
    )
    gathered = from_everyone(packed, "fsdp").reshape(model_width, -1)
    inputs_all = from_everyone(inputs, "tp").reshape(length_total, model_width)

    weight_blocks = jnp.concatenate(
        [gate_weight, up_weight, jnp.transpose(down_weight, (0, 2, 1))], axis=1
    )
    weights = from_everyone(swapped(weight_blocks, "fsdp"), "tp")
    weights = weights.reshape(tp_count, fsdp_count, 3, width_shard, hidden_shard)
    weights = jnp.transpose(weights, (2, 1, 3, 0, 4)).reshape(3, model_width, full_hidden)
    gate_mat, up_mat, down_mat = weights[0], weights[1], weights[2]

    my_routes = lax.dynamic_slice_in_dim(routes, my_offset, row_count, 0)
    named, picked = slot_picker(my_routes, cap_dev)
    cot_rows = jnp.einsum(
        "ect,td->ecd", picked[:, :cap_dev], cotangent, preferred_element_type=f32
    ).astype(bf16)
    cot_local = swapped(cot_rows, "fsdp").reshape(-1, model_width)

    qkv_mat = gathered[:, : q_cols + 2 * k_cols]
    out_mat_t = gathered[:, q_cols + 2 * k_cols : wide]
    router_mat = gathered[:, wide : wide + EXPERTS]
    gain_one = gathered[:, wide + EXPERTS].astype(f32)
    gain_two = gathered[:, wide + EXPERTS + 1].astype(f32)

    wide_all = inputs_all.astype(f32)
    inverse_all = lax.rsqrt(jnp.mean(wide_all * wide_all, axis=-1, keepdims=True) + EPSILON)
    normed_all = (wide_all * inverse_all * gain_one).astype(bf16)
    cosine, sine = rope_tables(segments[0])
    lin = jnp.dot(normed_all, qkv_mat, preferred_element_type=f32)
    query_heads, key_heads = q_cols // HEAD_SIZE, k_cols // HEAD_SIZE
    queries = rotary_apply(
        lin[:, :q_cols].reshape(length_total, query_heads, HEAD_SIZE), cosine, sine
    ).astype(bf16)
    keys = rotary_apply(
        lin[:, q_cols : q_cols + k_cols].reshape(length_total, key_heads, HEAD_SIZE), cosine, sine
    ).astype(bf16)
    values = lin[:, q_cols + k_cols :].astype(bf16).reshape(length_total, key_heads, HEAD_SIZE)
    queries = queries.reshape(length_total, key_heads, -1, HEAD_SIZE)
    place = jnp.arange(length_total, dtype=jnp.int32)
    allowed = (segments[0][:, None] == segments[0][None, :]) & (place[:, None] >= place[None, :])
    scores = head_scores(queries, keys, allowed)
    top_score = jnp.max(scores, axis=-1, keepdims=True)
    log_total = top_score + jnp.log(jnp.sum(jnp.exp(scores - top_score), axis=-1, keepdims=True))
    shares = jnp.exp(scores - log_total).astype(bf16)
    attended = (
        jnp.einsum("kgqt,tkd->qkgd", shares, values, preferred_element_type=f32)
        .reshape(length_total, q_cols)
        .astype(bf16)
    )
    branch = dot_right(attended, out_mat_t).astype(bf16)
    inputs_wide = inputs.astype(f32)
    middle = inputs_wide + added_up(branch.reshape(tp_count, row_count, model_width), "tp")
    inverse_two = lax.rsqrt(jnp.mean(middle * middle, axis=-1, keepdims=True) + EPSILON)
    normed_two = (middle * inverse_two * gain_two).astype(bf16)

    logits = jnp.dot(normed_two, router_mat, preferred_element_type=f32)
    chosen = jnp.sum(named * logits[:, None, :], axis=-1)
    gate_values = jax.nn.softmax(chosen, axis=-1)
    gates_low = gate_values.astype(bf16)
    gate_table = jnp.sum(named * gates_low.astype(f32)[:, :, None], axis=1)
    gates_mine = jnp.sum(picked[:, :cap_dev].astype(f32) * gate_table.T[:, None, :], axis=-1)

    rows_mine = jnp.einsum("ect,td->ecd", picked[:, :cap_dev], normed_two, preferred_element_type=f32).astype(bf16)
    gate_row = jnp.pad(gates_mine.astype(bf16)[:, None, :], ((0, 0), (0, 0), (0, model_width - cap_dev)))
    arrived = swapped(jnp.concatenate([rows_mine, gate_row], axis=1), "fsdp")
    rows_local = arrived[:, :cap_dev].reshape(-1, model_width)
    gate_sel = arrived[:, cap_dev, :cap_dev].astype(f32).reshape(-1, 1)

    grad_hidden = jnp.dot(cot_local, down_mat, preferred_element_type=f32)
    gate_act = jnp.dot(rows_local, gate_mat, preferred_element_type=f32)
    up_act = jnp.dot(rows_local, up_mat, preferred_element_type=f32)
    sigmoid_gate = jax.nn.sigmoid(gate_act)
    silu_gate = gate_act * sigmoid_gate
    grad_prod = grad_hidden * gate_sel
    grad_gate_pre = (
        grad_prod * up_act * sigmoid_gate * (1.0 + gate_act * (1.0 - sigmoid_gate))
    ).astype(bf16)
    grad_up_pre = (grad_prod * silu_gate).astype(bf16)
    grad_sel = jnp.sum(silu_gate * up_act * grad_hidden, axis=-1)
    grad_in = dot_right(grad_gate_pre, gate_mat) + dot_right(grad_up_pre, up_mat)
    sel_row = jnp.pad(
        grad_sel.reshape(fsdp_count, 1, cap_dev), ((0, 0), (0, 0), (0, model_width - cap_dev))
    ).astype(bf16)
    back = jnp.concatenate(
        [grad_in.astype(bf16).reshape(fsdp_count, cap_dev, model_width), sel_row], axis=1
    )
    back = swapped(back, "fsdp")
    hidden = (silu_gate * up_act * gate_sel).astype(bf16)
    expert_out = dot_right(hidden, down_mat).astype(bf16)
    out_back = swapped(expert_out.reshape(fsdp_count, cap_dev, model_width), "fsdp")

    def by_shard(left, right):
        both = dot_left(left, right).astype(bf16)
        return both.reshape(fsdp_count, width_shard, tp_count, hidden_shard)

    grads = jnp.stack(
        [
            by_shard(rows_local, grad_gate_pre),
            by_shard(rows_local, grad_up_pre),
            by_shard(cot_local, hidden),
        ],
        axis=1,
    )
    grads = jnp.transpose(grads, (3, 0, 1, 2, 4)).reshape(
        tp_count, fsdp_count, 3 * width_shard, hidden_shard
    )
    weight_grads = swapped(added_up(grads, "tp").astype(bf16), "fsdp").astype(f32)
    grad_gate_out = weight_grads[:, :width_shard]
    grad_up_out = weight_grads[:, width_shard : 2 * width_shard]
    grad_down_out = jnp.transpose(weight_grads[:, 2 * width_shard :], (0, 2, 1))

    picked_flat = picked[:, :cap_dev].reshape(-1, row_count)
    grad_rows = dot_left(picked_flat, back[:, :cap_dev].reshape(-1, model_width))
    sel_back = back[:, cap_dev, :cap_dev].astype(f32)
    gate_grad_table = jnp.sum(picked[:, :cap_dev].astype(f32) * sel_back[:, :, None], axis=1).T
    grad_gates = jnp.sum(named * gate_grad_table[:, None, :], axis=-1)
    grad_chosen = gate_values * (
        grad_gates - jnp.sum(gate_values * grad_gates, axis=-1, keepdims=True)
    )
    grad_logits = jnp.sum(grad_chosen[:, :, None] * named, axis=1).astype(bf16)
    router_part = dot_left(normed_two, grad_logits)
    grad_normed_two = grad_rows + dot_right(grad_logits, router_mat)
    grad_middle_norm, second_part = norm_back(middle, inverse_two, gain_two, grad_normed_two)
    grad_middle = cotangent.astype(f32) + grad_middle_norm
    output = (
        middle + dot_left(picked_flat, out_back.reshape(-1, model_width))
    ).astype(bf16)

    grad_branch = from_everyone(grad_middle.astype(bf16), "tp").reshape(length_total, model_width)
    out_part = dot_left(grad_branch, attended)
    grad_attended = (
        jnp.dot(grad_branch, out_mat_t, preferred_element_type=f32)
        .astype(bf16)
        .reshape(length_total, key_heads, -1, HEAD_SIZE)
    )
    whole = jnp.exp(head_scores(queries, keys, allowed) - log_total)
    grad_shares = jnp.einsum("qkgd,tkd->kgqt", grad_attended, values, preferred_element_type=f32)
    inner = jnp.sum(whole * grad_shares, axis=-1, keepdims=True)
    grad_scores = (whole * (grad_shares - inner)).astype(bf16)
    scale = HEAD_SIZE ** (-0.5)
    grad_rot_q = jnp.einsum("kgqt,tkd->qkgd", grad_scores, keys, preferred_element_type=f32) * scale
    grad_rot_k = jnp.einsum("kgqt,qkgd->tkd", grad_scores, queries, preferred_element_type=f32) * scale
    grad_values = jnp.einsum(
        "kgqt,qkgd->tkd", whole.astype(bf16), grad_attended, preferred_element_type=f32
    )
    grad_lin = jnp.concatenate(
        [
            rotate_back(
                grad_rot_q.reshape(length_total, query_heads, HEAD_SIZE), cosine, sine
            ).reshape(length_total, -1),
            rotate_back(grad_rot_k, cosine, sine).reshape(length_total, -1),
            grad_values.reshape(length_total, -1),
        ],
        axis=1,
    ).astype(bf16)
    qkv_part = dot_left(normed_all, grad_lin)
    grad_normed = added_up(
        dot_right(grad_lin, qkv_mat).astype(bf16).reshape(tp_count, row_count, model_width), "tp"
    )
    inverse_one = lax.dynamic_slice_in_dim(inverse_all, my_offset, row_count, 0)
    grad_inputs_norm, first_part = norm_back(inputs_wide, inverse_one, gain_one, grad_normed)
    grad_inputs = grad_middle + grad_inputs_norm

    token_parts = jnp.concatenate(
        [router_part, first_part[:, None], second_part[:, None]], axis=1
    )
    token_sums = jnp.sum(from_everyone(token_parts.T, "tp"), axis=0).T
    small = jnp.pad(token_sums, ((0, 0), (0, 128 - EXPERTS - 2)))
    sums_in = jnp.concatenate([qkv_part, out_part, small], axis=1).astype(bf16)
    sums = added_up(sums_in.reshape(fsdp_count, width_shard, -1), "fsdp")
    return (
        output,
        grad_inputs,
        sums[:, :q_cols],
        sums[:, q_cols : q_cols + k_cols],
        sums[:, q_cols + k_cols : q_cols + 2 * k_cols],
        sums[:, q_cols + 2 * k_cols : wide].T,
        sums[:, wide : wide + EXPERTS],
        sums[:, wide + EXPERTS],
        sums[:, wide + EXPERTS + 1],
        grad_gate_out,
        grad_up_out,
        grad_down_out,
    )


def solution(mesh):
    return jax.shard_map(
        per_device,
        mesh=mesh,
        in_specs=(
            P(("fsdp", "tp"), None),
            P("fsdp", None),
            P("fsdp", None),
            P("fsdp", "tp"),
            P("fsdp", "tp"),
            P("fsdp", "tp"),
            P("tp", "fsdp"),
            P("fsdp", None),
            P("fsdp"),
            P("fsdp"),
            P(None, "fsdp", "tp"),
            P(None, "fsdp", "tp"),
            P(None, "tp", "fsdp"),
            P(("fsdp", "tp"), None),
        ),
        out_specs=(
            P(("fsdp", "tp"), None),
            P(("fsdp", "tp"), None),
            P("fsdp", "tp"),
            P("fsdp", "tp"),
            P("fsdp", "tp"),
            P("tp", "fsdp"),
            P("fsdp", None),
            P("fsdp"),
            P("fsdp"),
            P(None, "fsdp", "tp"),
            P(None, "fsdp", "tp"),
            P(None, "tp", "fsdp"),
        ),
        check_vma=False,
    )
```

```python
import math

import jax
import jax.numpy as jnp
from jax import lax
from jax.experimental import pallas as pl
from jax.experimental.pallas import tpu as pltpu
from jax.sharding import PartitionSpec as P

HEAD_SIZE = 64
EXPERTS = 32
TOP = 8


EPSILON = 1e-06
ROPE_BASE = 10000.0
MASKED = -1e30


def from_everyone(shard, axis):
    copies = jnp.broadcast_to(shard, (lax.axis_size(axis), *shard.shape))
    return lax.all_to_all(copies, axis, split_axis=0, concat_axis=0, tiled=True)


def swapped(blocks, axis):
    return lax.all_to_all(blocks, axis, split_axis=0, concat_axis=0, tiled=True)


def added_up(blocks, axis):
    return jnp.sum(swapped(blocks, axis).astype(jnp.float32), axis=0)


def dot_right(left_mat, right_mat):
    return lax.dot_general(
        left_mat, right_mat, (((1,), (1,)), ((), ())), preferred_element_type=jnp.float32
    )


def dot_left(left_mat, right_mat):
    return lax.dot_general(
        left_mat, right_mat, (((0,), (0,)), ((), ())), preferred_element_type=jnp.float32
    )


def rope_tables(seg_ids):
    length_total = seg_ids.shape[-1]
    places = jnp.arange(length_total, dtype=jnp.int32)
    starts_new = jnp.concatenate(
        [
            jnp.ones(seg_ids.shape[:-1] + (1,), dtype=jnp.bool_),
            seg_ids[..., 1:] != seg_ids[..., :-1],
        ],
        axis=-1,
    )
    doc_start = lax.cummax(jnp.where(starts_new, places, 0), axis=seg_ids.ndim - 1)
    position = (places - doc_start).astype(jnp.float32)
    halves = jnp.arange(HEAD_SIZE // 2, dtype=jnp.int32).astype(jnp.float32)
    rate_list = jnp.exp(halves * (-2.0 * math.log(ROPE_BASE) / HEAD_SIZE))
    angles = position[..., None] * rate_list
    return (jnp.cos(angles), jnp.sin(angles))


def rotary_apply(values, cosine_lookup, sine_lookup):
    half_dim = values.shape[-1] // 2
    front_half = values[..., :half_dim]
    back_half = values[..., half_dim:]
    cos_wide = cosine_lookup[..., None, :]
    sin_wide = sine_lookup[..., None, :]
    return jnp.concatenate(
        [
            front_half * cos_wide - back_half * sin_wide,
            back_half * cos_wide + front_half * sin_wide,
        ],
        axis=-1,
    )


def rotate_back(values, cosine_lookup, sine_lookup):
    half_dim = values.shape[-1] // 2
    front_half = values[..., :half_dim]
    back_half = values[..., half_dim:]
    cos_wide = cosine_lookup[..., None, :]
    sin_wide = sine_lookup[..., None, :]
    return jnp.concatenate(
        [
            front_half * cos_wide + back_half * sin_wide,
            back_half * cos_wide - front_half * sin_wide,
        ],
        axis=-1,
    )


def norm_back(values, inverse, gain_vec, grad_out):
    scaled = grad_out * gain_vec
    grad_gain = jnp.sum(grad_out * values * inverse, axis=0)
    grad_vals = inverse * scaled - values * inverse * inverse * inverse * jnp.mean(
        scaled * values, axis=-1, keepdims=True
    )
    return (grad_vals, grad_gain)


MESH = pl.DeviceIdType.MESH
FSDP, TP, SPARE = 32, 4, 33
F32, BF16 = jnp.float32, jnp.bfloat16


def peer(me, k):
    z, x, y = me // 8, (me // 4) % 2, me % 4
    return ((z + k // 8) % 4 * 2 + (x + (k // 4) % 2) % 2) * 4 + (y + k % 4) % 4


def giver(me, k):
    z, x, y = me // 8, (me // 4) % 2, me % 4
    return ((z + 4 - k // 8) % 4 * 2 + (x + (k // 4) % 2) % 2) * 4 + (y + 4 - k % 4) % 4


def loop(low, high, step):
    def body(k, carry):
        step(k)
        return carry

    lax.fori_loop(low, high, body, 0)


def greet(me, tp):
    barrier = pltpu.get_barrier_semaphore()
    loop(
        1,
        FSDP,
        lambda k: pl.semaphore_signal(
            barrier, inc=1, device_id={"fsdp": peer(me, k)}, device_id_type=MESH
        ),
    )
    for k in range(1, TP):
        pl.semaphore_signal(
            barrier, inc=1, device_id={"tp": lax.rem(tp + k, TP)}, device_id_type=MESH
        )
    pl.semaphore_wait(barrier, FSDP - 1 + TP - 1)


def to_fsdp(src, dst, send, recv, where):
    return pltpu.make_async_remote_copy(
        src_ref=src,
        dst_ref=dst,
        send_sem=send,
        recv_sem=recv,
        device_id={"fsdp": where},
        device_id_type=MESH,
    )


def to_tp(src, dst, send, recv, where):
    return pltpu.make_async_remote_copy(
        src_ref=src,
        dst_ref=dst,
        send_sem=send,
        recv_sem=recv,
        device_id={"tp": where},
        device_id_type=MESH,
    )


def nn(a, b):
    return jnp.dot(a, b, preferred_element_type=F32)


def nt(a, b):
    return lax.dot_general(a, b, (((1,), (1,)), ((), ())), preferred_element_type=F32)


def tn(a, b):
    return lax.dot_general(a, b, (((0,), (0,)), ((), ())), preferred_element_type=F32)


def lanes(shape):
    return lax.broadcasted_iota(jnp.int32, shape, len(shape) - 1)


def rows_of(shape):
    return lax.broadcasted_iota(jnp.int32, shape, 0)


def half_swap(v):
    width = v.shape[-1]
    front = lanes(v.shape) % HEAD_SIZE < HEAD_SIZE // 2
    ahead = pltpu.roll(v, width - HEAD_SIZE // 2, 1)
    behind = pltpu.roll(v, HEAD_SIZE // 2, 1)
    return jnp.where(front, -ahead, behind)


def wide_table(table, width):
    return jnp.concatenate([table] * (width // 128), axis=1)


def pick(slot_ref, experts, count):
    parts = []
    for e in experts:
        row = slot_ref[pl.ds(e, 1), :]
        parts.append(jnp.broadcast_to(row, (count, row.shape[1])))
    both = jnp.concatenate(parts, axis=0)
    want = (rows_of(both.shape) % count).astype(F32)
    return (both == want).astype(BF16)


def forward_kernel(
    packed_ref, inputs_ref, seg_ref, routes_ref, blocks_ref, cot_ref,
    middle_ref, normed_two_ref, gates_ref, slot_ref, weights_ref, cot_main_ref, cot_spare_ref,
    packed_all_ref, heads_ref, normed_all_ref, attended_ref, cos_ref, sin_ref,
    inputs_all, blocks_in, send_main, send_spare, branch_out, branch_in,
    packed_send, packed_recv, blocks_send, blocks_recv, main_send, main_recv, spare_send, spare_recv,
    inputs_send, inputs_recv, weights_send, weights_recv, branch_send, branch_recv, own_sem,
):
    me, tp = lax.axis_index("fsdp"), lax.axis_index("tp")
    rows, width = inputs_ref.shape
    total = seg_ref.shape[1]
    greet(me, tp)

    def packed_copy(k):
        return to_fsdp(
            packed_ref, packed_all_ref.at[me], packed_send.at[k], packed_recv.at[k], peer(me, k)
        )

    def inputs_copy(k):
        return to_tp(
            inputs_ref, inputs_all.at[tp], inputs_send.at[k], inputs_recv.at[k], lax.rem(tp + k, TP)
        )

    def blocks_copy(k):
        p = peer(me, k)
        return to_fsdp(blocks_ref.at[p], blocks_in.at[me], blocks_send.at[k], blocks_recv.at[k], p)

    def main_copy(k):
        return to_fsdp(
            send_main.at[k], cot_main_ref.at[k], main_send.at[k], main_recv.at[k], peer(me, k)
        )

    def spare_copy(k):
        return to_fsdp(
            send_spare.at[k], cot_spare_ref.at[k], spare_send.at[k], spare_recv.at[k], peer(me, k)
        )

    def branch_copy(k):
        q = lax.rem(tp + k, TP)
        return to_tp(
            branch_out.at[q], branch_in.at[k], branch_send.at[k], branch_recv.at[k], q
        )

    for k in (2, 1, 3):
        inputs_copy(k).start()
    loop(1, FSDP, lambda k: packed_copy(k).start())
    loop(1, FSDP, lambda k: blocks_copy(k).start())
    keep = [
        pltpu.make_async_copy(packed_ref, packed_all_ref.at[me], own_sem.at[0]),
        pltpu.make_async_copy(inputs_ref, inputs_all.at[tp], own_sem.at[1]),
        pltpu.make_async_copy(blocks_ref.at[me], blocks_in.at[me], own_sem.at[2]),
    ]
    for copy in keep:
        copy.start()

    at = lanes((rows, 128))
    member = jnp.zeros((rows, 128), F32)
    for k in range(TOP):
        member = member + (routes_ref[:, k : k + 1] == at).astype(F32)
    earlier = (rows_of((rows, rows)) > lanes((rows, rows))).astype(BF16)
    slot = nn(earlier, member.astype(BF16))
    slot = jnp.where(member > 0, slot, -1.0)
    slot_ref[...] = jnp.transpose(slot)[:EXPERTS]

    def some_rows(i):
        hot = pick(slot_ref, [peer(me, 4 * i + j) for j in range(4)], 40)
        out = nn(hot, cot_ref[...])
        for j in range(4):
            send_main[4 * i + j] = out[40 * j : 40 * j + 32].astype(BF16)
            send_spare[4 * i + j] = out[40 * j + 32 : 40 * j + 33]

        def go(k):
            main_copy(k).start()
            spare_copy(k).start()

        loop(jnp.maximum(4 * i, 1), 4 * i + 4, go)

    loop(0, FSDP // 4, some_rows)
    cot_main_ref[0] = send_main[0]
    cot_spare_ref[0] = send_spare[0]

    seg_row = jnp.broadcast_to(seg_ref[...].astype(F32), (128, total))
    seg_col = jnp.transpose(seg_row)[:, :1]
    same = (seg_col == seg_row[:1]) & (rows_of((total, total)) >= lanes((total, total)))
    allowed = same.astype(F32)
    place = jnp.sum(allowed, axis=1, keepdims=True) - 1.0
    halves = (lanes((1, 128)) % (HEAD_SIZE // 2)).astype(F32)
    rate = jnp.exp(halves * (-2.0 * math.log(ROPE_BASE) / HEAD_SIZE))
    angle = place * rate
    cos_ref[...] = jnp.cos(angle)
    sin_ref[...] = jnp.sin(angle)

    for k in range(1, TP):
        inputs_copy(k).wait_recv()
    keep[1].wait()
    wide = inputs_all[...].reshape(total, width).astype(F32)
    inverse = lax.rsqrt(jnp.mean(wide * wide, axis=-1, keepdims=True) + EPSILON)

    loop(1, FSDP, lambda k: packed_copy(k).wait_recv())
    keep[0].wait()
    tail = jnp.transpose(packed_all_ref[:, :, 768:896].reshape(width, 128).astype(F32))
    normed = (wide * inverse * tail[EXPERTS : EXPERTS + 1]).astype(BF16)
    normed_all_ref[...] = normed
    lin = nn(normed, packed_all_ref[:, :, 0:512].reshape(width, 512))
    turn = lin[:, :384]
    turned = turn * wide_table(cos_ref[...], 384) + half_swap(turn) * wide_table(sin_ref[...], 384)
    heads_ref[:, :384] = turned.astype(BF16)
    heads_ref[:, 384:] = lin[:, 384:].astype(BF16)
    outs = []
    for h in range(4):
        g = h // 2
        q = heads_ref[:, 64 * h : 64 * h + 64]
        key = heads_ref[:, 256 + 64 * g : 320 + 64 * g]
        value = heads_ref[:, 384 + 64 * g : 448 + 64 * g]
        scores = jnp.where(allowed > 0, nt(q, key) * HEAD_SIZE ** (-0.5), MASKED)
        top = jnp.max(scores, axis=1, keepdims=True)
        grown = jnp.exp(scores - top)
        shares = (grown * (1.0 / jnp.sum(grown, axis=1, keepdims=True))).astype(BF16)
        outs.append(nn(shares, value))
    attended = jnp.concatenate(outs, axis=1).astype(BF16)
    attended_ref[...] = attended
    branch = nt(attended, packed_all_ref[:, :, 512:768].reshape(width, 256))
    branch_out[...] = branch.astype(BF16).reshape(TP, rows, width)
    for k in (2, 1, 3):
        branch_copy(k).start()

    loop(1, FSDP, lambda k: blocks_copy(k).wait_recv())
    keep[2].wait()
    sibling = tp + 1 - 2 * lax.rem(tp, 2)
    across = lax.rem(tp + 2, TP)
    first = to_tp(blocks_in, weights_ref.at[tp], weights_send.at[0], weights_recv.at[0], across)
    second = to_tp(blocks_in, weights_ref.at[tp], weights_send.at[1], weights_recv.at[1], sibling)
    third = to_tp(
        weights_ref.at[across], weights_ref.at[across], weights_send.at[2], weights_recv.at[2], sibling
    )
    first.start()
    second.start()
    mine = pltpu.make_async_copy(blocks_in, weights_ref.at[tp], own_sem.at[3])
    mine.start()

    for k in range(1, TP):
        branch_copy(k).wait_recv()
    middle = inputs_ref[...].astype(F32) + branch_out[tp].astype(F32)
    for k in range(1, TP):
        middle = middle + branch_in[k].astype(F32)
    middle_ref[...] = middle
    inverse_two = lax.rsqrt(jnp.mean(middle * middle, axis=-1, keepdims=True) + EPSILON)
    normed_two = (middle * inverse_two * tail[EXPERTS + 1 : EXPERTS + 2]).astype(BF16)
    normed_two_ref[...] = normed_two
    logits = nn(normed_two, packed_all_ref[:, :, 768:896].reshape(width, 128))
    logits = jnp.where(member > 0, logits, MASKED)
    grown = jnp.exp(logits - jnp.max(logits, axis=1, keepdims=True)) * member
    gates_ref[...] = grown / jnp.sum(grown, axis=1, keepdims=True)

    first.wait_recv()
    third.start()

    def got(k):
        main_copy(k).wait_recv()
        spare_copy(k).wait_recv()

    loop(1, FSDP, got)
    second.wait_recv()
    third.wait_recv()
    mine.wait()

    def gone(k):
        packed_copy(k).wait_send()
        blocks_copy(k).wait_send()
        main_copy(k).wait_send()
        spare_copy(k).wait_send()

    loop(1, FSDP, gone)
    for k in range(1, TP):
        inputs_copy(k).wait_send()
        branch_copy(k).wait_send()
    for copy in (first, second, third):
        copy.wait_send()


def shape(dims, kind):
    return jax.ShapeDtypeStruct(dims, kind)


def dma(count):
    return pltpu.SemaphoreType.DMA((count,))


def forward(packed, inputs, seg, routes, blocks, cot):
    rows, width = inputs.shape
    total = seg.shape[1]
    vmem = pl.BlockSpec(memory_space=pltpu.VMEM)
    out = (
        shape((rows, width), F32),
        shape((rows, width), BF16),
        shape((rows, 128), F32),
        shape((EXPERTS, rows), F32),
        shape((TP, *blocks.shape), BF16),
        shape((FSDP, 32, width), BF16),
        shape((FSDP, 1, width), F32),
        shape((FSDP, *packed.shape), BF16),
        shape((total, 512), BF16),
        shape((total, width), BF16),
        shape((total, 256), BF16),
        shape((total, 128), F32),
        shape((total, 128), F32),
    )
    return pl.pallas_call(
        forward_kernel,
        out_shape=out,
        in_specs=[vmem] * 6,
        out_specs=[vmem] * len(out),
        scratch_shapes=[
            pltpu.VMEM((TP, rows, width), BF16),
            pltpu.VMEM(blocks.shape, BF16),
            pltpu.VMEM((FSDP, 32, width), BF16),
            pltpu.VMEM((FSDP, 1, width), F32),
            pltpu.VMEM((TP, rows, width), BF16),
            pltpu.VMEM((TP, rows, width), BF16),
            *[dma(FSDP)] * 8,
            *[dma(TP)] * 6,
            dma(4),
        ],
        compiler_params=pltpu.CompilerParams(
            collective_id=1, has_side_effects=True, vmem_limit_bytes=56 * 2**20
        ),
        name="attention_forward",
    )(packed, inputs, seg, routes, blocks, cot)


def head_scores(queries, keys, allowed):
    scores = jnp.einsum(
        "qkgd,tkd->kgqt", queries, keys, preferred_element_type=jnp.float32
    ) * HEAD_SIZE ** (-0.5)
    return jnp.where(allowed, scores, MASKED)


def slot_picker(my_routes, cap_dev):
    rows = my_routes.shape[0]
    named = (my_routes[:, :, None] == jnp.arange(EXPERTS, dtype=jnp.int32)).astype(jnp.float32)
    member = jnp.sum(named, axis=1)
    earlier = jnp.tril(jnp.ones((rows, rows), jnp.bfloat16), -1)
    slot = jnp.dot(earlier, member.astype(jnp.bfloat16), preferred_element_type=jnp.float32)
    slot = jnp.where(member > 0, slot, -1.0)
    picked = slot.T[:, None, :] == jnp.arange(cap_dev + 1, dtype=jnp.float32)[None, :, None]
    return named, picked.astype(jnp.bfloat16)


def per_device(
    inputs,
    segments,
    routes,
    query_weight,
    key_projection_weight,
    value_projection_weight,
    out_weight,
    router_weight,
    first_gain,
    second_gain,
    gate_weight,
    up_weight,
    down_weight,
    cotangent,
):
    row_count, model_width = inputs.shape
    length_total = segments.shape[1]
    my_offset = lax.axis_index("tp") * row_count
    tp_count = lax.axis_size("tp")
    fsdp_count = lax.axis_size("fsdp")
    width_shard = query_weight.shape[0]
    q_cols, k_cols, o_cols = query_weight.shape[1], key_projection_weight.shape[1], out_weight.shape[0]
    expert_count, _, hidden_shard = gate_weight.shape
    full_hidden = tp_count * hidden_shard
    cap_dev = row_count * TOP * 33 // (EXPERTS * 32)
    f32, bf16 = jnp.float32, jnp.bfloat16

    wide = q_cols + 2 * k_cols + o_cols
    packed = jnp.concatenate(
        [
            query_weight,
            key_projection_weight,
            value_projection_weight,
            out_weight.T,
            router_weight,
            first_gain[:, None],
            second_gain[:, None],
            jnp.zeros((width_shard, 128 - EXPERTS - 2), bf16),
        ],
        axis=1,
    )
    weight_blocks = jnp.concatenate(
        [gate_weight, up_weight, jnp.transpose(down_weight, (0, 2, 1))], axis=1
    )
    my_routes = lax.dynamic_slice_in_dim(routes, my_offset, row_count, 0)
    (
        middle, normed_two, gates, slot, weights, cot_main, cot_spare,
        packed_all, heads, normed_all, attended, cos_wide, sin_wide,
    ) = forward(packed, inputs, segments, my_routes, weight_blocks, cotangent)
    weights = weights.reshape(tp_count, fsdp_count, 3, width_shard, hidden_shard)
    weights = jnp.transpose(weights, (2, 1, 3, 0, 4)).reshape(3, model_width, full_hidden)
    gate_mat, up_mat, down_mat = weights[0], weights[1], weights[2]
    me = lax.axis_index("fsdp")
    offs = jnp.arange(FSDP, dtype=jnp.int32)
    peers = peer(me, offs)
    givers = giver(me, offs)
    back_of = jnp.zeros((FSDP,), jnp.int32).at[givers].set(offs)
    cot_main, cot_spare = cot_main[back_of], cot_spare[back_of]
    cot_local = jnp.concatenate([cot_main, cot_spare.astype(bf16)], axis=1).reshape(-1, model_width)
    gathered = packed_all.reshape(model_width, -1)
    qkv_mat = gathered[:, : q_cols + 2 * k_cols]
    out_mat_t = gathered[:, q_cols + 2 * k_cols : wide]
    router_mat = gathered[:, wide : wide + EXPERTS]
    gain_one = gathered[:, wide + EXPERTS].astype(f32)
    gain_two = gathered[:, wide + EXPERTS + 1].astype(f32)
    query_heads, key_heads = q_cols // HEAD_SIZE, k_cols // HEAD_SIZE
    queries = heads[:, :q_cols].reshape(length_total, key_heads, -1, HEAD_SIZE)
    keys = heads[:, q_cols : q_cols + k_cols].reshape(length_total, key_heads, HEAD_SIZE)
    values = heads[:, q_cols + k_cols :].reshape(length_total, key_heads, HEAD_SIZE)
    cosine, sine = cos_wide[:, :32], sin_wide[:, :32]
    place = jnp.arange(length_total, dtype=jnp.int32)
    allowed = (segments[0][:, None] == segments[0][None, :]) & (place[:, None] >= place[None, :])
    scores = head_scores(queries, keys, allowed)
    top_score = jnp.max(scores, axis=-1, keepdims=True)
    log_total = top_score + jnp.log(jnp.sum(jnp.exp(scores - top_score), axis=-1, keepdims=True))
    inputs_wide = inputs.astype(f32)
    inverse_one = lax.rsqrt(jnp.mean(inputs_wide * inputs_wide, axis=-1, keepdims=True) + EPSILON)
    inverse_two = lax.rsqrt(jnp.mean(middle * middle, axis=-1, keepdims=True) + EPSILON)
    named = (my_routes[:, :, None] == jnp.arange(EXPERTS, dtype=jnp.int32)).astype(f32)
    gate_values = jnp.sum(named * gates[:, None, :EXPERTS], axis=-1)
    gate_table = gates[:, :EXPERTS].astype(bf16).astype(f32)
    picked = (slot[:, None, :] == jnp.arange(cap_dev + 1, dtype=f32)[None, :, None]).astype(bf16)
    gates_mine = jnp.sum(picked[:, :cap_dev].astype(f32) * gate_table.T[:, None, :], axis=-1)
    rows_mine = jnp.einsum("ect,td->ecd", picked[:, :cap_dev], normed_two, preferred_element_type=f32).astype(bf16)
    gate_row = jnp.pad(gates_mine.astype(bf16)[:, None, :], ((0, 0), (0, 0), (0, model_width - cap_dev)))
    arrived = swapped(jnp.concatenate([rows_mine, gate_row], axis=1), "fsdp")
    rows_local = arrived[:, :cap_dev].reshape(-1, model_width)
    gate_sel = arrived[:, cap_dev, :cap_dev].astype(f32).reshape(-1, 1)

    grad_hidden = jnp.dot(cot_local, down_mat, preferred_element_type=f32)
    gate_act = jnp.dot(rows_local, gate_mat, preferred_element_type=f32)
    up_act = jnp.dot(rows_local, up_mat, preferred_element_type=f32)
    sigmoid_gate = jax.nn.sigmoid(gate_act)
    silu_gate = gate_act * sigmoid_gate
    grad_prod = grad_hidden * gate_sel
    grad_gate_pre = (
        grad_prod * up_act * sigmoid_gate * (1.0 + gate_act * (1.0 - sigmoid_gate))
    ).astype(bf16)
    grad_up_pre = (grad_prod * silu_gate).astype(bf16)
    grad_sel = jnp.sum(silu_gate * up_act * grad_hidden, axis=-1)
    grad_in = dot_right(grad_gate_pre, gate_mat) + dot_right(grad_up_pre, up_mat)
    sel_row = jnp.pad(
        grad_sel.reshape(fsdp_count, 1, cap_dev), ((0, 0), (0, 0), (0, model_width - cap_dev))
    ).astype(bf16)
    back = jnp.concatenate(
        [grad_in.astype(bf16).reshape(fsdp_count, cap_dev, model_width), sel_row], axis=1
    )
    back = swapped(back, "fsdp")
    hidden = (silu_gate * up_act * gate_sel).astype(bf16)
    expert_out = dot_right(hidden, down_mat).astype(bf16)
    out_back = swapped(expert_out.reshape(fsdp_count, cap_dev, model_width), "fsdp")

    def by_shard(left, right):
        both = dot_left(left, right).astype(bf16)
        return both.reshape(fsdp_count, width_shard, tp_count, hidden_shard)

    grads = jnp.stack(
        [
            by_shard(rows_local, grad_gate_pre),
            by_shard(rows_local, grad_up_pre),
            by_shard(cot_local, hidden),
        ],
        axis=1,
    )
    grads = jnp.transpose(grads, (3, 0, 1, 2, 4)).reshape(
        tp_count, fsdp_count, 3 * width_shard, hidden_shard
    )
    weight_grads = swapped(added_up(grads, "tp").astype(bf16), "fsdp").astype(f32)
    grad_gate_out = weight_grads[:, :width_shard]
    grad_up_out = weight_grads[:, width_shard : 2 * width_shard]
    grad_down_out = jnp.transpose(weight_grads[:, 2 * width_shard :], (0, 2, 1))

    picked_flat = picked[:, :cap_dev].reshape(-1, row_count)
    grad_rows = dot_left(picked_flat, back[:, :cap_dev].reshape(-1, model_width))
    sel_back = back[:, cap_dev, :cap_dev].astype(f32)
    gate_grad_table = jnp.sum(picked[:, :cap_dev].astype(f32) * sel_back[:, :, None], axis=1).T
    grad_gates = jnp.sum(named * gate_grad_table[:, None, :], axis=-1)
    grad_chosen = gate_values * (
        grad_gates - jnp.sum(gate_values * grad_gates, axis=-1, keepdims=True)
    )
    grad_logits = jnp.sum(grad_chosen[:, :, None] * named, axis=1).astype(bf16)
    router_part = dot_left(normed_two, grad_logits)
    grad_normed_two = grad_rows + dot_right(grad_logits, router_mat)
    grad_middle_norm, second_part = norm_back(middle, inverse_two, gain_two, grad_normed_two)
    grad_middle = cotangent.astype(f32) + grad_middle_norm
    output = (
        middle + dot_left(picked_flat, out_back.reshape(-1, model_width))
    ).astype(bf16)

    grad_branch = from_everyone(grad_middle.astype(bf16), "tp").reshape(length_total, model_width)
    out_part = dot_left(grad_branch, attended)
    grad_attended = (
        jnp.dot(grad_branch, out_mat_t, preferred_element_type=f32)
        .astype(bf16)
        .reshape(length_total, key_heads, -1, HEAD_SIZE)
    )
    whole = jnp.exp(head_scores(queries, keys, allowed) - log_total)
    grad_shares = jnp.einsum("qkgd,tkd->kgqt", grad_attended, values, preferred_element_type=f32)
    inner = jnp.sum(whole * grad_shares, axis=-1, keepdims=True)
    grad_scores = (whole * (grad_shares - inner)).astype(bf16)
    scale = HEAD_SIZE ** (-0.5)
    grad_rot_q = jnp.einsum("kgqt,tkd->qkgd", grad_scores, keys, preferred_element_type=f32) * scale
    grad_rot_k = jnp.einsum("kgqt,qkgd->tkd", grad_scores, queries, preferred_element_type=f32) * scale
    grad_values = jnp.einsum(
        "kgqt,qkgd->tkd", whole.astype(bf16), grad_attended, preferred_element_type=f32
    )
    grad_lin = jnp.concatenate(
        [
            rotate_back(
                grad_rot_q.reshape(length_total, query_heads, HEAD_SIZE), cosine, sine
            ).reshape(length_total, -1),
            rotate_back(grad_rot_k, cosine, sine).reshape(length_total, -1),
            grad_values.reshape(length_total, -1),
        ],
        axis=1,
    ).astype(bf16)
    qkv_part = dot_left(normed_all, grad_lin)
    grad_normed = added_up(
        dot_right(grad_lin, qkv_mat).astype(bf16).reshape(tp_count, row_count, model_width), "tp"
    )
    grad_inputs_norm, first_part = norm_back(inputs_wide, inverse_one, gain_one, grad_normed)
    grad_inputs = grad_middle + grad_inputs_norm

    token_parts = jnp.concatenate(
        [router_part, first_part[:, None], second_part[:, None]], axis=1
    )
    token_sums = jnp.sum(from_everyone(token_parts.T, "tp"), axis=0).T
    small = jnp.pad(token_sums, ((0, 0), (0, 128 - EXPERTS - 2)))
    sums_in = jnp.concatenate([qkv_part, out_part, small], axis=1).astype(bf16)
    sums = added_up(sums_in.reshape(fsdp_count, width_shard, -1), "fsdp")
    return (
        output,
        grad_inputs,
        sums[:, :q_cols],
        sums[:, q_cols : q_cols + k_cols],
        sums[:, q_cols + k_cols : q_cols + 2 * k_cols],
        sums[:, q_cols + 2 * k_cols : wide].T,
        sums[:, wide : wide + EXPERTS],
        sums[:, wide + EXPERTS],
        sums[:, wide + EXPERTS + 1],
        grad_gate_out,
        grad_up_out,
        grad_down_out,
    )


def solution(mesh):
    return jax.shard_map(
        per_device,
        mesh=mesh,
        in_specs=(
            P(("fsdp", "tp"), None),
            P("fsdp", None),
            P("fsdp", None),
            P("fsdp", "tp"),
            P("fsdp", "tp"),
            P("fsdp", "tp"),
            P("tp", "fsdp"),
            P("fsdp", None),
            P("fsdp"),
            P("fsdp"),
            P(None, "fsdp", "tp"),
            P(None, "fsdp", "tp"),
            P(None, "tp", "fsdp"),
            P(("fsdp", "tp"), None),
        ),
        out_specs=(
            P(("fsdp", "tp"), None),
            P(("fsdp", "tp"), None),
            P("fsdp", "tp"),
            P("fsdp", "tp"),
            P("fsdp", "tp"),
            P("tp", "fsdp"),
            P("fsdp", None),
            P("fsdp"),
            P("fsdp"),
            P(None, "fsdp", "tp"),
            P(None, "fsdp", "tp"),
            P(None, "tp", "fsdp"),
        ),
        check_vma=False,
    )
```

```python
import math

import jax
import jax.numpy as jnp
from jax import lax
from jax.experimental import pallas as pl
from jax.experimental.pallas import tpu as pltpu
from jax.sharding import PartitionSpec as P

HEAD_SIZE = 64
EXPERTS = 32
TOP = 8


EPSILON = 1e-06
ROPE_BASE = 10000.0
MASKED = -1e30


MESH = pl.DeviceIdType.MESH
FSDP, TP, SPARE = 32, 4, 33
F32, BF16 = jnp.float32, jnp.bfloat16


def peer(me, k):
    z, x, y = me // 8, (me // 4) % 2, me % 4
    return ((z + k // 8) % 4 * 2 + (x + (k // 4) % 2) % 2) * 4 + (y + k % 4) % 4


def giver(me, k):
    z, x, y = me // 8, (me // 4) % 2, me % 4
    return ((z + 4 - k // 8) % 4 * 2 + (x + (k // 4) % 2) % 2) * 4 + (y + 4 - k % 4) % 4


def loop(low, high, step):
    def body(k, carry):
        step(k)
        return carry

    lax.fori_loop(low, high, body, 0)


def greet(me, tp):
    barrier = pltpu.get_barrier_semaphore()
    loop(
        1,
        FSDP,
        lambda k: pl.semaphore_signal(
            barrier, inc=1, device_id={"fsdp": peer(me, k)}, device_id_type=MESH
        ),
    )
    for k in range(1, TP):
        pl.semaphore_signal(
            barrier, inc=1, device_id={"tp": lax.rem(tp + k, TP)}, device_id_type=MESH
        )
    pl.semaphore_wait(barrier, FSDP - 1 + TP - 1)


def to_fsdp(src, dst, send, recv, where):
    return pltpu.make_async_remote_copy(
        src_ref=src,
        dst_ref=dst,
        send_sem=send,
        recv_sem=recv,
        device_id={"fsdp": where},
        device_id_type=MESH,
    )


def to_tp(src, dst, send, recv, where):
    return pltpu.make_async_remote_copy(
        src_ref=src,
        dst_ref=dst,
        send_sem=send,
        recv_sem=recv,
        device_id={"tp": where},
        device_id_type=MESH,
    )


def nn(a, b):
    return jnp.dot(a, b, preferred_element_type=F32)


def nt(a, b):
    return lax.dot_general(a, b, (((1,), (1,)), ((), ())), preferred_element_type=F32)


def tn(a, b):
    return lax.dot_general(a, b, (((0,), (0,)), ((), ())), preferred_element_type=F32)


def lanes(shape):
    return lax.broadcasted_iota(jnp.int32, shape, len(shape) - 1)


def rows_of(shape):
    return lax.broadcasted_iota(jnp.int32, shape, 0)


def half_swap(v):
    width = v.shape[-1]
    front = lanes(v.shape) % HEAD_SIZE < HEAD_SIZE // 2
    ahead = pltpu.roll(v, width - HEAD_SIZE // 2, 1)
    behind = pltpu.roll(v, HEAD_SIZE // 2, 1)
    return jnp.where(front, -ahead, behind)


def wide_table(table, width):
    return jnp.concatenate([table] * (width // 128), axis=1)


def pick(slot_ref, experts, count):
    parts = []
    for e in experts:
        row = slot_ref[pl.ds(e, 1), :]
        parts.append(jnp.broadcast_to(row, (count, row.shape[1])))
    both = jnp.concatenate(parts, axis=0)
    want = (rows_of(both.shape) % count).astype(F32)
    return (both == want).astype(BF16)


def forward_kernel(
    packed_ref, inputs_ref, seg_ref, routes_ref, blocks_ref, cot_ref,
    middle_ref, normed_two_ref, gates_ref, slot_ref, weights_ref, cot_main_ref, cot_spare_ref,
    packed_all_ref, heads_ref, normed_all_ref, attended_ref, cos_ref, sin_ref,
    inputs_all, blocks_in, send_main, send_spare, branch_out, branch_in,
    packed_send, packed_recv, blocks_send, blocks_recv, main_send, main_recv, spare_send, spare_recv,
    inputs_send, inputs_recv, weights_send, weights_recv, branch_send, branch_recv, own_sem,
):
    me, tp = lax.axis_index("fsdp"), lax.axis_index("tp")
    rows, width = inputs_ref.shape
    total = seg_ref.shape[1]
    greet(me, tp)

    def packed_copy(k):
        return to_fsdp(
            packed_ref, packed_all_ref.at[me], packed_send.at[k], packed_recv.at[k], peer(me, k)
        )

    def inputs_copy(k):
        return to_tp(
            inputs_ref, inputs_all.at[tp], inputs_send.at[k], inputs_recv.at[k], lax.rem(tp + k, TP)
        )

    def blocks_copy(k):
        p = peer(me, k)
        return to_fsdp(blocks_ref.at[p], blocks_in.at[me], blocks_send.at[k], blocks_recv.at[k], p)

    def main_copy(k):
        return to_fsdp(
            send_main.at[k], cot_main_ref.at[k], main_send.at[k], main_recv.at[k], peer(me, k)
        )

    def spare_copy(k):
        return to_fsdp(
            send_spare.at[k], cot_spare_ref.at[k], spare_send.at[k], spare_recv.at[k], peer(me, k)
        )

    def branch_copy(k):
        q = lax.rem(tp + k, TP)
        return to_tp(
            branch_out.at[q], branch_in.at[k], branch_send.at[k], branch_recv.at[k], q
        )

    for k in (2, 1, 3):
        inputs_copy(k).start()
    loop(1, FSDP, lambda k: packed_copy(k).start())
    loop(1, FSDP, lambda k: blocks_copy(k).start())
    keep = [
        pltpu.make_async_copy(packed_ref, packed_all_ref.at[me], own_sem.at[0]),
        pltpu.make_async_copy(inputs_ref, inputs_all.at[tp], own_sem.at[1]),
        pltpu.make_async_copy(blocks_ref.at[me], blocks_in.at[me], own_sem.at[2]),
    ]
    for copy in keep:
        copy.start()

    at = lanes((rows, 128))
    member = jnp.zeros((rows, 128), F32)
    for k in range(TOP):
        member = member + (routes_ref[:, k : k + 1] == at).astype(F32)
    earlier = (rows_of((rows, rows)) > lanes((rows, rows))).astype(BF16)
    slot = nn(earlier, member.astype(BF16))
    slot = jnp.where(member > 0, slot, -1.0)
    slot_ref[...] = jnp.transpose(slot)[:EXPERTS]

    def some_rows(i):
        hot = pick(slot_ref, [peer(me, 4 * i + j) for j in range(4)], 40)
        out = nn(hot, cot_ref[...])
        for j in range(4):
            send_main[4 * i + j] = out[40 * j : 40 * j + 32].astype(BF16)
            send_spare[4 * i + j] = out[40 * j + 32 : 40 * j + 33]

        def go(k):
            main_copy(k).start()
            spare_copy(k).start()

        loop(jnp.maximum(4 * i, 1), 4 * i + 4, go)

    loop(0, FSDP // 4, some_rows)
    cot_main_ref[0] = send_main[0]
    cot_spare_ref[0] = send_spare[0]

    seg_row = jnp.broadcast_to(seg_ref[...].astype(F32), (128, total))
    seg_col = jnp.transpose(seg_row)[:, :1]
    same = (seg_col == seg_row[:1]) & (rows_of((total, total)) >= lanes((total, total)))
    allowed = same.astype(F32)
    place = jnp.sum(allowed, axis=1, keepdims=True) - 1.0
    halves = (lanes((1, 128)) % (HEAD_SIZE // 2)).astype(F32)
    rate = jnp.exp(halves * (-2.0 * math.log(ROPE_BASE) / HEAD_SIZE))
    angle = place * rate
    cos_ref[...] = jnp.cos(angle)
    sin_ref[...] = jnp.sin(angle)

    for k in range(1, TP):
        inputs_copy(k).wait_recv()
    keep[1].wait()
    wide = inputs_all[...].reshape(total, width).astype(F32)
    inverse = lax.rsqrt(jnp.mean(wide * wide, axis=-1, keepdims=True) + EPSILON)

    loop(1, FSDP, lambda k: packed_copy(k).wait_recv())
    keep[0].wait()
    tail = jnp.transpose(packed_all_ref[:, :, 768:896].reshape(width, 128).astype(F32))
    normed = (wide * inverse * tail[EXPERTS : EXPERTS + 1]).astype(BF16)
    normed_all_ref[...] = normed
    lin = nn(normed, packed_all_ref[:, :, 0:512].reshape(width, 512))
    turn = lin[:, :384]
    turned = turn * wide_table(cos_ref[...], 384) + half_swap(turn) * wide_table(sin_ref[...], 384)
    heads_ref[:, :384] = turned.astype(BF16)
    heads_ref[:, 384:] = lin[:, 384:].astype(BF16)
    outs = []
    for h in range(4):
        g = h // 2
        q = heads_ref[:, 64 * h : 64 * h + 64]
        key = heads_ref[:, 256 + 64 * g : 320 + 64 * g]
        value = heads_ref[:, 384 + 64 * g : 448 + 64 * g]
        scores = jnp.where(allowed > 0, nt(q, key) * HEAD_SIZE ** (-0.5), MASKED)
        top = jnp.max(scores, axis=1, keepdims=True)
        grown = jnp.exp(scores - top)
        shares = (grown * (1.0 / jnp.sum(grown, axis=1, keepdims=True))).astype(BF16)
        outs.append(nn(shares, value))
    attended = jnp.concatenate(outs, axis=1).astype(BF16)
    attended_ref[...] = attended
    branch = nt(attended, packed_all_ref[:, :, 512:768].reshape(width, 256))
    branch_out[...] = branch.astype(BF16).reshape(TP, rows, width)
    for k in (2, 1, 3):
        branch_copy(k).start()

    loop(1, FSDP, lambda k: blocks_copy(k).wait_recv())
    keep[2].wait()
    sibling = tp + 1 - 2 * lax.rem(tp, 2)
    across = lax.rem(tp + 2, TP)
    first = to_tp(blocks_in, weights_ref.at[tp], weights_send.at[0], weights_recv.at[0], across)
    second = to_tp(blocks_in, weights_ref.at[tp], weights_send.at[1], weights_recv.at[1], sibling)
    third = to_tp(
        weights_ref.at[across], weights_ref.at[across], weights_send.at[2], weights_recv.at[2], sibling
    )
    first.start()
    second.start()
    mine = pltpu.make_async_copy(blocks_in, weights_ref.at[tp], own_sem.at[3])
    mine.start()

    for k in range(1, TP):
        branch_copy(k).wait_recv()
    middle = inputs_ref[...].astype(F32) + branch_out[tp].astype(F32)
    for k in range(1, TP):
        middle = middle + branch_in[k].astype(F32)
    middle_ref[...] = middle
    inverse_two = lax.rsqrt(jnp.mean(middle * middle, axis=-1, keepdims=True) + EPSILON)
    normed_two = (middle * inverse_two * tail[EXPERTS + 1 : EXPERTS + 2]).astype(BF16)
    normed_two_ref[...] = normed_two
    logits = nn(normed_two, packed_all_ref[:, :, 768:896].reshape(width, 128))
    logits = jnp.where(member > 0, logits, MASKED)
    grown = jnp.exp(logits - jnp.max(logits, axis=1, keepdims=True)) * member
    gates_ref[...] = grown / jnp.sum(grown, axis=1, keepdims=True)

    first.wait_recv()
    third.start()

    def got(k):
        main_copy(k).wait_recv()
        spare_copy(k).wait_recv()

    loop(1, FSDP, got)
    second.wait_recv()
    third.wait_recv()
    mine.wait()

    def gone(k):
        packed_copy(k).wait_send()
        blocks_copy(k).wait_send()
        main_copy(k).wait_send()
        spare_copy(k).wait_send()

    loop(1, FSDP, gone)
    for k in range(1, TP):
        inputs_copy(k).wait_send()
        branch_copy(k).wait_send()
    for copy in (first, second, third):
        copy.wait_send()


def shape(dims, kind):
    return jax.ShapeDtypeStruct(dims, kind)


def dma(count):
    return pltpu.SemaphoreType.DMA((count,))


def forward(packed, inputs, seg, routes, blocks, cot):
    rows, width = inputs.shape
    total = seg.shape[1]
    vmem = pl.BlockSpec(memory_space=pltpu.VMEM)
    out = (
        shape((rows, width), F32),
        shape((rows, width), BF16),
        shape((rows, 128), F32),
        shape((EXPERTS, rows), F32),
        shape((TP, *blocks.shape), BF16),
        shape((FSDP, 32, width), BF16),
        shape((FSDP, 1, width), F32),
        shape((FSDP, *packed.shape), BF16),
        shape((total, 512), BF16),
        shape((total, width), BF16),
        shape((total, 256), BF16),
        shape((total, 128), F32),
        shape((total, 128), F32),
    )
    return pl.pallas_call(
        forward_kernel,
        out_shape=out,
        in_specs=[vmem] * 6,
        out_specs=[vmem] * len(out),
        scratch_shapes=[
            pltpu.VMEM((TP, rows, width), BF16),
            pltpu.VMEM(blocks.shape, BF16),
            pltpu.VMEM((FSDP, 32, width), BF16),
            pltpu.VMEM((FSDP, 1, width), F32),
            pltpu.VMEM((TP, rows, width), BF16),
            pltpu.VMEM((TP, rows, width), BF16),
            *[dma(FSDP)] * 8,
            *[dma(TP)] * 6,
            dma(4),
        ],
        compiler_params=pltpu.CompilerParams(
            collective_id=1, has_side_effects=True, vmem_limit_bytes=56 * 2**20
        ),
        name="attention_forward",
    )(packed, inputs, seg, routes, blocks, cot)


def greet_fsdp(me):
    barrier = pltpu.get_barrier_semaphore()
    loop(
        1,
        FSDP,
        lambda k: pl.semaphore_signal(
            barrier, inc=1, device_id={"fsdp": peer(me, k)}, device_id_type=MESH
        ),
    )
    pl.semaphore_wait(barrier, FSDP - 1)


def to_column(table, count):
    n = table.shape[0]
    spread = jnp.broadcast_to(table[:, None, :], (n, count, 128)).reshape(n * count, 128)
    mine = lanes(spread.shape) == rows_of(spread.shape) % count
    return jnp.sum(jnp.where(mine, spread, 0.0), axis=1, keepdims=True)


def to_table(column, count):
    n = column.shape[0] // count
    spread = jnp.broadcast_to(column, (n * count, 128))
    mine = lanes(spread.shape) == rows_of(spread.shape) % count
    return jnp.sum(jnp.where(mine, spread, 0.0).reshape(n, count, 128), axis=1)


def expert_kernel(
    normed_two_ref, gates_ref, slot_ref, weights_ref, cot_main_ref, cot_spare_ref,
    middle_ref, cot_ref, tail_ref,
    out_main_ref, out_spare_ref, grads_ref, grad_middle_ref, router_part_ref, second_ref,
    hot_main_ref, hot_spare_ref,
    gate_mat, up_mat, down_mat, gate_t, row_send, spare_send, row_in, spare_in,
    back_send, back_spare_send, back_in, back_spare_in,
    hidden_ref, dgate_ref, dup_ref, ghidden_ref, sel_ref, gg_ref,
    row_s, row_r, spare_s, spare_r, back_s, back_r, bspare_s, bspare_r,
):
    me = lax.axis_index("fsdp")
    rows, width = normed_two_ref.shape
    main = FSDP * 32
    greet_fsdp(me)

    def row_copy(k):
        return to_fsdp(row_send.at[k], row_in.at[k], row_s.at[k], row_r.at[k], peer(me, k))

    def spare_copy(k):
        return to_fsdp(spare_send.at[k], spare_in.at[k], spare_s.at[k], spare_r.at[k], peer(me, k))

    def back_copy(k):
        return to_fsdp(back_send.at[k], back_in.at[k], back_s.at[k], back_r.at[k], giver(me, k))

    def bspare_copy(k):
        return to_fsdp(
            back_spare_send.at[k], back_spare_in.at[k], bspare_s.at[k], bspare_r.at[k], giver(me, k)
        )

    gates_low = gates_ref[...].astype(BF16).astype(F32)
    gate_t[...] = jnp.transpose(gates_low)[:EXPERTS]

    def some_rows(i):
        experts = [peer(me, 4 * i + j) for j in range(4)]
        hot = pick(slot_ref, experts, 40)
        out = nn(hot, normed_two_ref[...])
        for j in range(4):
            k = 4 * i + j
            mine = hot[40 * j : 40 * j + 40].astype(F32)
            column = jnp.sum(mine * gate_t[pl.ds(experts[j], 1), :], axis=1, keepdims=True)
            row_send[k] = out[40 * j : 40 * j + 32].astype(BF16)
            spare_send[k, :, :1024] = out[40 * j + 32 : 40 * j + 33]
            spare_send[k, :, 1024:] = to_table(column, 40)
            hot_main_ref[k] = hot[40 * j : 40 * j + 32]
            hot_spare_ref[pl.ds(k, 1), :] = mine[32:33]

        def go(k):
            row_copy(k).start()
            spare_copy(k).start()

        loop(jnp.maximum(4 * i, 1), 4 * i + 4, go)

    loop(0, FSDP // 4, some_rows)
    row_in[0] = row_send[0]
    spare_in[0] = spare_send[0]

    for j in range(TP):
        cols = slice(128 * j, 128 * j + 128)
        gate_mat[:, cols] = weights_ref[j, :, 0:32, :].reshape(width, 128)
        up_mat[:, cols] = weights_ref[j, :, 32:64, :].reshape(width, 128)
        down_mat[:, cols] = weights_ref[j, :, 64:96, :].reshape(width, 128)

    def hidden_grads(i):
        cot_rows = cot_main_ref[pl.ds(8 * i, 8)].reshape(256, width)
        ghidden_ref[pl.ds(256 * i, 256), :] = nn(cot_rows, down_mat[...])

    loop(0, 4, hidden_grads)
    cot_spare = cot_spare_ref[...].reshape(FSDP, width).astype(BF16)
    ghidden_ref[pl.ds(main, FSDP), :] = nn(cot_spare, down_mat[...])

    def expert_rows(x, gate, where):
        gate_act = nn(x, gate_mat[...])
        up_act = nn(x, up_mat[...])
        grad_hidden = ghidden_ref[where, :]
        sigmoid_gate = 1.0 / (1.0 + jnp.exp(-gate_act))
        silu_gate = gate_act * sigmoid_gate
        both = silu_gate * up_act
        hidden_ref[where, :] = (both * gate).astype(BF16)
        grad_prod = grad_hidden * gate
        dgate = (
            grad_prod * up_act * sigmoid_gate * (1.0 + gate_act * (1.0 - sigmoid_gate))
        ).astype(BF16)
        dup = (grad_prod * silu_gate).astype(BF16)
        dgate_ref[where, :] = dgate
        dup_ref[where, :] = dup
        grad_in = nt(dgate, gate_mat[...]) + nt(dup, up_mat[...])
        return grad_in, jnp.sum(both * grad_hidden, axis=1, keepdims=True)

    def some_experts(i):
        def got(k):
            row_copy(k).wait_recv()
            spare_copy(k).wait_recv()

        loop(jnp.maximum(8 * i, 1), 8 * i + 8, got)
        x = row_in[pl.ds(8 * i, 8)].reshape(256, width)
        gate = to_column(spare_in[pl.ds(8 * i, 8), :, 1024:].reshape(8, 128), 32)
        grad_in, sel = expert_rows(x, gate, pl.ds(256 * i, 256))
        back_send[pl.ds(8 * i, 8)] = grad_in.astype(BF16).reshape(8, 32, width)
        sel_ref[pl.ds(8 * i, 8), :] = to_table(sel, 32)
        loop(jnp.maximum(8 * i, 1), 8 * i + 8, lambda k: back_copy(k).start())

    loop(0, 4, some_experts)
    spare = spare_in[...].reshape(FSDP, 1152)
    spare_gate = spare[:, 1056:1057]
    spare_rows = spare[:, :1024].astype(BF16)
    grad_in, sel = expert_rows(spare_rows, spare_gate, pl.ds(main, FSDP))
    sel_all = jnp.where(lanes((FSDP, 128)) == 32, sel, sel_ref[...])
    for k in range(FSDP):
        back_spare_send[k, :, :1024] = grad_in[k : k + 1]
        back_spare_send[k, :, 1024:] = sel_all[k : k + 1]
    loop(1, FSDP, lambda k: bspare_copy(k).start())
    back_in[0] = back_send[0]
    back_spare_in[0] = back_spare_send[0]

    def outputs(i):
        out = nt(hidden_ref[pl.ds(256 * i, 256), :], down_mat[...])
        out_main_ref[pl.ds(8 * i, 8)] = out.astype(BF16).reshape(8, 32, width)

    loop(0, 4, outputs)
    out = nt(hidden_ref[pl.ds(main, FSDP), :], down_mat[...])
    for k in range(FSDP):
        out_spare_ref[k] = out[k : k + 1]

    def weight_grads(i):
        at = pl.ds(pl.multiple_of(256 * i, 256), 256)
        x = row_in[:, :, at].reshape(main, 256)
        x_spare = spare_in[:, :, at].reshape(FSDP, 256).astype(BF16)
        c = cot_main_ref[:, :, at].reshape(main, 256)
        c_spare = cot_spare_ref[:, :, at].reshape(FSDP, 256).astype(BF16)
        for m, (a, a_spare, b) in enumerate(
            ((x, x_spare, dgate_ref), (x, x_spare, dup_ref), (c, c_spare, hidden_ref))
        ):
            part = tn(a, b[pl.ds(0, main), :]) + tn(a_spare, b[pl.ds(main, FSDP), :])
            part = part.astype(BF16)
            for j in range(TP):
                grads_ref[j, pl.ds(8 * i, 8), 32 * m : 32 * m + 32, :] = part[
                    :, 128 * j : 128 * j + 128
                ].reshape(8, 32, 128)

    loop(0, 4, weight_grads)

    def back_got(k):
        back_copy(k).wait_recv()
        bspare_copy(k).wait_recv()

    loop(1, FSDP, back_got)
    hot = hot_main_ref[...].reshape(main, rows)
    hot_spare = hot_spare_ref[...]
    back_spare = back_spare_in[...].reshape(FSDP, 1152)
    grad_rows = tn(hot, back_in[...].reshape(main, width)) + tn(
        hot_spare.astype(BF16), back_spare[:, :1024].astype(BF16)
    )
    sel = back_spare[:, 1024:]
    by_slot = jnp.sum(
        (hot.astype(F32) * to_column(sel, 32)).reshape(FSDP, 32, rows), axis=1
    ) + hot_spare * sel[:, 32:33]
    gg_ref[...] = jnp.zeros_like(gg_ref)
    for k in range(FSDP):
        gg_ref[pl.ds(peer(me, k), 1), :] = by_slot[k : k + 1]
    grad_gates = jnp.transpose(gg_ref[...])
    gates = gates_ref[...]
    grad_chosen = gates * (grad_gates - jnp.sum(gates * grad_gates, axis=1, keepdims=True))
    grad_logits = grad_chosen.astype(BF16)
    tail = tail_ref[...].reshape(width, 128)
    gain_two = jnp.transpose(tail.astype(F32))[EXPERTS + 1 : EXPERTS + 2]
    router_part_ref[...] = tn(normed_two_ref[...], grad_logits)
    dy = grad_rows + nt(grad_logits, tail)
    middle = middle_ref[...]
    inverse = lax.rsqrt(jnp.mean(middle * middle, axis=-1, keepdims=True) + EPSILON)
    scaled = dy * gain_two
    second_ref[...] = jnp.sum(dy * middle * inverse, axis=0, keepdims=True)
    grad_middle_ref[...] = (
        cot_ref[...].astype(F32)
        + inverse * scaled
        - middle
        * inverse
        * inverse
        * inverse
        * jnp.mean(scaled * middle, axis=-1, keepdims=True)
    )

    def gone(k):
        row_copy(k).wait_send()
        spare_copy(k).wait_send()
        back_copy(k).wait_send()
        bspare_copy(k).wait_send()

    loop(1, FSDP, gone)


def experts(normed_two, gates, slot, weights, cot_main, cot_spare, middle, cot, tail):
    rows, width = normed_two.shape
    hidden = 128 * TP
    slots = FSDP * SPARE
    vmem = pl.BlockSpec(memory_space=pltpu.VMEM)
    out = (
        shape((FSDP, 32, width), BF16),
        shape((FSDP, 1, width), F32),
        shape(weights.shape, BF16),
        shape((rows, width), F32),
        shape((width, 128), F32),
        shape((1, width), F32),
        shape((FSDP, 32, rows), BF16),
        shape((FSDP, rows), F32),
    )
    return pl.pallas_call(
        expert_kernel,
        out_shape=out,
        in_specs=[vmem] * 9,
        out_specs=[vmem] * len(out),
        scratch_shapes=[
            *[pltpu.VMEM((width, hidden), BF16)] * 3,
            pltpu.VMEM((EXPERTS, rows), F32),
            *[pltpu.VMEM((FSDP, 32, width), BF16), pltpu.VMEM((FSDP, 1, width + 128), F32)] * 4,
            *[pltpu.VMEM((slots, hidden), BF16)] * 3,
            pltpu.VMEM((slots, hidden), F32),
            pltpu.VMEM((FSDP, 128), F32),
            pltpu.VMEM((128, 128), F32),
            *[dma(FSDP)] * 8,
        ],
        compiler_params=pltpu.CompilerParams(
            collective_id=2, has_side_effects=True, vmem_limit_bytes=56 * 2**20
        ),
        name="experts",
    )(normed_two, gates, slot, weights, cot_main, cot_spare, middle, cot, tail)


def backward_kernel(
    grad_middle_ref, packed_all_ref, heads_ref, normed_all_ref, attended_ref, cos_ref, sin_ref,
    seg_ref, out_main_ref, out_spare_ref, grads_ref, middle_ref, hot_main_ref, hot_spare_ref,
    inputs_ref, router_part_ref, second_ref,
    output_ref, grad_inputs_ref, sums_ref, weight_grads_ref,
    branch_own, branch_all, out_in, out_spare_in, pair_in, across_send, across_in, dw_send, dw_in,
    normed_send, normed_in, sums_send, sums_in, small_own, small_in,
    branch_s, branch_r, out_s, out_r, spare_s, spare_r, pair_s, pair_r, across_s, across_r,
    dw_s, dw_r, normed_s, normed_r, sums_s, sums_r, small_s, small_r,
):
    me, tp = lax.axis_index("fsdp"), lax.axis_index("tp")
    rows, width = inputs_ref.shape
    total = seg_ref.shape[1]
    core = lax.rem(tp, 2)
    sibling = tp + 1 - 2 * core
    across = lax.rem(tp + 2, TP)
    greet(me, tp)

    def branch_copy(k):
        return to_tp(
            branch_own, branch_all.at[tp], branch_s.at[k], branch_r.at[k], lax.rem(tp + k, TP)
        )

    def out_copy(k):
        return to_fsdp(out_main_ref.at[k], out_in.at[k], out_s.at[k], out_r.at[k], giver(me, k))

    def spare_copy(k):
        return to_fsdp(
            out_spare_ref.at[k], out_spare_in.at[k], spare_s.at[k], spare_r.at[k], giver(me, k)
        )

    def pair_copy(x):
        return to_tp(
            grads_ref.at[2 * x + 1 - core], pair_in.at[x], pair_s.at[x], pair_r.at[x], sibling
        )

    across_copy = to_tp(across_send, across_in, across_s.at[0], across_r.at[0], across)

    def dw_copy(k):
        p = peer(me, k)
        return to_fsdp(dw_send.at[p], dw_in.at[me], dw_s.at[k], dw_r.at[k], p)

    def normed_copy(k):
        q = lax.rem(tp + k, TP)
        return to_tp(normed_send.at[q], normed_in.at[k], normed_s.at[k], normed_r.at[k], q)

    def sums_copy(k):
        p = peer(me, k)
        return to_fsdp(sums_send.at[p], sums_in.at[k], sums_s.at[k], sums_r.at[k], p)

    def small_copy(k):
        return to_tp(small_own, small_in.at[k], small_s.at[k], small_r.at[k], lax.rem(tp + k, TP))

    grad_middle = grad_middle_ref[...]
    branch_own[...] = grad_middle.astype(BF16)
    for k in (2, 1, 3):
        branch_copy(k).start()
    for x in range(2):
        pair_copy(x).start()

    def out_go(k):
        out_copy(k).start()
        spare_copy(k).start()

    loop(1, FSDP, out_go)
    branch_all[tp] = branch_own[...]
    out_in[0] = out_main_ref[0]
    out_spare_in[0] = out_spare_ref[0]

    for x in range(2):
        pair_copy(x).wait_recv()
    far = 1 - tp // 2
    across_send[...] = (
        grads_ref[2 * far + core].astype(F32) + pair_in[far].astype(F32)
    ).astype(BF16)
    across_copy.start()

    seg_row = jnp.broadcast_to(seg_ref[...].astype(F32), (128, total))
    seg_col = jnp.transpose(seg_row)[:, :1]
    allowed = (
        (seg_col == seg_row[:1]) & (rows_of((total, total)) >= lanes((total, total)))
    ).astype(F32)

    for k in range(1, TP):
        branch_copy(k).wait_recv()
    branch = branch_all[...].reshape(total, width)
    out_part = tn(branch, attended_ref[...])
    grad_attended = nn(branch, packed_all_ref[:, :, 512:768].reshape(width, 256)).astype(BF16)
    scale = HEAD_SIZE ** (-0.5)
    dq, dk, dv = [], [], []
    for g in range(2):
        key = heads_ref[:, 256 + 64 * g : 320 + 64 * g]
        value = heads_ref[:, 384 + 64 * g : 448 + 64 * g]
        dk_sum, dv_sum = None, None
        for h in (2 * g, 2 * g + 1):
            q = heads_ref[:, 64 * h : 64 * h + 64]
            da = grad_attended[:, 64 * h : 64 * h + 64]
            scores = jnp.where(allowed > 0, nt(q, key) * scale, MASKED)
            top = jnp.max(scores, axis=1, keepdims=True)
            grown = jnp.exp(scores - top)
            whole = grown * (1.0 / jnp.sum(grown, axis=1, keepdims=True))
            grad_shares = nt(da, value)
            inner = jnp.sum(whole * grad_shares, axis=1, keepdims=True)
            grad_scores = (whole * (grad_shares - inner)).astype(BF16)
            dq.append(nn(grad_scores, key) * scale)
            dk_one = tn(grad_scores, q) * scale
            dv_one = tn(whole.astype(BF16), da)
            dk_sum = dk_one if dk_sum is None else dk_sum + dk_one
            dv_sum = dv_one if dv_sum is None else dv_sum + dv_one
        dk.append(dk_sum)
        dv.append(dv_sum)
    turned = jnp.concatenate(dq + dk, axis=1)
    turn = turned * wide_table(cos_ref[...], 384) - half_swap(turned) * wide_table(
        sin_ref[...], 384
    )
    grad_lin = jnp.concatenate([turn] + dv, axis=1).astype(BF16)
    grad_normed = nt(grad_lin, packed_all_ref[:, :, 0:512].reshape(width, 512))
    normed_send[...] = grad_normed.astype(BF16).reshape(TP, rows, width)
    for k in (2, 1, 3):
        normed_copy(k).start()
    gain_one = jnp.transpose(packed_all_ref[:, :, 768:896].reshape(width, 128).astype(F32))[
        EXPERTS : EXPERTS + 1
    ]
    first = jnp.sum(grad_normed * normed_all_ref[...].astype(F32), axis=0, keepdims=True) / gain_one

    qkv_part = tn(normed_all_ref[...], grad_lin)
    sums_send[:, :, 0:512] = qkv_part.astype(BF16).reshape(FSDP, 32, 512)
    sums_send[:, :, 512:768] = out_part.astype(BF16).reshape(FSDP, 32, 256)
    at = rows_of((128, width))
    gains = jnp.where(at == EXPERTS, first, 0.0) + jnp.where(at == EXPERTS + 1, second_ref[...], 0.0)
    small = router_part_ref[...] + jnp.transpose(gains)
    sums_send[:, :, 768:896] = small.astype(BF16).reshape(FSDP, 32, 128)
    loop(1, FSDP, lambda k: sums_copy(k).start())
    sums_in[0] = sums_send[me]

    across_copy.wait_recv()
    near = tp // 2
    dw_send[...] = (
        grads_ref[tp].astype(F32) + pair_in[near].astype(F32) + across_in[...].astype(F32)
    ).astype(BF16)
    loop(1, FSDP, lambda k: dw_copy(k).start())
    dw_in[me] = dw_send[me]

    for k in range(1, TP):
        normed_copy(k).wait_recv()
    dy = normed_send[tp].astype(F32)
    for k in range(1, TP):
        dy = dy + normed_in[k].astype(F32)
    wide = inputs_ref[...].astype(F32)
    inverse = lax.rsqrt(jnp.mean(wide * wide, axis=-1, keepdims=True) + EPSILON)
    scaled = dy * gain_one
    grad_inputs_ref[...] = (
        grad_middle
        + inverse * scaled
        - wide
        * inverse
        * inverse
        * inverse
        * jnp.mean(scaled * wide, axis=-1, keepdims=True)
    )

    def out_got(k):
        out_copy(k).wait_recv()
        spare_copy(k).wait_recv()

    loop(1, FSDP, out_got)
    hot = hot_main_ref[...].reshape(FSDP * 32, rows)
    output_ref[...] = (
        middle_ref[...]
        + tn(hot, out_in[...].reshape(FSDP * 32, width))
        + tn(hot_spare_ref[...].astype(BF16), out_spare_in[...].reshape(FSDP, width).astype(BF16))
    ).astype(BF16)

    loop(1, FSDP, lambda k: sums_copy(k).wait_recv())
    sums = jnp.sum(sums_in[...].astype(F32), axis=0)
    sums_ref[:, :768] = sums[:, :768]
    small_own[...] = sums[:, 768:]
    for k in (2, 1, 3):
        small_copy(k).start()
    loop(1, FSDP, lambda k: dw_copy(k).wait_recv())
    weight_grads_ref[...] = dw_in[...].astype(F32)
    for k in range(1, TP):
        small_copy(k).wait_recv()
    sums_ref[:, 768:] = small_own[...] + small_in[1] + small_in[2] + small_in[3]

    def gone(k):
        out_copy(k).wait_send()
        spare_copy(k).wait_send()
        sums_copy(k).wait_send()
        dw_copy(k).wait_send()

    loop(1, FSDP, gone)
    for k in range(1, TP):
        branch_copy(k).wait_send()
        normed_copy(k).wait_send()
        small_copy(k).wait_send()
    for x in range(2):
        pair_copy(x).wait_send()
    across_copy.wait_send()


def backward(*operands):
    grads, inputs, packed_all = operands[10], operands[14], operands[1]
    rows, width = inputs.shape
    vmem = pl.BlockSpec(memory_space=pltpu.VMEM)
    out = (
        shape((rows, width), BF16),
        shape((rows, width), F32),
        shape(packed_all.shape[1:], F32),
        shape(grads.shape[1:], F32),
    )
    return pl.pallas_call(
        backward_kernel,
        out_shape=out,
        in_specs=[vmem] * len(operands),
        out_specs=[vmem] * len(out),
        scratch_shapes=[
            pltpu.VMEM((rows, width), BF16),
            pltpu.VMEM((TP, rows, width), BF16),
            pltpu.VMEM((FSDP, 32, width), BF16),
            pltpu.VMEM((FSDP, 1, width), F32),
            pltpu.VMEM((2, *grads.shape[1:]), BF16),
            *[pltpu.VMEM(grads.shape[1:], BF16)] * 4,
            *[pltpu.VMEM((TP, rows, width), BF16)] * 2,
            *[pltpu.VMEM(packed_all.shape, BF16)] * 2,
            pltpu.VMEM((32, 128), F32),
            pltpu.VMEM((TP, 32, 128), F32),
            *[dma(TP)] * 2,
            *[dma(FSDP)] * 4,
            *[dma(2)] * 2,
            *[dma(1)] * 2,
            *[dma(FSDP)] * 2,
            *[dma(TP)] * 2,
            *[dma(FSDP)] * 2,
            *[dma(TP)] * 2,
        ],
        compiler_params=pltpu.CompilerParams(
            collective_id=3, has_side_effects=True, vmem_limit_bytes=56 * 2**20
        ),
        name="attention_backward",
    )(*operands)


def per_device(
    inputs,
    segments,
    routes,
    query_weight,
    key_projection_weight,
    value_projection_weight,
    out_weight,
    router_weight,
    first_gain,
    second_gain,
    gate_weight,
    up_weight,
    down_weight,
    cotangent,
):
    row_count = inputs.shape[0]
    my_offset = lax.axis_index("tp") * row_count
    width_shard = query_weight.shape[0]
    q_cols, k_cols, o_cols = query_weight.shape[1], key_projection_weight.shape[1], out_weight.shape[0]

    wide = q_cols + 2 * k_cols + o_cols
    packed = jnp.concatenate(
        [
            query_weight,
            key_projection_weight,
            value_projection_weight,
            out_weight.T,
            router_weight,
            first_gain[:, None],
            second_gain[:, None],
            jnp.zeros((width_shard, 128 - EXPERTS - 2), BF16),
        ],
        axis=1,
    )
    blocks = jnp.concatenate(
        [gate_weight, up_weight, jnp.transpose(down_weight, (0, 2, 1))], axis=1
    )
    my_routes = lax.dynamic_slice_in_dim(routes, my_offset, row_count, 0)
    (
        middle, normed_two, gates, slot, weights, cot_main, cot_spare,
        packed_all, heads, normed_all, attended, cosine, sine,
    ) = forward(packed, inputs, segments, my_routes, blocks, cotangent)
    tail = packed_all[:, :, wide:]
    (
        out_main, out_spare, grads, grad_middle, router_part, second_part, hot_main, hot_spare
    ) = experts(normed_two, gates, slot, weights, cot_main, cot_spare, middle, cotangent, tail)
    output, grad_inputs, sums, weight_grads = backward(
        grad_middle, packed_all, heads, normed_all, attended, cosine, sine, segments,
        out_main, out_spare, grads, middle, hot_main, hot_spare, inputs, router_part, second_part,
    )
    return (
        output,
        grad_inputs,
        sums[:, :q_cols],
        sums[:, q_cols : q_cols + k_cols],
        sums[:, q_cols + k_cols : q_cols + 2 * k_cols],
        sums[:, q_cols + 2 * k_cols : wide].T,
        sums[:, wide : wide + EXPERTS],
        sums[:, wide + EXPERTS],
        sums[:, wide + EXPERTS + 1],
        weight_grads[:, :width_shard],
        weight_grads[:, width_shard : 2 * width_shard],
        jnp.transpose(weight_grads[:, 2 * width_shard :], (0, 2, 1)),
    )


def solution(mesh):
    return jax.shard_map(
        per_device,
        mesh=mesh,
        in_specs=(
            P(("fsdp", "tp"), None),
            P("fsdp", None),
            P("fsdp", None),
            P("fsdp", "tp"),
            P("fsdp", "tp"),
            P("fsdp", "tp"),
            P("tp", "fsdp"),
            P("fsdp", None),
            P("fsdp"),
            P("fsdp"),
            P(None, "fsdp", "tp"),
            P(None, "fsdp", "tp"),
            P(None, "tp", "fsdp"),
            P(("fsdp", "tp"), None),
        ),
        out_specs=(
            P(("fsdp", "tp"), None),
            P(("fsdp", "tp"), None),
            P("fsdp", "tp"),
            P("fsdp", "tp"),
            P("fsdp", "tp"),
            P("tp", "fsdp"),
            P("fsdp", None),
            P("fsdp"),
            P("fsdp"),
            P(None, "fsdp", "tp"),
            P(None, "fsdp", "tp"),
            P(None, "tp", "fsdp"),
        ),
        check_vma=False,
    )
```

```python
import math

import jax
import jax.numpy as jnp
from jax import lax
from jax.experimental import pallas as pl
from jax.experimental.pallas import tpu as pltpu
from jax.sharding import PartitionSpec as P

HEAD_SIZE = 64
EXPERTS = 32
TOP = 8


EPSILON = 1e-06
ROPE_BASE = 10000.0
MASKED = -1e30


MESH = pl.DeviceIdType.MESH
FSDP, TP, SPARE = 32, 4, 33
F32, BF16 = jnp.float32, jnp.bfloat16


def peer(me, k):
    z, x, y = me // 8, (me // 4) % 2, me % 4
    return ((z + k // 8) % 4 * 2 + (x + (k // 4) % 2) % 2) * 4 + (y + k % 4) % 4


def giver(me, k):
    z, x, y = me // 8, (me // 4) % 2, me % 4
    return ((z + 4 - k // 8) % 4 * 2 + (x + (k // 4) % 2) % 2) * 4 + (y + 4 - k % 4) % 4


def side(tp, k):
    return lax.rem(tp + 2 * ((k // 4) % 2), TP)


def loop(low, high, step):
    def body(k, carry):
        step(k)
        return carry

    lax.fori_loop(low, high, body, 0)


def greet(me, tp):
    barrier = pltpu.get_barrier_semaphore()

    def signal(k):
        for q in (tp, lax.rem(tp + 2, TP)):
            pl.semaphore_signal(
                barrier,
                inc=1,
                device_id={"fsdp": peer(me, k), "tp": q},
                device_id_type=MESH,
            )

    loop(1, FSDP, signal)
    for k in range(1, TP):
        pl.semaphore_signal(
            barrier, inc=1, device_id={"tp": lax.rem(tp + k, TP)}, device_id_type=MESH
        )
    pl.semaphore_wait(barrier, 2 * (FSDP - 1) + TP - 1)


def to_fsdp(src, dst, send, recv, where):
    return pltpu.make_async_remote_copy(
        src_ref=src,
        dst_ref=dst,
        send_sem=send,
        recv_sem=recv,
        device_id={"fsdp": where},
        device_id_type=MESH,
    )


def to_tp(src, dst, send, recv, where):
    return pltpu.make_async_remote_copy(
        src_ref=src,
        dst_ref=dst,
        send_sem=send,
        recv_sem=recv,
        device_id={"tp": where},
        device_id_type=MESH,
    )


def to_side(src, dst, send, recv, where, q):
    return pltpu.make_async_remote_copy(
        src_ref=src,
        dst_ref=dst,
        send_sem=send,
        recv_sem=recv,
        device_id={"fsdp": where, "tp": q},
        device_id_type=MESH,
    )


def nn(a, b):
    return jnp.dot(a, b, preferred_element_type=F32)


def nt(a, b):
    return lax.dot_general(a, b, (((1,), (1,)), ((), ())), preferred_element_type=F32)


def tn(a, b):
    return lax.dot_general(a, b, (((0,), (0,)), ((), ())), preferred_element_type=F32)


def lanes(shape):
    return lax.broadcasted_iota(jnp.int32, shape, len(shape) - 1)


def rows_of(shape):
    return lax.broadcasted_iota(jnp.int32, shape, 0)


def half_swap(v):
    width = v.shape[-1]
    front = lanes(v.shape) % HEAD_SIZE < HEAD_SIZE // 2
    ahead = pltpu.roll(v, width - HEAD_SIZE // 2, 1)
    behind = pltpu.roll(v, HEAD_SIZE // 2, 1)
    return jnp.where(front, -ahead, behind)


def wide_table(table, width):
    return jnp.concatenate([table] * (width // 128), axis=1)


def pick(slot_ref, experts, count):
    parts = []
    for e in experts:
        row = slot_ref[pl.ds(e, 1), :]
        parts.append(jnp.broadcast_to(row, (count, row.shape[1])))
    both = jnp.concatenate(parts, axis=0)
    want = (rows_of(both.shape) % count).astype(F32)
    return (both == want).astype(BF16)


def forward_kernel(
    packed_ref, inputs_ref, seg_ref, routes_ref, blocks_ref, cot_ref,
    middle_ref, normed_two_ref, gates_ref, slot_ref, weights_ref, cot_main_ref, cot_spare_ref,
    packed_all_ref, heads_ref, normed_all_ref, attended_ref, cos_ref, sin_ref,
    inputs_all, blocks_in, send_main, send_spare, branch_out, branch_in,
    packed_send, packed_recv, blocks_send, blocks_recv, main_send, main_recv, spare_send, spare_recv,
    inputs_send, inputs_recv, weights_send, weights_recv, branch_send, branch_recv, own_sem,
):
    me, tp = lax.axis_index("fsdp"), lax.axis_index("tp")
    rows, width = inputs_ref.shape
    total = seg_ref.shape[1]
    greet(me, tp)

    def packed_copy(k):
        return to_fsdp(
            packed_ref, packed_all_ref.at[me], packed_send.at[k], packed_recv.at[k], peer(me, k)
        )

    core = lax.rem(tp, 2)
    sibling = tp + 1 - 2 * core
    across = lax.rem(tp + 2, TP)

    def inputs_copy(k):
        block, where = ((tp, across), (tp, sibling), (across, sibling))[k]
        src = inputs_ref if k < 2 else inputs_all.at[block]
        return to_tp(src, inputs_all.at[block], inputs_send.at[k], inputs_recv.at[k], where)

    def blocks_copy(k):
        p = peer(me, k)
        return to_side(
            blocks_ref.at[p], blocks_in.at[me], blocks_send.at[k], blocks_recv.at[k], p, side(tp, k)
        )

    def main_copy(k):
        return to_side(
            send_main.at[k],
            cot_main_ref.at[k],
            main_send.at[k],
            main_recv.at[k],
            peer(me, k),
            side(tp, k),
        )

    def spare_copy(k):
        return to_side(
            send_spare.at[k],
            cot_spare_ref.at[k],
            spare_send.at[k],
            spare_recv.at[k],
            peer(me, k),
            side(tp, k),
        )

    def branch_copy(x):
        return to_tp(
            branch_out.at[2 * x + 1 - core],
            branch_in.at[x],
            branch_send.at[x],
            branch_recv.at[x],
            sibling,
        )

    branch_across = to_tp(
        branch_in.at[2], branch_in.at[3], branch_send.at[2], branch_recv.at[2], across
    )

    inputs_copy(0).start()
    inputs_copy(1).start()
    loop(1, FSDP, lambda k: packed_copy(k).start())
    loop(1, FSDP, lambda k: blocks_copy(k).start())
    keep = [
        pltpu.make_async_copy(packed_ref, packed_all_ref.at[me], own_sem.at[0]),
        pltpu.make_async_copy(inputs_ref, inputs_all.at[tp], own_sem.at[1]),
        pltpu.make_async_copy(blocks_ref.at[me], blocks_in.at[me], own_sem.at[2]),
    ]
    for copy in keep:
        copy.start()

    at = lanes((rows, 128))
    member = jnp.zeros((rows, 128), F32)
    for k in range(TOP):
        member = member + (routes_ref[:, k : k + 1] == at).astype(F32)
    earlier = (rows_of((rows, rows)) > lanes((rows, rows))).astype(BF16)
    slot = nn(earlier, member.astype(BF16))
    slot = jnp.where(member > 0, slot, -1.0)
    slot_ref[...] = jnp.transpose(slot)[:EXPERTS]

    def some_rows(i):
        hot = pick(slot_ref, [peer(me, 4 * i + j) for j in range(4)], 40)
        out = nn(hot, cot_ref[...])
        for j in range(4):
            send_main[4 * i + j] = out[40 * j : 40 * j + 32].astype(BF16)
            send_spare[4 * i + j] = out[40 * j + 32 : 40 * j + 33]

        def go(k):
            main_copy(k).start()
            spare_copy(k).start()

        loop(jnp.maximum(4 * i, 1), 4 * i + 4, go)

    loop(0, FSDP // 4, some_rows)
    cot_main_ref[0] = send_main[0]
    cot_spare_ref[0] = send_spare[0]

    seg_row = jnp.broadcast_to(seg_ref[...].astype(F32), (128, total))
    seg_col = jnp.transpose(seg_row)[:, :1]
    same = (seg_col == seg_row[:1]) & (rows_of((total, total)) >= lanes((total, total)))
    allowed = same.astype(F32)
    place = jnp.sum(allowed, axis=1, keepdims=True) - 1.0
    halves = (lanes((1, 128)) % (HEAD_SIZE // 2)).astype(F32)
    rate = jnp.exp(halves * (-2.0 * math.log(ROPE_BASE) / HEAD_SIZE))
    angle = place * rate
    cos_ref[...] = jnp.cos(angle)
    sin_ref[...] = jnp.sin(angle)

    inputs_copy(0).wait_recv()
    inputs_copy(2).start()
    inputs_copy(1).wait_recv()
    inputs_copy(2).wait_recv()
    keep[1].wait()
    wide = inputs_all[...].reshape(total, width).astype(F32)
    inverse = lax.rsqrt(jnp.mean(wide * wide, axis=-1, keepdims=True) + EPSILON)

    loop(1, FSDP, lambda k: packed_copy(k).wait_recv())
    keep[0].wait()
    tail = jnp.transpose(packed_all_ref[:, :, 768:896].reshape(width, 128).astype(F32))
    normed = (wide * inverse * tail[EXPERTS : EXPERTS + 1]).astype(BF16)
    normed_all_ref[...] = normed
    lin = nn(normed, packed_all_ref[:, :, 0:512].reshape(width, 512))
    turn = lin[:, :384]
    turned = turn * wide_table(cos_ref[...], 384) + half_swap(turn) * wide_table(sin_ref[...], 384)
    heads_ref[:, :384] = turned.astype(BF16)
    heads_ref[:, 384:] = lin[:, 384:].astype(BF16)
    outs = []
    for h in range(4):
        g = h // 2
        q = heads_ref[:, 64 * h : 64 * h + 64]
        key = heads_ref[:, 256 + 64 * g : 320 + 64 * g]
        value = heads_ref[:, 384 + 64 * g : 448 + 64 * g]
        scores = jnp.where(allowed > 0, nt(q, key) * HEAD_SIZE ** (-0.5), MASKED)
        top = jnp.max(scores, axis=1, keepdims=True)
        grown = jnp.exp(scores - top)
        shares = (grown * (1.0 / jnp.sum(grown, axis=1, keepdims=True))).astype(BF16)
        outs.append(nn(shares, value))
    attended = jnp.concatenate(outs, axis=1).astype(BF16)
    attended_ref[...] = attended
    branch = nt(attended, packed_all_ref[:, :, 512:768].reshape(width, 256))
    branch_out[...] = branch.astype(BF16).reshape(TP, rows, width)
    for x in range(2):
        branch_copy(x).start()
    for x in range(2):
        branch_copy(x).wait_recv()
    near = tp // 2
    far = 1 - near
    branch_in[2] = (
        branch_out[across].astype(F32) + branch_in[far].astype(F32)
    ).astype(BF16)
    branch_across.start()

    loop(1, FSDP, lambda k: blocks_copy(k).wait_recv())
    keep[2].wait()
    first = to_tp(blocks_in, weights_ref.at[tp], weights_send.at[0], weights_recv.at[0], across)
    second = to_tp(blocks_in, weights_ref.at[tp], weights_send.at[1], weights_recv.at[1], sibling)
    third = to_tp(
        weights_ref.at[across], weights_ref.at[across], weights_send.at[2], weights_recv.at[2], sibling
    )
    first.start()
    second.start()
    mine = pltpu.make_async_copy(blocks_in, weights_ref.at[tp], own_sem.at[3])
    mine.start()

    branch_across.wait_recv()
    middle = inputs_ref[...].astype(F32) + branch_out[tp].astype(F32)
    middle = middle + branch_in[near].astype(F32) + branch_in[3].astype(F32)
    middle_ref[...] = middle
    inverse_two = lax.rsqrt(jnp.mean(middle * middle, axis=-1, keepdims=True) + EPSILON)
    normed_two = (middle * inverse_two * tail[EXPERTS + 1 : EXPERTS + 2]).astype(BF16)
    normed_two_ref[...] = normed_two
    logits = nn(normed_two, packed_all_ref[:, :, 768:896].reshape(width, 128))
    logits = jnp.where(member > 0, logits, MASKED)
    grown = jnp.exp(logits - jnp.max(logits, axis=1, keepdims=True)) * member
    gates_ref[...] = grown / jnp.sum(grown, axis=1, keepdims=True)

    first.wait_recv()
    third.start()

    def got(k):
        main_copy(k).wait_recv()
        spare_copy(k).wait_recv()

    loop(1, FSDP, got)
    second.wait_recv()
    third.wait_recv()
    mine.wait()

    def gone(k):
        packed_copy(k).wait_send()
        blocks_copy(k).wait_send()
        main_copy(k).wait_send()
        spare_copy(k).wait_send()

    loop(1, FSDP, gone)
    for k in range(3):
        inputs_copy(k).wait_send()
    for x in range(2):
        branch_copy(x).wait_send()
    for copy in (branch_across, first, second, third):
        copy.wait_send()


def shape(dims, kind):
    return jax.ShapeDtypeStruct(dims, kind)


def dma(count):
    return pltpu.SemaphoreType.DMA((count,))


def forward(packed, inputs, seg, routes, blocks, cot):
    rows, width = inputs.shape
    total = seg.shape[1]
    vmem = pl.BlockSpec(memory_space=pltpu.VMEM)
    out = (
        shape((rows, width), F32),
        shape((rows, width), BF16),
        shape((rows, 128), F32),
        shape((EXPERTS, rows), F32),
        shape((TP, *blocks.shape), BF16),
        shape((FSDP, 32, width), BF16),
        shape((FSDP, 1, width), F32),
        shape((FSDP, *packed.shape), BF16),
        shape((total, 512), BF16),
        shape((total, width), BF16),
        shape((total, 256), BF16),
        shape((total, 128), F32),
        shape((total, 128), F32),
    )
    return pl.pallas_call(
        forward_kernel,
        out_shape=out,
        in_specs=[vmem] * 6,
        out_specs=[vmem] * len(out),
        scratch_shapes=[
            pltpu.VMEM((TP, rows, width), BF16),
            pltpu.VMEM(blocks.shape, BF16),
            pltpu.VMEM((FSDP, 32, width), BF16),
            pltpu.VMEM((FSDP, 1, width), F32),
            pltpu.VMEM((TP, rows, width), BF16),
            pltpu.VMEM((TP, rows, width), BF16),
            *[dma(FSDP)] * 8,
            *[dma(TP)] * 6,
            dma(4),
        ],
        compiler_params=pltpu.CompilerParams(
            collective_id=1, has_side_effects=True, vmem_limit_bytes=56 * 2**20
        ),
        name="attention_forward",
    )(packed, inputs, seg, routes, blocks, cot)


def greet_fsdp(me, tp):
    barrier = pltpu.get_barrier_semaphore()
    loop(
        1,
        FSDP,
        lambda k: pl.semaphore_signal(
            barrier,
            inc=1,
            device_id={"fsdp": peer(me, k), "tp": side(tp, k)},
            device_id_type=MESH,
        ),
    )
    pl.semaphore_wait(barrier, FSDP - 1)


def to_column(table, count):
    n = table.shape[0]
    spread = jnp.broadcast_to(table[:, None, :], (n, count, 128)).reshape(n * count, 128)
    mine = lanes(spread.shape) == rows_of(spread.shape) % count
    return jnp.sum(jnp.where(mine, spread, 0.0), axis=1, keepdims=True)


def to_table(column, count):
    n = column.shape[0] // count
    spread = jnp.broadcast_to(column, (n * count, 128))
    mine = lanes(spread.shape) == rows_of(spread.shape) % count
    return jnp.sum(jnp.where(mine, spread, 0.0).reshape(n, count, 128), axis=1)


def expert_kernel(
    normed_two_ref, gates_ref, slot_ref, weights_ref, cot_main_ref, cot_spare_ref,
    middle_ref, cot_ref, tail_ref,
    out_main_ref, out_spare_ref, grads_ref, grad_middle_ref, router_part_ref, second_ref,
    hot_main_ref, hot_spare_ref,
    gate_mat, up_mat, down_mat, gate_t, row_send, spare_send, row_in, spare_in,
    back_send, back_spare_send, back_in, back_spare_in,
    hidden_ref, dgate_ref, dup_ref, ghidden_ref, sel_ref, gg_ref,
    row_s, row_r, spare_s, spare_r, back_s, back_r, bspare_s, bspare_r,
):
    me, tp = lax.axis_index("fsdp"), lax.axis_index("tp")
    half = (me // 4) % 2
    rows, width = normed_two_ref.shape
    main = FSDP * 32
    greet_fsdp(me, tp)

    def row_copy(k):
        return to_side(
            row_send.at[k], row_in.at[k], row_s.at[k], row_r.at[k], peer(me, k), side(tp, k)
        )

    def spare_copy(k):
        return to_side(
            spare_send.at[k], spare_in.at[k], spare_s.at[k], spare_r.at[k], peer(me, k), side(tp, k)
        )

    def back_copy(k):
        return to_side(
            back_send.at[k], back_in.at[k], back_s.at[k], back_r.at[k], giver(me, k), side(tp, k)
        )

    def bspare_copy(k):
        return to_side(
            back_spare_send.at[k],
            back_spare_in.at[k],
            bspare_s.at[k],
            bspare_r.at[k],
            giver(me, k),
            side(tp, k),
        )

    gates_low = gates_ref[...].astype(BF16).astype(F32)
    gate_t[...] = jnp.transpose(gates_low)[:EXPERTS]

    def some_rows(i):
        experts = [peer(me, 4 * i + j) for j in range(4)]
        hot = pick(slot_ref, experts, 40)
        out = nn(hot, normed_two_ref[...])
        for j in range(4):
            k = 4 * i + j
            mine = hot[40 * j : 40 * j + 40].astype(F32)
            column = jnp.sum(mine * gate_t[pl.ds(experts[j], 1), :], axis=1, keepdims=True)
            row_send[k] = out[40 * j : 40 * j + 32].astype(BF16)
            spare_send[k, :, :1024] = out[40 * j + 32 : 40 * j + 33]
            spare_send[k, :, 1024:] = to_table(column, 40)
            hot_main_ref[k] = hot[40 * j : 40 * j + 32]
            hot_spare_ref[pl.ds(k, 1), :] = mine[32:33]

        def go(k):
            row_copy(k).start()
            spare_copy(k).start()

        loop(jnp.maximum(4 * i, 1), 4 * i + 4, go)

    loop(0, FSDP // 4, some_rows)
    row_in[0] = row_send[0]
    spare_in[0] = spare_send[0]

    def side_by_side(i):
        at = pl.ds(pl.multiple_of(128 * i, 128), 128)
        swap = 2 * lax.rem(half + i, 2)
        for j in range(TP):
            cols = slice(128 * j, 128 * j + 128)
            block = weights_ref[lax.rem(j + swap, TP), pl.ds(4 * i, 4)]
            gate_mat[at, cols] = block[:, 0:32].reshape(128, 128)
            up_mat[at, cols] = block[:, 32:64].reshape(128, 128)
            down_mat[at, cols] = block[:, 64:96].reshape(128, 128)

    loop(0, 8, side_by_side)

    def hidden_grads(i):
        cot_rows = cot_main_ref[pl.ds(8 * i, 8)].reshape(256, width)
        ghidden_ref[pl.ds(256 * i, 256), :] = nn(cot_rows, down_mat[...])

    loop(0, 4, hidden_grads)
    cot_spare = cot_spare_ref[...].reshape(FSDP, width).astype(BF16)
    ghidden_ref[pl.ds(main, FSDP), :] = nn(cot_spare, down_mat[...])

    def expert_rows(x, gate, where):
        gate_act = nn(x, gate_mat[...])
        up_act = nn(x, up_mat[...])
        grad_hidden = ghidden_ref[where, :]
        sigmoid_gate = 1.0 / (1.0 + jnp.exp(-gate_act))
        silu_gate = gate_act * sigmoid_gate
        both = silu_gate * up_act
        hidden_ref[where, :] = (both * gate).astype(BF16)
        grad_prod = grad_hidden * gate
        dgate = (
            grad_prod * up_act * sigmoid_gate * (1.0 + gate_act * (1.0 - sigmoid_gate))
        ).astype(BF16)
        dup = (grad_prod * silu_gate).astype(BF16)
        dgate_ref[where, :] = dgate
        dup_ref[where, :] = dup
        grad_in = nt(dgate, gate_mat[...]) + nt(dup, up_mat[...])
        return grad_in, jnp.sum(both * grad_hidden, axis=1, keepdims=True)

    def some_experts(i):
        def got(k):
            row_copy(k).wait_recv()
            spare_copy(k).wait_recv()

        loop(jnp.maximum(8 * i, 1), 8 * i + 8, got)
        x = row_in[pl.ds(8 * i, 8)].reshape(256, width)
        gate = to_column(spare_in[pl.ds(8 * i, 8), :, 1024:].reshape(8, 128), 32)
        grad_in, sel = expert_rows(x, gate, pl.ds(256 * i, 256))
        back_send[pl.ds(8 * i, 8)] = grad_in.astype(BF16).reshape(8, 32, width)
        sel_ref[pl.ds(8 * i, 8), :] = to_table(sel, 32)
        loop(jnp.maximum(8 * i, 1), 8 * i + 8, lambda k: back_copy(k).start())

    loop(0, 4, some_experts)
    spare = spare_in[...].reshape(FSDP, 1152)
    spare_gate = spare[:, 1056:1057]
    spare_rows = spare[:, :1024].astype(BF16)
    grad_in, sel = expert_rows(spare_rows, spare_gate, pl.ds(main, FSDP))
    sel_all = jnp.where(lanes((FSDP, 128)) == 32, sel, sel_ref[...])
    for k in range(FSDP):
        back_spare_send[k, :, :1024] = grad_in[k : k + 1]
        back_spare_send[k, :, 1024:] = sel_all[k : k + 1]
    loop(1, FSDP, lambda k: bspare_copy(k).start())
    back_in[0] = back_send[0]
    back_spare_in[0] = back_spare_send[0]

    def outputs(i):
        out = nt(hidden_ref[pl.ds(256 * i, 256), :], down_mat[...])
        out_main_ref[pl.ds(8 * i, 8)] = out.astype(BF16).reshape(8, 32, width)

    loop(0, 4, outputs)
    out = nt(hidden_ref[pl.ds(main, FSDP), :], down_mat[...])
    for k in range(FSDP):
        out_spare_ref[k] = out[k : k + 1]

    def weight_grads(i):
        at = pl.ds(pl.multiple_of(256 * i, 256), 256)
        x = row_in[:, :, at].reshape(main, 256)
        x_spare = spare_in[:, :, at].reshape(FSDP, 256).astype(BF16)
        c = cot_main_ref[:, :, at].reshape(main, 256)
        c_spare = cot_spare_ref[:, :, at].reshape(FSDP, 256).astype(BF16)
        for m, (a, a_spare, b) in enumerate(
            ((x, x_spare, dgate_ref), (x, x_spare, dup_ref), (c, c_spare, hidden_ref))
        ):
            part = tn(a, b[pl.ds(0, main), :]) + tn(a_spare, b[pl.ds(main, FSDP), :])
            part = part.astype(BF16)
            for j in range(TP):
                for h in range(2):
                    grads_ref[
                        lax.rem(j + 2 * lax.rem(half + h, 2), TP),
                        pl.ds(8 * i + 4 * h, 4),
                        32 * m : 32 * m + 32,
                        :,
                    ] = part[128 * h : 128 * h + 128, 128 * j : 128 * j + 128].reshape(4, 32, 128)

    loop(0, 4, weight_grads)

    def back_got(k):
        back_copy(k).wait_recv()
        bspare_copy(k).wait_recv()

    loop(1, FSDP, back_got)
    hot = hot_main_ref[...].reshape(main, rows)
    hot_spare = hot_spare_ref[...]
    back_spare = back_spare_in[...].reshape(FSDP, 1152)
    grad_rows = tn(hot, back_in[...].reshape(main, width)) + tn(
        hot_spare.astype(BF16), back_spare[:, :1024].astype(BF16)
    )
    sel = back_spare[:, 1024:]
    by_slot = jnp.sum(
        (hot.astype(F32) * to_column(sel, 32)).reshape(FSDP, 32, rows), axis=1
    ) + hot_spare * sel[:, 32:33]
    gg_ref[...] = jnp.zeros_like(gg_ref)
    for k in range(FSDP):
        gg_ref[pl.ds(peer(me, k), 1), :] = by_slot[k : k + 1]
    grad_gates = jnp.transpose(gg_ref[...])
    gates = gates_ref[...]
    grad_chosen = gates * (grad_gates - jnp.sum(gates * grad_gates, axis=1, keepdims=True))
    grad_logits = grad_chosen.astype(BF16)
    tail = tail_ref[...].reshape(width, 128)
    gain_two = jnp.transpose(tail.astype(F32))[EXPERTS + 1 : EXPERTS + 2]
    router_part_ref[...] = tn(normed_two_ref[...], grad_logits)
    dy = grad_rows + nt(grad_logits, tail)
    middle = middle_ref[...]
    inverse = lax.rsqrt(jnp.mean(middle * middle, axis=-1, keepdims=True) + EPSILON)
    scaled = dy * gain_two
    second_ref[...] = jnp.sum(dy * middle * inverse, axis=0, keepdims=True)
    grad_middle_ref[...] = (
        cot_ref[...].astype(F32)
        + inverse * scaled
        - middle
        * inverse
        * inverse
        * inverse
        * jnp.mean(scaled * middle, axis=-1, keepdims=True)
    )

    def gone(k):
        row_copy(k).wait_send()
        spare_copy(k).wait_send()
        back_copy(k).wait_send()
        bspare_copy(k).wait_send()

    loop(1, FSDP, gone)


def experts(normed_two, gates, slot, weights, cot_main, cot_spare, middle, cot, tail):
    rows, width = normed_two.shape
    hidden = 128 * TP
    slots = FSDP * SPARE
    vmem = pl.BlockSpec(memory_space=pltpu.VMEM)
    out = (
        shape((FSDP, 32, width), BF16),
        shape((FSDP, 1, width), F32),
        shape(weights.shape, BF16),
        shape((rows, width), F32),
        shape((width, 128), F32),
        shape((1, width), F32),
        shape((FSDP, 32, rows), BF16),
        shape((FSDP, rows), F32),
    )
    return pl.pallas_call(
        expert_kernel,
        out_shape=out,
        in_specs=[vmem] * 9,
        out_specs=[vmem] * len(out),
        scratch_shapes=[
            *[pltpu.VMEM((width, hidden), BF16)] * 3,
            pltpu.VMEM((EXPERTS, rows), F32),
            *[pltpu.VMEM((FSDP, 32, width), BF16), pltpu.VMEM((FSDP, 1, width + 128), F32)] * 4,
            *[pltpu.VMEM((slots, hidden), BF16)] * 3,
            pltpu.VMEM((slots, hidden), F32),
            pltpu.VMEM((FSDP, 128), F32),
            pltpu.VMEM((128, 128), F32),
            *[dma(FSDP)] * 8,
        ],
        compiler_params=pltpu.CompilerParams(
            collective_id=2, has_side_effects=True, vmem_limit_bytes=56 * 2**20
        ),
        name="experts",
    )(normed_two, gates, slot, weights, cot_main, cot_spare, middle, cot, tail)


def backward_kernel(
    grad_middle_ref, packed_all_ref, heads_ref, normed_all_ref, attended_ref, cos_ref, sin_ref,
    seg_ref, out_main_ref, out_spare_ref, grads_ref, middle_ref, hot_main_ref, hot_spare_ref,
    inputs_ref, router_part_ref, second_ref,
    output_ref, grad_inputs_ref, sums_ref, weight_grads_ref,
    branch_own, branch_all, out_in, out_spare_in, pair_in, across_send, across_in, dw_send, dw_in,
    normed_send, normed_in, sums_send, sums_in, small_own, small_in,
    branch_s, branch_r, out_s, out_r, spare_s, spare_r, pair_s, pair_r, across_s, across_r,
    dw_s, dw_r, normed_s, normed_r, sums_s, sums_r, small_s, small_r,
):
    me, tp = lax.axis_index("fsdp"), lax.axis_index("tp")
    rows, width = inputs_ref.shape
    total = seg_ref.shape[1]
    core = lax.rem(tp, 2)
    sibling = tp + 1 - 2 * core
    across = lax.rem(tp + 2, TP)
    greet(me, tp)

    def branch_copy(k):
        block, where = ((tp, across), (tp, sibling), (across, sibling))[k]
        src = branch_own if k < 2 else branch_all.at[block]
        return to_tp(src, branch_all.at[block], branch_s.at[k], branch_r.at[k], where)

    def out_copy(k):
        return to_side(
            out_main_ref.at[k], out_in.at[k], out_s.at[k], out_r.at[k], giver(me, k), side(tp, k)
        )

    def spare_copy(k):
        return to_side(
            out_spare_ref.at[k],
            out_spare_in.at[k],
            spare_s.at[k],
            spare_r.at[k],
            giver(me, k),
            side(tp, k),
        )

    def pair_copy(x):
        return to_tp(
            grads_ref.at[2 * x + 1 - core], pair_in.at[x], pair_s.at[x], pair_r.at[x], sibling
        )

    across_copy = to_tp(across_send, across_in, across_s.at[0], across_r.at[0], across)

    def dw_copy(k):
        p = peer(me, k)
        return to_side(dw_send.at[p], dw_in.at[me], dw_s.at[k], dw_r.at[k], p, side(tp, k))

    def normed_copy(x):
        return to_tp(
            normed_send.at[2 * x + 1 - core],
            normed_in.at[x],
            normed_s.at[x],
            normed_r.at[x],
            sibling,
        )

    normed_across = to_tp(
        normed_in.at[2], normed_in.at[3], normed_s.at[2], normed_r.at[2], across
    )

    def sums_copy(k):
        p = peer(me, k)
        return to_fsdp(sums_send.at[p], sums_in.at[k], sums_s.at[k], sums_r.at[k], p)

    def small_copy(k):
        return to_tp(small_own, small_in.at[k], small_s.at[k], small_r.at[k], lax.rem(tp + k, TP))

    grad_middle = grad_middle_ref[...]
    branch_own[...] = grad_middle.astype(BF16)
    branch_copy(0).start()
    branch_copy(1).start()
    for x in range(2):
        pair_copy(x).start()

    def out_go(k):
        out_copy(k).start()
        spare_copy(k).start()

    loop(1, FSDP, out_go)
    branch_all[tp] = branch_own[...]
    branch_copy(0).wait_recv()
    branch_copy(2).start()
    out_in[0] = out_main_ref[0]
    out_spare_in[0] = out_spare_ref[0]

    for x in range(2):
        pair_copy(x).wait_recv()
    near = tp // 2
    far = 1 - near
    across_send[...] = (
        grads_ref[2 * far + core].astype(F32) + pair_in[far].astype(F32)
    ).astype(BF16)
    across_copy.start()

    seg_row = jnp.broadcast_to(seg_ref[...].astype(F32), (128, total))
    seg_col = jnp.transpose(seg_row)[:, :1]
    allowed = (
        (seg_col == seg_row[:1]) & (rows_of((total, total)) >= lanes((total, total)))
    ).astype(F32)

    branch_copy(1).wait_recv()
    branch_copy(2).wait_recv()
    branch = branch_all[...].reshape(total, width)
    out_part = tn(branch, attended_ref[...])
    grad_attended = nn(branch, packed_all_ref[:, :, 512:768].reshape(width, 256)).astype(BF16)
    scale = HEAD_SIZE ** (-0.5)
    dq, dk, dv = [], [], []
    for g in range(2):
        key = heads_ref[:, 256 + 64 * g : 320 + 64 * g]
        value = heads_ref[:, 384 + 64 * g : 448 + 64 * g]
        dk_sum, dv_sum = None, None
        for h in (2 * g, 2 * g + 1):
            q = heads_ref[:, 64 * h : 64 * h + 64]
            da = grad_attended[:, 64 * h : 64 * h + 64]
            scores = jnp.where(allowed > 0, nt(q, key) * scale, MASKED)
            top = jnp.max(scores, axis=1, keepdims=True)
            grown = jnp.exp(scores - top)
            whole = grown * (1.0 / jnp.sum(grown, axis=1, keepdims=True))
            grad_shares = nt(da, value)
            inner = jnp.sum(whole * grad_shares, axis=1, keepdims=True)
            grad_scores = (whole * (grad_shares - inner)).astype(BF16)
            dq.append(nn(grad_scores, key) * scale)
            dk_one = tn(grad_scores, q) * scale
            dv_one = tn(whole.astype(BF16), da)
            dk_sum = dk_one if dk_sum is None else dk_sum + dk_one
            dv_sum = dv_one if dv_sum is None else dv_sum + dv_one
        dk.append(dk_sum)
        dv.append(dv_sum)
    turned = jnp.concatenate(dq + dk, axis=1)
    turn = turned * wide_table(cos_ref[...], 384) - half_swap(turned) * wide_table(
        sin_ref[...], 384
    )
    grad_lin = jnp.concatenate([turn] + dv, axis=1).astype(BF16)
    grad_normed = nt(grad_lin, packed_all_ref[:, :, 0:512].reshape(width, 512))
    normed_send[...] = grad_normed.astype(BF16).reshape(TP, rows, width)
    for x in range(2):
        normed_copy(x).start()
    gain_one = jnp.transpose(packed_all_ref[:, :, 768:896].reshape(width, 128).astype(F32))[
        EXPERTS : EXPERTS + 1
    ]
    first = jnp.sum(grad_normed * normed_all_ref[...].astype(F32), axis=0, keepdims=True) / gain_one

    qkv_part = tn(normed_all_ref[...], grad_lin)
    sums_send[:, :, 0:512] = qkv_part.astype(BF16).reshape(FSDP, 32, 512)
    sums_send[:, :, 512:768] = out_part.astype(BF16).reshape(FSDP, 32, 256)
    at = rows_of((128, width))
    gains = jnp.where(at == EXPERTS, first, 0.0) + jnp.where(at == EXPERTS + 1, second_ref[...], 0.0)
    small = router_part_ref[...] + jnp.transpose(gains)
    sums_send[:, :, 768:896] = small.astype(BF16).reshape(FSDP, 32, 128)
    loop(1, FSDP, lambda k: sums_copy(k).start())
    sums_in[0] = sums_send[me]

    for x in range(2):
        normed_copy(x).wait_recv()
    normed_in[2] = (
        normed_send[across].astype(F32) + normed_in[far].astype(F32)
    ).astype(BF16)
    normed_across.start()

    across_copy.wait_recv()
    dw_send[...] = (
        grads_ref[tp].astype(F32) + pair_in[near].astype(F32) + across_in[...].astype(F32)
    ).astype(BF16)
    loop(1, FSDP, lambda k: dw_copy(k).start())
    dw_in[me] = dw_send[me]

    normed_across.wait_recv()
    dy = normed_send[tp].astype(F32) + normed_in[near].astype(F32) + normed_in[3].astype(F32)
    wide = inputs_ref[...].astype(F32)
    inverse = lax.rsqrt(jnp.mean(wide * wide, axis=-1, keepdims=True) + EPSILON)
    scaled = dy * gain_one
    grad_inputs_ref[...] = (
        grad_middle
        + inverse * scaled
        - wide
        * inverse
        * inverse
        * inverse
        * jnp.mean(scaled * wide, axis=-1, keepdims=True)
    )

    def out_got(k):
        out_copy(k).wait_recv()
        spare_copy(k).wait_recv()

    loop(1, FSDP, out_got)
    hot = hot_main_ref[...].reshape(FSDP * 32, rows)
    output_ref[...] = (
        middle_ref[...]
        + tn(hot, out_in[...].reshape(FSDP * 32, width))
        + tn(hot_spare_ref[...].astype(BF16), out_spare_in[...].reshape(FSDP, width).astype(BF16))
    ).astype(BF16)

    loop(1, FSDP, lambda k: sums_copy(k).wait_recv())
    sums = jnp.sum(sums_in[...].astype(F32), axis=0)
    sums_ref[:, :768] = sums[:, :768]
    small_own[...] = sums[:, 768:]
    for k in (2, 1, 3):
        small_copy(k).start()
    loop(1, FSDP, lambda k: dw_copy(k).wait_recv())
    weight_grads_ref[...] = dw_in[...].astype(F32)
    for k in range(1, TP):
        small_copy(k).wait_recv()
    sums_ref[:, 768:] = small_own[...] + small_in[1] + small_in[2] + small_in[3]

    def gone(k):
        out_copy(k).wait_send()
        spare_copy(k).wait_send()
        sums_copy(k).wait_send()
        dw_copy(k).wait_send()

    loop(1, FSDP, gone)
    for k in range(3):
        branch_copy(k).wait_send()
        small_copy(k + 1).wait_send()
    for x in range(2):
        normed_copy(x).wait_send()
        pair_copy(x).wait_send()
    normed_across.wait_send()
    across_copy.wait_send()


def backward(*operands):
    grads, inputs, packed_all = operands[10], operands[14], operands[1]
    rows, width = inputs.shape
    vmem = pl.BlockSpec(memory_space=pltpu.VMEM)
    out = (
        shape((rows, width), BF16),
        shape((rows, width), F32),
        shape(packed_all.shape[1:], F32),
        shape(grads.shape[1:], F32),
    )
    return pl.pallas_call(
        backward_kernel,
        out_shape=out,
        in_specs=[vmem] * len(operands),
        out_specs=[vmem] * len(out),
        scratch_shapes=[
            pltpu.VMEM((rows, width), BF16),
            pltpu.VMEM((TP, rows, width), BF16),
            pltpu.VMEM((FSDP, 32, width), BF16),
            pltpu.VMEM((FSDP, 1, width), F32),
            pltpu.VMEM((2, *grads.shape[1:]), BF16),
            *[pltpu.VMEM(grads.shape[1:], BF16)] * 4,
            *[pltpu.VMEM((TP, rows, width), BF16)] * 2,
            *[pltpu.VMEM(packed_all.shape, BF16)] * 2,
            pltpu.VMEM((32, 128), F32),
            pltpu.VMEM((TP, 32, 128), F32),
            *[dma(TP)] * 2,
            *[dma(FSDP)] * 4,
            *[dma(2)] * 2,
            *[dma(1)] * 2,
            *[dma(FSDP)] * 2,
            *[dma(TP)] * 2,
            *[dma(FSDP)] * 2,
            *[dma(TP)] * 2,
        ],
        compiler_params=pltpu.CompilerParams(
            collective_id=3, has_side_effects=True, vmem_limit_bytes=56 * 2**20
        ),
        name="attention_backward",
    )(*operands)


def per_device(
    inputs,
    segments,
    routes,
    query_weight,
    key_projection_weight,
    value_projection_weight,
    out_weight,
    router_weight,
    first_gain,
    second_gain,
    gate_weight,
    up_weight,
    down_weight,
    cotangent,
):
    row_count = inputs.shape[0]
    my_offset = lax.axis_index("tp") * row_count
    width_shard = query_weight.shape[0]
    q_cols, k_cols, o_cols = query_weight.shape[1], key_projection_weight.shape[1], out_weight.shape[0]

    wide = q_cols + 2 * k_cols + o_cols
    packed = jnp.concatenate(
        [
            query_weight,
            key_projection_weight,
            value_projection_weight,
            out_weight.T,
            router_weight,
            first_gain[:, None],
            second_gain[:, None],
            jnp.zeros((width_shard, 128 - EXPERTS - 2), BF16),
        ],
        axis=1,
    )
    blocks = jnp.concatenate(
        [gate_weight, up_weight, jnp.transpose(down_weight, (0, 2, 1))], axis=1
    )
    my_routes = lax.dynamic_slice_in_dim(routes, my_offset, row_count, 0)
    (
        middle, normed_two, gates, slot, weights, cot_main, cot_spare,
        packed_all, heads, normed_all, attended, cosine, sine,
    ) = forward(packed, inputs, segments, my_routes, blocks, cotangent)
    tail = packed_all[:, :, wide:]
    (
        out_main, out_spare, grads, grad_middle, router_part, second_part, hot_main, hot_spare
    ) = experts(normed_two, gates, slot, weights, cot_main, cot_spare, middle, cotangent, tail)
    output, grad_inputs, sums, weight_grads = backward(
        grad_middle, packed_all, heads, normed_all, attended, cosine, sine, segments,
        out_main, out_spare, grads, middle, hot_main, hot_spare, inputs, router_part, second_part,
    )
    return (
        output,
        grad_inputs,
        sums[:, :q_cols],
        sums[:, q_cols : q_cols + k_cols],
        sums[:, q_cols + k_cols : q_cols + 2 * k_cols],
        sums[:, q_cols + 2 * k_cols : wide].T,
        sums[:, wide : wide + EXPERTS],
        sums[:, wide + EXPERTS],
        sums[:, wide + EXPERTS + 1],
        weight_grads[:, :width_shard],
        weight_grads[:, width_shard : 2 * width_shard],
        jnp.transpose(weight_grads[:, 2 * width_shard :], (0, 2, 1)),
    )


def solution(mesh):
    return jax.shard_map(
        per_device,
        mesh=mesh,
        in_specs=(
            P(("fsdp", "tp"), None),
            P("fsdp", None),
            P("fsdp", None),
            P("fsdp", "tp"),
            P("fsdp", "tp"),
            P("fsdp", "tp"),
            P("tp", "fsdp"),
            P("fsdp", None),
            P("fsdp"),
            P("fsdp"),
            P(None, "fsdp", "tp"),
            P(None, "fsdp", "tp"),
            P(None, "tp", "fsdp"),
            P(("fsdp", "tp"), None),
        ),
        out_specs=(
            P(("fsdp", "tp"), None),
            P(("fsdp", "tp"), None),
            P("fsdp", "tp"),
            P("fsdp", "tp"),
            P("fsdp", "tp"),
            P("tp", "fsdp"),
            P("fsdp", None),
            P("fsdp"),
            P("fsdp"),
            P(None, "fsdp", "tp"),
            P(None, "fsdp", "tp"),
            P(None, "tp", "fsdp"),
        ),
        check_vma=False,
    )
```

```python
import math

import jax
import jax.numpy as jnp
from jax import lax
from jax.experimental import pallas as pl
from jax.experimental.pallas import tpu as pltpu
from jax.sharding import PartitionSpec as P

HEAD_SIZE = 64
EXPERTS = 32
TOP = 8


EPSILON = 1e-06
ROPE_BASE = 10000.0
MASKED = -1e30


MESH = pl.DeviceIdType.MESH
FSDP, TP, SPARE = 32, 4, 33
F32, BF16 = jnp.float32, jnp.bfloat16


def peer(me, k):
    z, x, y = me // 8, (me // 4) % 2, me % 4
    return ((z + k // 8) % 4 * 2 + (x + (k // 4) % 2) % 2) * 4 + (y + k % 4) % 4


def giver(me, k):
    z, x, y = me // 8, (me // 4) % 2, me % 4
    return ((z + 4 - k // 8) % 4 * 2 + (x + (k // 4) % 2) % 2) * 4 + (y + 4 - k % 4) % 4


def side(tp, k):
    return lax.rem(tp + 2 * ((k // 4) % 2), TP)


def loop(low, high, step):
    def body(k, carry):
        step(k)
        return carry

    lax.fori_loop(low, high, body, 0)


def greet(me, tp):
    barrier = pltpu.get_barrier_semaphore()

    def signal(k):
        for q in (tp, lax.rem(tp + 2, TP)):
            pl.semaphore_signal(
                barrier,
                inc=1,
                device_id={"fsdp": peer(me, k), "tp": q},
                device_id_type=MESH,
            )

    loop(1, FSDP, signal)
    for k in range(1, TP):
        pl.semaphore_signal(
            barrier, inc=1, device_id={"tp": lax.rem(tp + k, TP)}, device_id_type=MESH
        )
    pl.semaphore_wait(barrier, 2 * (FSDP - 1) + TP - 1)


def to_fsdp(src, dst, send, recv, where):
    return pltpu.make_async_remote_copy(
        src_ref=src,
        dst_ref=dst,
        send_sem=send,
        recv_sem=recv,
        device_id={"fsdp": where},
        device_id_type=MESH,
    )


def to_tp(src, dst, send, recv, where):
    return pltpu.make_async_remote_copy(
        src_ref=src,
        dst_ref=dst,
        send_sem=send,
        recv_sem=recv,
        device_id={"tp": where},
        device_id_type=MESH,
    )


def to_side(src, dst, send, recv, where, q):
    return pltpu.make_async_remote_copy(
        src_ref=src,
        dst_ref=dst,
        send_sem=send,
        recv_sem=recv,
        device_id={"fsdp": where, "tp": q},
        device_id_type=MESH,
    )


def nn(a, b):
    return jnp.dot(a, b, preferred_element_type=F32)


def nt(a, b):
    return lax.dot_general(a, b, (((1,), (1,)), ((), ())), preferred_element_type=F32)


def tn(a, b):
    return lax.dot_general(a, b, (((0,), (0,)), ((), ())), preferred_element_type=F32)


def lanes(shape):
    return lax.broadcasted_iota(jnp.int32, shape, len(shape) - 1)


def rows_of(shape):
    return lax.broadcasted_iota(jnp.int32, shape, 0)


def half_swap(v):
    width = v.shape[-1]
    front = lanes(v.shape) % HEAD_SIZE < HEAD_SIZE // 2
    ahead = pltpu.roll(v, width - HEAD_SIZE // 2, 1)
    behind = pltpu.roll(v, HEAD_SIZE // 2, 1)
    return jnp.where(front, -ahead, behind)


def wide_table(table, width):
    return jnp.concatenate([table] * (width // 128), axis=1)


def pick(slot_ref, experts, count):
    parts = []
    for e in experts:
        row = slot_ref[pl.ds(e, 1), :]
        parts.append(jnp.broadcast_to(row, (count, row.shape[1])))
    both = jnp.concatenate(parts, axis=0)
    want = (rows_of(both.shape) % count).astype(F32)
    return (both == want).astype(BF16)


def forward_part(
    packed_ref, inputs_ref, seg_ref, routes_ref, blocks_ref, cot_ref,
    middle_ref, normed_two_ref, gates_ref, slot_ref, weights_ref, cot_main_ref, cot_spare_ref,
    packed_all_ref, heads_ref, normed_all_ref, attended_ref, cos_ref, sin_ref,
    inputs_all, blocks_in, send_main, send_spare, branch_out, branch_in,
    packed_send, packed_recv, blocks_send, blocks_recv, main_send, main_recv, spare_send, spare_recv,
    inputs_send, inputs_recv, weights_send, weights_recv, branch_send, branch_recv, own_sem,
):
    me, tp = lax.axis_index("fsdp"), lax.axis_index("tp")
    rows, width = inputs_ref.shape
    total = seg_ref.shape[1]
    greet(me, tp)

    def packed_copy(k):
        return to_fsdp(
            packed_ref, packed_all_ref.at[me], packed_send.at[k], packed_recv.at[k], peer(me, k)
        )

    core = lax.rem(tp, 2)
    sibling = tp + 1 - 2 * core
    across = lax.rem(tp + 2, TP)

    def inputs_copy(k):
        block, where = ((tp, across), (tp, sibling), (across, sibling))[k]
        src = inputs_ref if k < 2 else inputs_all.at[block]
        return to_tp(src, inputs_all.at[block], inputs_send.at[k], inputs_recv.at[k], where)

    def blocks_copy(k):
        p = peer(me, k)
        return to_side(
            blocks_ref.at[p], blocks_in.at[me], blocks_send.at[k], blocks_recv.at[k], p, side(tp, k)
        )

    def main_copy(k):
        return to_side(
            send_main.at[k],
            cot_main_ref.at[k],
            main_send.at[k],
            main_recv.at[k],
            peer(me, k),
            side(tp, k),
        )

    def spare_copy(k):
        return to_side(
            send_spare.at[k],
            cot_spare_ref.at[k],
            spare_send.at[k],
            spare_recv.at[k],
            peer(me, k),
            side(tp, k),
        )

    def branch_copy(x):
        return to_tp(
            branch_out.at[2 * x + 1 - core],
            branch_in.at[x],
            branch_send.at[x],
            branch_recv.at[x],
            sibling,
        )

    branch_across = to_tp(
        branch_in.at[2], branch_in.at[3], branch_send.at[2], branch_recv.at[2], across
    )

    inputs_copy(0).start()
    inputs_copy(1).start()
    loop(1, FSDP, lambda k: packed_copy(k).start())
    loop(1, FSDP, lambda k: blocks_copy(k).start())
    keep = [
        pltpu.make_async_copy(packed_ref, packed_all_ref.at[me], own_sem.at[0]),
        pltpu.make_async_copy(inputs_ref, inputs_all.at[tp], own_sem.at[1]),
        pltpu.make_async_copy(blocks_ref.at[me], blocks_in.at[me], own_sem.at[2]),
    ]
    for copy in keep:
        copy.start()

    at = lanes((rows, 128))
    member = jnp.zeros((rows, 128), F32)
    for k in range(TOP):
        member = member + (routes_ref[:, k : k + 1] == at).astype(F32)
    earlier = (rows_of((rows, rows)) > lanes((rows, rows))).astype(BF16)
    slot = nn(earlier, member.astype(BF16))
    slot = jnp.where(member > 0, slot, -1.0)
    slot_ref[...] = jnp.transpose(slot)[:EXPERTS]

    def some_rows(i):
        hot = pick(slot_ref, [peer(me, 4 * i + j) for j in range(4)], 40)
        out = nn(hot, cot_ref[...])
        for j in range(4):
            send_main[4 * i + j] = out[40 * j : 40 * j + 32].astype(BF16)
            send_spare[4 * i + j] = out[40 * j + 32 : 40 * j + 33]

        def go(k):
            main_copy(k).start()
            spare_copy(k).start()

        loop(jnp.maximum(4 * i, 1), 4 * i + 4, go)

    loop(0, FSDP // 4, some_rows)
    cot_main_ref[0] = send_main[0]
    cot_spare_ref[0] = send_spare[0]

    seg_row = jnp.broadcast_to(seg_ref[...].astype(F32), (128, total))
    seg_col = jnp.transpose(seg_row)[:, :1]
    same = (seg_col == seg_row[:1]) & (rows_of((total, total)) >= lanes((total, total)))
    allowed = same.astype(F32)
    place = jnp.sum(allowed, axis=1, keepdims=True) - 1.0
    halves = (lanes((1, 128)) % (HEAD_SIZE // 2)).astype(F32)
    rate = jnp.exp(halves * (-2.0 * math.log(ROPE_BASE) / HEAD_SIZE))
    angle = place * rate
    cos_ref[...] = jnp.cos(angle)
    sin_ref[...] = jnp.sin(angle)

    inputs_copy(0).wait_recv()
    inputs_copy(2).start()
    inputs_copy(1).wait_recv()
    inputs_copy(2).wait_recv()
    keep[1].wait()
    wide = inputs_all[...].reshape(total, width).astype(F32)
    inverse = lax.rsqrt(jnp.mean(wide * wide, axis=-1, keepdims=True) + EPSILON)

    loop(1, FSDP, lambda k: packed_copy(k).wait_recv())
    keep[0].wait()
    tail = jnp.transpose(packed_all_ref[:, :, 768:896].reshape(width, 128).astype(F32))
    normed = (wide * inverse * tail[EXPERTS : EXPERTS + 1]).astype(BF16)
    normed_all_ref[...] = normed
    lin = nn(normed, packed_all_ref[:, :, 0:512].reshape(width, 512))
    turn = lin[:, :384]
    turned = turn * wide_table(cos_ref[...], 384) + half_swap(turn) * wide_table(sin_ref[...], 384)
    heads_ref[:, :384] = turned.astype(BF16)
    heads_ref[:, 384:] = lin[:, 384:].astype(BF16)
    outs = []
    for h in range(4):
        g = h // 2
        q = heads_ref[:, 64 * h : 64 * h + 64]
        key = heads_ref[:, 256 + 64 * g : 320 + 64 * g]
        value = heads_ref[:, 384 + 64 * g : 448 + 64 * g]
        scores = jnp.where(allowed > 0, nt(q, key) * HEAD_SIZE ** (-0.5), MASKED)
        top = jnp.max(scores, axis=1, keepdims=True)
        grown = jnp.exp(scores - top)
        shares = (grown * (1.0 / jnp.sum(grown, axis=1, keepdims=True))).astype(BF16)
        outs.append(nn(shares, value))
    attended = jnp.concatenate(outs, axis=1).astype(BF16)
    attended_ref[...] = attended
    branch = nt(attended, packed_all_ref[:, :, 512:768].reshape(width, 256))
    branch_out[...] = branch.astype(BF16).reshape(TP, rows, width)
    for x in range(2):
        branch_copy(x).start()
    for x in range(2):
        branch_copy(x).wait_recv()
    near = tp // 2
    far = 1 - near
    branch_in[2] = (
        branch_out[across].astype(F32) + branch_in[far].astype(F32)
    ).astype(BF16)
    branch_across.start()

    loop(1, FSDP, lambda k: blocks_copy(k).wait_recv())
    keep[2].wait()
    first = to_tp(blocks_in, weights_ref.at[tp], weights_send.at[0], weights_recv.at[0], across)
    second = to_tp(blocks_in, weights_ref.at[tp], weights_send.at[1], weights_recv.at[1], sibling)
    third = to_tp(
        weights_ref.at[across], weights_ref.at[across], weights_send.at[2], weights_recv.at[2], sibling
    )
    first.start()
    second.start()
    mine = pltpu.make_async_copy(blocks_in, weights_ref.at[tp], own_sem.at[3])
    mine.start()

    for x in range(2):
        branch_copy(x).wait_send()
    branch_across.wait_recv()
    middle = inputs_ref[...].astype(F32) + branch_out[tp].astype(F32)
    middle = middle + branch_in[near].astype(F32) + branch_in[3].astype(F32)
    middle_ref[...] = middle
    inverse_two = lax.rsqrt(jnp.mean(middle * middle, axis=-1, keepdims=True) + EPSILON)
    normed_two = (middle * inverse_two * tail[EXPERTS + 1 : EXPERTS + 2]).astype(BF16)
    normed_two_ref[...] = normed_two
    logits = nn(normed_two, packed_all_ref[:, :, 768:896].reshape(width, 128))
    logits = jnp.where(member > 0, logits, MASKED)
    grown = jnp.exp(logits - jnp.max(logits, axis=1, keepdims=True)) * member
    gates_ref[...] = grown / jnp.sum(grown, axis=1, keepdims=True)

    def pass_weights():
        first.wait_recv()
        third.start()

    def weights_ready():
        second.wait_recv()
        third.wait_recv()
        mine.wait()
        for copy in (first, second, third):
            copy.wait_send()

    def cot_ready():
        def got(k):
            main_copy(k).wait_recv()
            spare_copy(k).wait_recv()
            main_copy(k).wait_send()

        loop(1, FSDP, got)

    def sent():
        def gone(k):
            packed_copy(k).wait_send()
            blocks_copy(k).wait_send()
            spare_copy(k).wait_send()

        loop(1, FSDP, gone)
        for k in range(3):
            inputs_copy(k).wait_send()
        branch_across.wait_send()

    return pass_weights, weights_ready, cot_ready, sent


def shape(dims, kind):
    return jax.ShapeDtypeStruct(dims, kind)


def dma(count):
    return pltpu.SemaphoreType.DMA((count,))


def to_column(table, count):
    n = table.shape[0]
    spread = jnp.broadcast_to(table[:, None, :], (n, count, 128)).reshape(n * count, 128)
    mine = lanes(spread.shape) == rows_of(spread.shape) % count
    return jnp.sum(jnp.where(mine, spread, 0.0), axis=1, keepdims=True)


def to_table(column, count):
    n = column.shape[0] // count
    spread = jnp.broadcast_to(column, (n * count, 128))
    mine = lanes(spread.shape) == rows_of(spread.shape) % count
    return jnp.sum(jnp.where(mine, spread, 0.0).reshape(n, count, 128), axis=1)


def expert_part(
    pass_weights, weights_ready, cot_ready, start_pairs,
    normed_two_ref, gates_ref, slot_ref, weights_ref, cot_main_ref, cot_spare_ref,
    middle_ref, cot_ref, packed_all_ref,
    out_main_ref, out_spare_ref, grads_ref, grad_middle_ref, router_part_ref, second_ref,
    hot_main_ref, hot_spare_ref,
    gate_mat, up_mat, down_mat, gate_t, row_send, spare_send, row_in, spare_in,
    back_send, back_spare_send, back_in, back_spare_in,
    hidden_ref, dgate_ref, dup_ref, ghidden_ref, sel_ref, gg_ref,
    out_in, out_spare_in,
    row_s, row_r, spare_s, spare_r, back_s, back_r, bspare_s, bspare_r,
    out_s, out_r, out_spare_s, out_spare_r,
):
    me, tp = lax.axis_index("fsdp"), lax.axis_index("tp")
    half = (me // 4) % 2
    rows, width = normed_two_ref.shape
    main = FSDP * 32

    def row_copy(k):
        return to_side(
            row_send.at[k], row_in.at[k], row_s.at[k], row_r.at[k], peer(me, k), side(tp, k)
        )

    def spare_copy(k):
        return to_side(
            spare_send.at[k], spare_in.at[k], spare_s.at[k], spare_r.at[k], peer(me, k), side(tp, k)
        )

    def back_copy(k):
        return to_side(
            back_send.at[k], back_in.at[k], back_s.at[k], back_r.at[k], giver(me, k), side(tp, k)
        )

    def bspare_copy(k):
        return to_side(
            back_spare_send.at[k],
            back_spare_in.at[k],
            bspare_s.at[k],
            bspare_r.at[k],
            giver(me, k),
            side(tp, k),
        )

    def out_copy(k):
        return to_side(
            out_main_ref.at[k], out_in.at[k], out_s.at[k], out_r.at[k], giver(me, k), side(tp, k)
        )

    def out_spare_copy(k):
        return to_side(
            out_spare_ref.at[k],
            out_spare_in.at[k],
            out_spare_s.at[k],
            out_spare_r.at[k],
            giver(me, k),
            side(tp, k),
        )

    gates_low = gates_ref[...].astype(BF16).astype(F32)
    gate_t[...] = jnp.transpose(gates_low)[:EXPERTS]

    def some_rows(i):
        experts = [peer(me, 4 * i + j) for j in range(4)]
        hot = pick(slot_ref, experts, 40)
        out = nn(hot, normed_two_ref[...])
        for j in range(4):
            k = 4 * i + j
            mine = hot[40 * j : 40 * j + 40].astype(F32)
            column = jnp.sum(mine * gate_t[pl.ds(experts[j], 1), :], axis=1, keepdims=True)
            row_send[k] = out[40 * j : 40 * j + 32].astype(BF16)
            spare_send[k, :, :1024] = out[40 * j + 32 : 40 * j + 33]
            spare_send[k, :, 1024:] = to_table(column, 40)
            hot_main_ref[k] = hot[40 * j : 40 * j + 32]
            hot_spare_ref[pl.ds(k, 1), :] = mine[32:33]

        def go(k):
            row_copy(k).start()
            spare_copy(k).start()

        loop(jnp.maximum(4 * i, 1), 4 * i + 4, go)

    loop(0, FSDP // 4, some_rows)
    row_in[0] = row_send[0]
    spare_in[0] = spare_send[0]

    pass_weights()
    weights_ready()

    def side_by_side(i):
        at = pl.ds(pl.multiple_of(128 * i, 128), 128)
        swap = 2 * lax.rem(half + i, 2)
        for j in range(TP):
            cols = slice(128 * j, 128 * j + 128)
            block = weights_ref[lax.rem(j + swap, TP), pl.ds(4 * i, 4)]
            gate_mat[at, cols] = block[:, 0:32].reshape(128, 128)
            up_mat[at, cols] = block[:, 32:64].reshape(128, 128)
            down_mat[at, cols] = block[:, 64:96].reshape(128, 128)

    loop(0, 8, side_by_side)

    cot_ready()

    def hidden_grads(i):
        cot_rows = cot_main_ref[pl.ds(8 * i, 8)].reshape(256, width)
        ghidden_ref[pl.ds(256 * i, 256), :] = nn(cot_rows, down_mat[...])

    loop(0, 4, hidden_grads)
    cot_spare = cot_spare_ref[...].reshape(FSDP, width).astype(BF16)
    ghidden_ref[pl.ds(main, FSDP), :] = nn(cot_spare, down_mat[...])

    def expert_rows(x, gate, where):
        gate_act = nn(x, gate_mat[...])
        up_act = nn(x, up_mat[...])
        grad_hidden = ghidden_ref[where, :]
        sigmoid_gate = 1.0 / (1.0 + jnp.exp(-gate_act))
        silu_gate = gate_act * sigmoid_gate
        both = silu_gate * up_act
        hidden_ref[where, :] = (both * gate).astype(BF16)
        grad_prod = grad_hidden * gate
        dgate = (
            grad_prod * up_act * sigmoid_gate * (1.0 + gate_act * (1.0 - sigmoid_gate))
        ).astype(BF16)
        dup = (grad_prod * silu_gate).astype(BF16)
        dgate_ref[where, :] = dgate
        dup_ref[where, :] = dup
        grad_in = nt(dgate, gate_mat[...]) + nt(dup, up_mat[...])
        return grad_in, jnp.sum(both * grad_hidden, axis=1, keepdims=True)

    def some_experts(i):
        def got(k):
            row_copy(k).wait_recv()
            spare_copy(k).wait_recv()

        loop(jnp.maximum(8 * i, 1), 8 * i + 8, got)
        x = row_in[pl.ds(8 * i, 8)].reshape(256, width)
        gate = to_column(spare_in[pl.ds(8 * i, 8), :, 1024:].reshape(8, 128), 32)
        grad_in, sel = expert_rows(x, gate, pl.ds(256 * i, 256))
        back_send[pl.ds(8 * i, 8)] = grad_in.astype(BF16).reshape(8, 32, width)
        sel_ref[pl.ds(8 * i, 8), :] = to_table(sel, 32)
        loop(jnp.maximum(8 * i, 1), 8 * i + 8, lambda k: back_copy(k).start())

    loop(0, 4, some_experts)
    spare = spare_in[...].reshape(FSDP, 1152)
    spare_gate = spare[:, 1056:1057]
    spare_rows = spare[:, :1024].astype(BF16)
    grad_in, sel = expert_rows(spare_rows, spare_gate, pl.ds(main, FSDP))
    sel_all = jnp.where(lanes((FSDP, 128)) == 32, sel, sel_ref[...])
    for k in range(FSDP):
        back_spare_send[k, :, :1024] = grad_in[k : k + 1]
        back_spare_send[k, :, 1024:] = sel_all[k : k + 1]
    loop(1, FSDP, lambda k: bspare_copy(k).start())
    back_in[0] = back_send[0]
    back_spare_in[0] = back_spare_send[0]

    loop(1, FSDP, lambda k: row_copy(k).wait_send())

    def outputs(i):
        out = nt(hidden_ref[pl.ds(256 * i, 256), :], down_mat[...])
        out_main_ref[pl.ds(8 * i, 8)] = out.astype(BF16).reshape(8, 32, width)
        loop(jnp.maximum(8 * i, 1), 8 * i + 8, lambda k: out_copy(k).start())

    loop(0, 4, outputs)
    out = nt(hidden_ref[pl.ds(main, FSDP), :], down_mat[...])
    for k in range(FSDP):
        out_spare_ref[k] = out[k : k + 1]
    loop(1, FSDP, lambda k: out_spare_copy(k).start())
    out_in[0] = out_main_ref[0]
    out_spare_in[0] = out_spare_ref[0]

    def weight_grads(i):
        at = pl.ds(pl.multiple_of(256 * i, 256), 256)
        x = row_in[:, :, at].reshape(main, 256)
        x_spare = spare_in[:, :, at].reshape(FSDP, 256).astype(BF16)
        c = cot_main_ref[:, :, at].reshape(main, 256)
        c_spare = cot_spare_ref[:, :, at].reshape(FSDP, 256).astype(BF16)
        for m, (a, a_spare, b) in enumerate(
            ((x, x_spare, dgate_ref), (x, x_spare, dup_ref), (c, c_spare, hidden_ref))
        ):
            part = tn(a, b[pl.ds(0, main), :]) + tn(a_spare, b[pl.ds(main, FSDP), :])
            part = part.astype(BF16)
            for j in range(TP):
                for h in range(2):
                    grads_ref[
                        lax.rem(j + 2 * lax.rem(half + h, 2), TP),
                        pl.ds(8 * i + 4 * h, 4),
                        32 * m : 32 * m + 32,
                        :,
                    ] = part[128 * h : 128 * h + 128, 128 * j : 128 * j + 128].reshape(4, 32, 128)

    loop(0, 4, weight_grads)

    start_pairs()

    def back_got(k):
        back_copy(k).wait_recv()
        bspare_copy(k).wait_recv()

    loop(1, FSDP, back_got)
    hot = hot_main_ref[...].reshape(main, rows)
    hot_spare = hot_spare_ref[...]
    back_spare = back_spare_in[...].reshape(FSDP, 1152)
    grad_rows = tn(hot, back_in[...].reshape(main, width)) + tn(
        hot_spare.astype(BF16), back_spare[:, :1024].astype(BF16)
    )
    sel = back_spare[:, 1024:]
    by_slot = jnp.sum(
        (hot.astype(F32) * to_column(sel, 32)).reshape(FSDP, 32, rows), axis=1
    ) + hot_spare * sel[:, 32:33]
    gg_ref[...] = jnp.zeros_like(gg_ref)
    for k in range(FSDP):
        gg_ref[pl.ds(peer(me, k), 1), :] = by_slot[k : k + 1]
    grad_gates = jnp.transpose(gg_ref[...])
    gates = gates_ref[...]
    grad_chosen = gates * (grad_gates - jnp.sum(gates * grad_gates, axis=1, keepdims=True))
    grad_logits = grad_chosen.astype(BF16)
    tail = packed_all_ref[:, :, 768:896].reshape(width, 128)
    gain_two = jnp.transpose(tail.astype(F32))[EXPERTS + 1 : EXPERTS + 2]
    router_part_ref[...] = tn(normed_two_ref[...], grad_logits)
    dy = grad_rows + nt(grad_logits, tail)
    middle = middle_ref[...]
    inverse = lax.rsqrt(jnp.mean(middle * middle, axis=-1, keepdims=True) + EPSILON)
    scaled = dy * gain_two
    second_ref[...] = jnp.sum(dy * middle * inverse, axis=0, keepdims=True)
    grad_middle_ref[...] = (
        cot_ref[...].astype(F32)
        + inverse * scaled
        - middle
        * inverse
        * inverse
        * inverse
        * jnp.mean(scaled * middle, axis=-1, keepdims=True)
    )

    def out_ready():
        def got(k):
            out_copy(k).wait_recv()
            out_spare_copy(k).wait_recv()

        loop(1, FSDP, got)

    def sent():
        def gone(k):
            spare_copy(k).wait_send()
            back_copy(k).wait_send()
            bspare_copy(k).wait_send()
            out_copy(k).wait_send()
            out_spare_copy(k).wait_send()

        loop(1, FSDP, gone)

    return out_ready, sent


def backward_part(
    out_ready, pair_copy,
    grad_middle_ref, packed_all_ref, heads_ref, normed_all_ref, attended_ref, cos_ref, sin_ref,
    seg_ref, grads_ref, middle_ref, hot_main_ref, hot_spare_ref,
    inputs_ref, router_part_ref, second_ref,
    output_ref, grad_inputs_ref, sums_ref, weight_grads_ref,
    branch_own, branch_all, out_in, out_spare_in, pair_in, across_send, across_in, dw_send, dw_in,
    normed_send, normed_in, sums_send, sums_in, small_own, small_in,
    branch_s, branch_r, across_s, across_r,
    dw_s, dw_r, normed_s, normed_r, sums_s, sums_r, small_s, small_r,
):
    me, tp = lax.axis_index("fsdp"), lax.axis_index("tp")
    rows, width = inputs_ref.shape
    total = seg_ref.shape[1]
    core = lax.rem(tp, 2)
    sibling = tp + 1 - 2 * core
    across = lax.rem(tp + 2, TP)

    def branch_copy(k):
        block, where = ((tp, across), (tp, sibling), (across, sibling))[k]
        src = branch_own if k < 2 else branch_all.at[block]
        return to_tp(src, branch_all.at[block], branch_s.at[k], branch_r.at[k], where)

    across_copy = to_tp(across_send, across_in, across_s.at[0], across_r.at[0], across)

    def dw_copy(k):
        p = peer(me, k)
        return to_side(dw_send.at[p], dw_in.at[me], dw_s.at[k], dw_r.at[k], p, side(tp, k))

    def normed_copy(x):
        return to_tp(
            normed_send.at[2 * x + 1 - core],
            normed_in.at[x],
            normed_s.at[x],
            normed_r.at[x],
            sibling,
        )

    normed_across = to_tp(
        normed_in.at[2], normed_in.at[3], normed_s.at[2], normed_r.at[2], across
    )

    def sums_copy(k):
        p = peer(me, k)
        return to_fsdp(sums_send.at[p], sums_in.at[k], sums_s.at[k], sums_r.at[k], p)

    def small_copy(k):
        return to_tp(small_own, small_in.at[k], small_s.at[k], small_r.at[k], lax.rem(tp + k, TP))

    grad_middle = grad_middle_ref[...]
    branch_own[...] = grad_middle.astype(BF16)
    branch_copy(0).start()
    branch_copy(1).start()
    branch_all[tp] = branch_own[...]
    branch_copy(0).wait_recv()
    branch_copy(2).start()

    for x in range(2):
        pair_copy(x).wait_recv()
    near = tp // 2
    far = 1 - near
    across_send[...] = (
        grads_ref[2 * far + core].astype(F32) + pair_in[far].astype(F32)
    ).astype(BF16)
    across_copy.start()

    seg_row = jnp.broadcast_to(seg_ref[...].astype(F32), (128, total))
    seg_col = jnp.transpose(seg_row)[:, :1]
    allowed = (
        (seg_col == seg_row[:1]) & (rows_of((total, total)) >= lanes((total, total)))
    ).astype(F32)

    branch_copy(1).wait_recv()
    branch_copy(2).wait_recv()
    branch = branch_all[...].reshape(total, width)
    out_part = tn(branch, attended_ref[...])
    grad_attended = nn(branch, packed_all_ref[:, :, 512:768].reshape(width, 256)).astype(BF16)
    scale = HEAD_SIZE ** (-0.5)
    dq, dk, dv = [], [], []
    for g in range(2):
        key = heads_ref[:, 256 + 64 * g : 320 + 64 * g]
        value = heads_ref[:, 384 + 64 * g : 448 + 64 * g]
        dk_sum, dv_sum = None, None
        for h in (2 * g, 2 * g + 1):
            q = heads_ref[:, 64 * h : 64 * h + 64]
            da = grad_attended[:, 64 * h : 64 * h + 64]
            scores = jnp.where(allowed > 0, nt(q, key) * scale, MASKED)
            top = jnp.max(scores, axis=1, keepdims=True)
            grown = jnp.exp(scores - top)
            whole = grown * (1.0 / jnp.sum(grown, axis=1, keepdims=True))
            grad_shares = nt(da, value)
            inner = jnp.sum(whole * grad_shares, axis=1, keepdims=True)
            grad_scores = (whole * (grad_shares - inner)).astype(BF16)
            dq.append(nn(grad_scores, key) * scale)
            dk_one = tn(grad_scores, q) * scale
            dv_one = tn(whole.astype(BF16), da)
            dk_sum = dk_one if dk_sum is None else dk_sum + dk_one
            dv_sum = dv_one if dv_sum is None else dv_sum + dv_one
        dk.append(dk_sum)
        dv.append(dv_sum)
    turned = jnp.concatenate(dq + dk, axis=1)
    turn = turned * wide_table(cos_ref[...], 384) - half_swap(turned) * wide_table(
        sin_ref[...], 384
    )
    grad_lin = jnp.concatenate([turn] + dv, axis=1).astype(BF16)
    grad_normed = nt(grad_lin, packed_all_ref[:, :, 0:512].reshape(width, 512))
    normed_send[...] = grad_normed.astype(BF16).reshape(TP, rows, width)
    for x in range(2):
        normed_copy(x).start()
    gain_one = jnp.transpose(packed_all_ref[:, :, 768:896].reshape(width, 128).astype(F32))[
        EXPERTS : EXPERTS + 1
    ]
    first = jnp.sum(grad_normed * normed_all_ref[...].astype(F32), axis=0, keepdims=True) / gain_one

    qkv_part = tn(normed_all_ref[...], grad_lin)
    sums_send[:, :, 0:512] = qkv_part.astype(BF16).reshape(FSDP, 32, 512)
    sums_send[:, :, 512:768] = out_part.astype(BF16).reshape(FSDP, 32, 256)
    at = rows_of((128, width))
    gains = jnp.where(at == EXPERTS, first, 0.0) + jnp.where(at == EXPERTS + 1, second_ref[...], 0.0)
    small = router_part_ref[...] + jnp.transpose(gains)
    sums_send[:, :, 768:896] = small.astype(BF16).reshape(FSDP, 32, 128)
    loop(1, FSDP, lambda k: sums_copy(k).start())
    sums_in[0] = sums_send[me]

    for x in range(2):
        normed_copy(x).wait_recv()
    normed_in[2] = (
        normed_send[across].astype(F32) + normed_in[far].astype(F32)
    ).astype(BF16)
    normed_across.start()

    across_copy.wait_recv()
    dw_send[...] = (
        grads_ref[tp].astype(F32) + pair_in[near].astype(F32) + across_in[...].astype(F32)
    ).astype(BF16)
    loop(1, FSDP, lambda k: dw_copy(k).start())
    dw_in[me] = dw_send[me]

    normed_across.wait_recv()
    dy = normed_send[tp].astype(F32) + normed_in[near].astype(F32) + normed_in[3].astype(F32)
    wide = inputs_ref[...].astype(F32)
    inverse = lax.rsqrt(jnp.mean(wide * wide, axis=-1, keepdims=True) + EPSILON)
    scaled = dy * gain_one
    grad_inputs_ref[...] = (
        grad_middle
        + inverse * scaled
        - wide
        * inverse
        * inverse
        * inverse
        * jnp.mean(scaled * wide, axis=-1, keepdims=True)
    )

    out_ready()
    hot = hot_main_ref[...].reshape(FSDP * 32, rows)
    output_ref[...] = (
        middle_ref[...]
        + tn(hot, out_in[...].reshape(FSDP * 32, width))
        + tn(hot_spare_ref[...].astype(BF16), out_spare_in[...].reshape(FSDP, width).astype(BF16))
    ).astype(BF16)

    loop(1, FSDP, lambda k: sums_copy(k).wait_recv())
    sums = jnp.sum(sums_in[...].astype(F32), axis=0)
    sums_ref[:, :768] = sums[:, :768]
    small_own[...] = sums[:, 768:]
    for k in (2, 1, 3):
        small_copy(k).start()
    loop(1, FSDP, lambda k: dw_copy(k).wait_recv())
    weight_grads_ref[...] = dw_in[...].astype(F32)
    for k in range(1, TP):
        small_copy(k).wait_recv()
    sums_ref[:, 768:] = small_own[...] + small_in[1] + small_in[2] + small_in[3]

    def gone(k):
        sums_copy(k).wait_send()
        dw_copy(k).wait_send()

    loop(1, FSDP, gone)
    for k in range(3):
        branch_copy(k).wait_send()
        small_copy(k + 1).wait_send()
    for x in range(2):
        normed_copy(x).wait_send()
        pair_copy(x).wait_send()
    normed_across.wait_send()
    across_copy.wait_send()


def layer_kernel(
    packed_ref, inputs_ref, seg_ref, routes_ref, blocks_ref, cot_ref,
    output_ref, grad_inputs_ref, sums_ref, weight_grads_ref,
    middle, normed_two, gates, slot, weights, cot_main, cot_spare, packed_all, heads, normed_all,
    attended, cosine, sine,
    inputs_all, blocks_in, rows_out, spare_out, branch_out, branch_in,
    router_part, second_part, hot_main, hot_spare, grad_middle, out_spare,
    gate_mat, up_mat, down_mat, gate_t, row_send, spare_send, row_in, spare_in,
    back_spare_send, back_in, back_spare_in,
    hidden, dgate, dup, ghidden, sel, gate_grads, out_in, out_spare_in,
    branch_own, branch_all, pair_in, across_send, across_in, dw_send, dw_in, normed_in,
    sums_send, sums_in, small_own, small_in,
    *sems,
):
    tp = lax.axis_index("tp")
    sems = list(sems)

    def take(count):
        taken = sems[:count]
        del sems[:count]
        return taken

    pass_weights, weights_ready, cot_ready, forward_sent = forward_part(
        packed_ref, inputs_ref, seg_ref, routes_ref, blocks_ref, cot_ref,
        middle, normed_two, gates, slot, weights, cot_main, cot_spare,
        packed_all, heads, normed_all, attended, cosine, sine,
        inputs_all, blocks_in, rows_out, spare_out, branch_out, branch_in,
        *take(15),
    )
    core = lax.rem(tp, 2)
    pair_s, pair_r = take(2)

    def pair_copy(x):
        return to_tp(
            weights.at[2 * x + 1 - core],
            pair_in.at[x],
            pair_s.at[x],
            pair_r.at[x],
            tp + 1 - 2 * core,
        )

    def start_pairs():
        for x in range(2):
            pair_copy(x).start()

    out_ready, expert_sent = expert_part(
        pass_weights, weights_ready, cot_ready, start_pairs,
        normed_two, gates, slot, weights, cot_main, cot_spare, middle, cot_ref,
        packed_all,
        row_send, out_spare, weights, grad_middle, router_part, second_part, hot_main, hot_spare,
        gate_mat, up_mat, down_mat, gate_t, row_send, spare_send, row_in, spare_in,
        rows_out, back_spare_send, back_in, back_spare_in,
        hidden, dgate, dup, ghidden, sel, gate_grads, out_in, out_spare_in,
        *take(12),
    )
    backward_part(
        out_ready, pair_copy,
        grad_middle, packed_all, heads, normed_all, attended, cosine, sine, seg_ref,
        weights, middle, hot_main, hot_spare, inputs_ref, router_part, second_part,
        output_ref, grad_inputs_ref, sums_ref, weight_grads_ref,
        branch_own, branch_all, out_in, out_spare_in, pair_in, across_send, across_in,
        dw_send, dw_in, branch_out, normed_in, sums_send, sums_in, small_own, small_in,
        *take(12),
    )
    forward_sent()
    expert_sent()


def layer(packed, inputs, seg, routes, blocks, cot):
    rows, width = inputs.shape
    total = seg.shape[1]
    hidden = 128 * TP
    slots = FSDP * SPARE
    vmem = pl.BlockSpec(memory_space=pltpu.VMEM)
    out = (
        shape((rows, width), BF16),
        shape((rows, width), F32),
        shape(packed.shape, F32),
        shape(blocks.shape, F32),
    )
    block = pltpu.VMEM((FSDP, 32, width), BF16)
    spare = pltpu.VMEM((FSDP, 1, width), F32)
    spare_wide = pltpu.VMEM((FSDP, 1, width + 128), F32)
    four = pltpu.VMEM((TP, rows, width), BF16)
    shards = pltpu.VMEM(blocks.shape, BF16)
    packs = pltpu.VMEM((FSDP, *packed.shape), BF16)
    return pl.pallas_call(
        layer_kernel,
        out_shape=out,
        in_specs=[vmem] * 6,
        out_specs=[vmem] * len(out),
        scratch_shapes=[
            pltpu.VMEM((rows, width), F32),
            pltpu.VMEM((rows, width), BF16),
            pltpu.VMEM((rows, 128), F32),
            pltpu.VMEM((EXPERTS, rows), F32),
            pltpu.VMEM((TP, *blocks.shape), BF16),
            block,
            spare,
            packs,
            pltpu.VMEM((total, 512), BF16),
            pltpu.VMEM((total, width), BF16),
            pltpu.VMEM((total, 256), BF16),
            pltpu.VMEM((total, 128), F32),
            pltpu.VMEM((total, 128), F32),
            four,
            shards,
            block,
            spare,
            four,
            four,
            pltpu.VMEM((width, 128), F32),
            pltpu.VMEM((1, width), F32),
            pltpu.VMEM((FSDP, 32, rows), BF16),
            pltpu.VMEM((FSDP, rows), F32),
            pltpu.VMEM((rows, width), F32),
            spare,
            *[pltpu.VMEM((width, hidden), BF16)] * 3,
            pltpu.VMEM((EXPERTS, rows), F32),
            block,
            spare_wide,
            block,
            spare_wide,
            spare_wide,
            block,
            spare_wide,
            *[pltpu.VMEM((slots, hidden), BF16)] * 3,
            pltpu.VMEM((slots, hidden), F32),
            pltpu.VMEM((FSDP, 128), F32),
            pltpu.VMEM((128, 128), F32),
            block,
            spare,
            pltpu.VMEM((rows, width), BF16),
            four,
            pltpu.VMEM((2, *blocks.shape), BF16),
            *[shards] * 4,
            four,
            packs,
            packs,
            pltpu.VMEM((32, 128), F32),
            pltpu.VMEM((TP, 32, 128), F32),
            *[dma(FSDP)] * 8,
            *[dma(TP)] * 6,
            dma(4),
            *[dma(2)] * 2,
            *[dma(FSDP)] * 12,
            *[dma(TP)] * 2,
            *[dma(1)] * 2,
            *[dma(FSDP)] * 2,
            *[dma(TP)] * 2,
            *[dma(FSDP)] * 2,
            *[dma(TP)] * 2,
        ],
        compiler_params=pltpu.CompilerParams(
            collective_id=1, has_side_effects=True, vmem_limit_bytes=62 * 2**20
        ),
        name="layer",
    )(packed, inputs, seg, routes, blocks, cot)


def per_device(
    inputs,
    segments,
    routes,
    query_weight,
    key_projection_weight,
    value_projection_weight,
    out_weight,
    router_weight,
    first_gain,
    second_gain,
    gate_weight,
    up_weight,
    down_weight,
    cotangent,
):
    row_count = inputs.shape[0]
    my_offset = lax.axis_index("tp") * row_count
    width_shard = query_weight.shape[0]
    q_cols, k_cols, o_cols = query_weight.shape[1], key_projection_weight.shape[1], out_weight.shape[0]

    wide = q_cols + 2 * k_cols + o_cols
    packed = jnp.concatenate(
        [
            query_weight,
            key_projection_weight,
            value_projection_weight,
            out_weight.T,
            router_weight,
            first_gain[:, None],
            second_gain[:, None],
            jnp.zeros((width_shard, 128 - EXPERTS - 2), BF16),
        ],
        axis=1,
    )
    blocks = jnp.concatenate(
        [gate_weight, up_weight, jnp.transpose(down_weight, (0, 2, 1))], axis=1
    )
    my_routes = lax.dynamic_slice_in_dim(routes, my_offset, row_count, 0)
    output, grad_inputs, sums, weight_grads = layer(
        packed, inputs, segments, my_routes, blocks, cotangent
    )
    return (
        output,
        grad_inputs,
        sums[:, :q_cols],
        sums[:, q_cols : q_cols + k_cols],
        sums[:, q_cols + k_cols : q_cols + 2 * k_cols],
        sums[:, q_cols + 2 * k_cols : wide].T,
        sums[:, wide : wide + EXPERTS],
        sums[:, wide + EXPERTS],
        sums[:, wide + EXPERTS + 1],
        weight_grads[:, :width_shard],
        weight_grads[:, width_shard : 2 * width_shard],
        jnp.transpose(weight_grads[:, 2 * width_shard :], (0, 2, 1)),
    )


def solution(mesh):
    return jax.shard_map(
        per_device,
        mesh=mesh,
        in_specs=(
            P(("fsdp", "tp"), None),
            P("fsdp", None),
            P("fsdp", None),
            P("fsdp", "tp"),
            P("fsdp", "tp"),
            P("fsdp", "tp"),
            P("tp", "fsdp"),
            P("fsdp", None),
            P("fsdp"),
            P("fsdp"),
            P(None, "fsdp", "tp"),
            P(None, "fsdp", "tp"),
            P(None, "tp", "fsdp"),
            P(("fsdp", "tp"), None),
        ),
        out_specs=(
            P(("fsdp", "tp"), None),
            P(("fsdp", "tp"), None),
            P("fsdp", "tp"),
            P("fsdp", "tp"),
            P("fsdp", "tp"),
            P("tp", "fsdp"),
            P("fsdp", None),
            P("fsdp"),
            P("fsdp"),
            P(None, "fsdp", "tp"),
            P(None, "fsdp", "tp"),
            P(None, "tp", "fsdp"),
        ),
        check_vma=False,
    )
```

```python
import math

import jax
import jax.numpy as jnp
from jax import lax
from jax.experimental import pallas as pl
from jax.experimental.pallas import tpu as pltpu
from jax.sharding import PartitionSpec as P

HEAD_SIZE = 64
EXPERTS = 32
TOP = 8


EPSILON = 1e-06
ROPE_BASE = 10000.0
MASKED = -1e30


MESH = pl.DeviceIdType.MESH
FSDP, TP, SPARE = 32, 4, 33
F32, BF16 = jnp.float32, jnp.bfloat16


def offset(k):
    a, b, c = k % 4, (k // 4) % 4, k // 16
    return a, (b + c) % 2, (a + b) % 4


def peer(me, k):
    dz, dx, dy = offset(k)
    z, x, y = me // 8, (me // 4) % 2, me % 4
    return ((z + dz) % 4 * 2 + (x + dx) % 2) * 4 + (y + dy) % 4


def giver(me, k):
    dz, dx, dy = offset(k)
    z, x, y = me // 8, (me // 4) % 2, me % 4
    return ((z + 4 - dz) % 4 * 2 + (x + dx) % 2) * 4 + (y + 4 - dy) % 4


def side(tp, k):
    return lax.rem(tp + 2 * offset(k)[1], TP)


def loop(low, high, step):
    def body(k, carry):
        step(k)
        return carry

    lax.fori_loop(low, high, body, 0)


def greet(me, tp):
    barrier = pltpu.get_barrier_semaphore()

    def signal(k, q):
        pl.semaphore_signal(
            barrier, inc=1, device_id={"fsdp": peer(me, k), "tp": q}, device_id_type=MESH
        )

    loop(1, FSDP, lambda k: signal(k, tp))
    loop(0, 16, lambda n: signal(n + 16 * ((n // 4 + 1) % 2), lax.rem(tp + 2, TP)))
    for k in range(1, TP):
        pl.semaphore_signal(
            barrier, inc=1, device_id={"tp": lax.rem(tp + k, TP)}, device_id_type=MESH
        )
    pl.semaphore_wait(barrier, FSDP - 1 + 16 + TP - 1)


def to_fsdp(src, dst, send, recv, where):
    return pltpu.make_async_remote_copy(
        src_ref=src,
        dst_ref=dst,
        send_sem=send,
        recv_sem=recv,
        device_id={"fsdp": where},
        device_id_type=MESH,
    )


def to_tp(src, dst, send, recv, where):
    return pltpu.make_async_remote_copy(
        src_ref=src,
        dst_ref=dst,
        send_sem=send,
        recv_sem=recv,
        device_id={"tp": where},
        device_id_type=MESH,
    )


def to_side(src, dst, send, recv, where, q):
    return pltpu.make_async_remote_copy(
        src_ref=src,
        dst_ref=dst,
        send_sem=send,
        recv_sem=recv,
        device_id={"fsdp": where, "tp": q},
        device_id_type=MESH,
    )


def nn(a, b):
    return jnp.dot(a, b, preferred_element_type=F32)


def nt(a, b):
    return lax.dot_general(a, b, (((1,), (1,)), ((), ())), preferred_element_type=F32)


def tn(a, b):
    return lax.dot_general(a, b, (((0,), (0,)), ((), ())), preferred_element_type=F32)


def lanes(shape):
    return lax.broadcasted_iota(jnp.int32, shape, len(shape) - 1)


def rows_of(shape):
    return lax.broadcasted_iota(jnp.int32, shape, 0)


def half_swap(v):
    width = v.shape[-1]
    front = lanes(v.shape) % HEAD_SIZE < HEAD_SIZE // 2
    ahead = pltpu.roll(v, width - HEAD_SIZE // 2, 1)
    behind = pltpu.roll(v, HEAD_SIZE // 2, 1)
    return jnp.where(front, -ahead, behind)


def wide_table(table, width):
    return jnp.concatenate([table] * (width // 128), axis=1)


def pick(slot_ref, experts, count):
    parts = []
    for e in experts:
        row = slot_ref[pl.ds(e, 1), :]
        parts.append(jnp.broadcast_to(row, (count, row.shape[1])))
    both = jnp.concatenate(parts, axis=0)
    want = (rows_of(both.shape) % count).astype(F32)
    return (both == want).astype(BF16)


def forward_part(
    query_ref, key_ref, value_ref, out_weight_ref, router_ref, first_gain_ref, second_gain_ref,
    gate_ref, up_ref, down_ref, inputs_ref, seg_ref, routes_ref, cot_ref,
    middle_ref, normed_two_ref, gates_ref, slot_ref, weights_ref, cot_main_ref, cot_spare_ref,
    packed_all_ref, out_all_ref, heads_ref, normed_all_ref, attended_ref, cos_ref, sin_ref,
    packed_ref, blocks_ref, inputs_all, blocks_in, send_main, send_spare, branch_out, branch_in,
    packed_send, packed_recv, outw_send, outw_recv, blocks_send, blocks_recv, main_send, main_recv, spare_send, spare_recv,
    inputs_send, inputs_recv, weights_send, weights_recv, branch_send, branch_recv, own_sem,
):
    me, tp = lax.axis_index("fsdp"), lax.axis_index("tp")
    rows, width = inputs_ref.shape
    total = seg_ref.shape[1]
    packed_ref[...] = jnp.zeros_like(packed_ref)
    packed_ref[:, 0:256] = query_ref[...]
    packed_ref[:, 256:384] = key_ref[...]
    packed_ref[:, 384:512] = value_ref[...]
    packed_ref[:, 512:544] = router_ref[...]
    shard = query_ref.shape[0]
    same_place = rows_of((shard, shard)) == lanes((shard, shard))
    for n, gain_ref in enumerate((first_gain_ref, second_gain_ref)):
        gain = jnp.broadcast_to(gain_ref[...].astype(F32), (shard, shard))
        column = jnp.sum(jnp.where(same_place, gain, 0.0), axis=1, keepdims=True)
        packed_ref[:, 544 + n : 545 + n] = column.astype(BF16)
    greet(me, tp)

    def outw_copy(k):
        return to_fsdp(
            out_weight_ref, out_all_ref.at[me], outw_send.at[k], outw_recv.at[k], peer(me, k)
        )

    def packed_copy(k):
        return to_fsdp(
            packed_ref, packed_all_ref.at[me], packed_send.at[k], packed_recv.at[k], peer(me, k)
        )

    core = lax.rem(tp, 2)
    sibling = tp + 1 - 2 * core
    across = lax.rem(tp + 2, TP)

    def inputs_copy(k):
        block, where = ((tp, across), (tp, sibling), (across, sibling))[k]
        src = inputs_ref if k < 2 else inputs_all.at[block]
        return to_tp(src, inputs_all.at[block], inputs_send.at[k], inputs_recv.at[k], where)

    def blocks_copy(k):
        p = peer(me, k)
        return to_side(
            blocks_ref.at[p], blocks_in.at[me], blocks_send.at[k], blocks_recv.at[k], p, side(tp, k)
        )

    def main_copy(k):
        return to_side(
            send_main.at[k],
            cot_main_ref.at[k],
            main_send.at[k],
            main_recv.at[k],
            peer(me, k),
            side(tp, k),
        )

    def spare_copy(k):
        return to_side(
            send_spare.at[k],
            cot_spare_ref.at[k],
            spare_send.at[k],
            spare_recv.at[k],
            peer(me, k),
            side(tp, k),
        )

    def branch_copy(x):
        return to_tp(
            branch_out.at[2 * x + 1 - core],
            branch_in.at[x],
            branch_send.at[x],
            branch_recv.at[x],
            sibling,
        )

    branch_across = to_tp(
        branch_in.at[2], branch_in.at[3], branch_send.at[2], branch_recv.at[2], across
    )

    inputs_copy(0).start()
    inputs_copy(1).start()
    loop(1, FSDP, lambda k: packed_copy(k).start())
    blocks_ref[:, 0:32, :] = gate_ref[...]
    blocks_ref[:, 32:64, :] = up_ref[...]
    blocks_ref[:, 64:96, :] = down_ref[...]
    loop(1, FSDP, lambda k: outw_copy(k).start())
    loop(1, FSDP, lambda k: blocks_copy(k).start())
    keep = [
        pltpu.make_async_copy(packed_ref, packed_all_ref.at[me], own_sem.at[0]),
        pltpu.make_async_copy(inputs_ref, inputs_all.at[tp], own_sem.at[1]),
        pltpu.make_async_copy(blocks_ref.at[me], blocks_in.at[me], own_sem.at[2]),
        pltpu.make_async_copy(out_weight_ref, out_all_ref.at[me], own_sem.at[4]),
    ]
    for copy in keep:
        copy.start()

    mine = routes_ref[:, pl.ds(pl.multiple_of(tp * rows, rows), rows)]
    at = rows_of((128, rows))
    member_t = jnp.zeros((128, rows), F32)
    for k in range(TOP):
        member_t = member_t + (mine[k : k + 1] == at).astype(F32)
    earlier = (rows_of((rows, rows)) < lanes((rows, rows))).astype(BF16)
    slot = nn(member_t.astype(BF16), earlier)
    slot_ref[...] = jnp.where(member_t > 0, slot, -1.0)[:EXPERTS]
    member = jnp.transpose(member_t)

    def some_rows(i):
        hot = pick(slot_ref, [peer(me, 4 * i + j) for j in range(4)], 40)
        out = nn(hot, cot_ref[...])
        for j in range(4):
            send_main[4 * i + j] = out[40 * j : 40 * j + 32].astype(BF16)
            send_spare[4 * i + j] = out[40 * j + 32 : 40 * j + 33]

        def go(k):
            main_copy(k).start()
            spare_copy(k).start()

        loop(jnp.maximum(4 * i, 1), 4 * i + 4, go)

    loop(0, FSDP // 4, some_rows)
    cot_main_ref[0] = send_main[0]
    cot_spare_ref[0] = send_spare[0]

    seg_row = jnp.broadcast_to(seg_ref[...].astype(F32), (128, total))
    seg_col = jnp.transpose(seg_row)[:, :1]
    same = (seg_col == seg_row[:1]) & (rows_of((total, total)) >= lanes((total, total)))
    allowed = same.astype(F32)
    place = jnp.sum(allowed, axis=1, keepdims=True) - 1.0
    halves = (lanes((1, 128)) % (HEAD_SIZE // 2)).astype(F32)
    rate = jnp.exp(halves * (-2.0 * math.log(ROPE_BASE) / HEAD_SIZE))
    angle = place * rate
    cos_ref[...] = jnp.cos(angle)
    sin_ref[...] = jnp.sin(angle)

    inputs_copy(0).wait_recv()
    inputs_copy(2).start()
    inputs_copy(1).wait_recv()
    inputs_copy(2).wait_recv()
    keep[1].wait()
    wide = inputs_all[...].reshape(total, width).astype(F32)
    inverse = lax.rsqrt(jnp.mean(wide * wide, axis=-1, keepdims=True) + EPSILON)

    loop(1, FSDP, lambda k: packed_copy(k).wait_recv())
    keep[0].wait()
    tail = jnp.transpose(packed_all_ref[:, :, 512:640].reshape(width, 128).astype(F32))
    normed = (wide * inverse * tail[EXPERTS : EXPERTS + 1]).astype(BF16)
    normed_all_ref[...] = normed
    lin = nn(normed, packed_all_ref[:, :, 0:512].reshape(width, 512))
    turn = lin[:, :384]
    turned = turn * wide_table(cos_ref[...], 384) + half_swap(turn) * wide_table(sin_ref[...], 384)
    heads_ref[:, :384] = turned.astype(BF16)
    heads_ref[:, 384:] = lin[:, 384:].astype(BF16)
    outs = []
    for h in range(4):
        g = h // 2
        q = heads_ref[:, 64 * h : 64 * h + 64]
        key = heads_ref[:, 256 + 64 * g : 320 + 64 * g]
        value = heads_ref[:, 384 + 64 * g : 448 + 64 * g]
        scores = jnp.where(allowed > 0, nt(q, key) * HEAD_SIZE ** (-0.5), MASKED)
        top = jnp.max(scores, axis=1, keepdims=True)
        grown = jnp.exp(scores - top)
        shares = (grown * (1.0 / jnp.sum(grown, axis=1, keepdims=True))).astype(BF16)
        outs.append(nn(shares, value))
    attended = jnp.concatenate(outs, axis=1).astype(BF16)
    attended_ref[...] = attended
    loop(1, FSDP, lambda k: outw_copy(k).wait_recv())
    keep[3].wait()
    branch = nt(attended, out_all_ref[...].reshape(width, 256))
    branch_out[...] = branch.astype(BF16).reshape(TP, rows, width)
    for x in range(2):
        branch_copy(x).start()
    for x in range(2):
        branch_copy(x).wait_recv()
    near = tp // 2
    far = 1 - near
    branch_in[2] = (
        branch_out[across].astype(F32) + branch_in[far].astype(F32)
    ).astype(BF16)
    branch_across.start()

    loop(1, FSDP, lambda k: blocks_copy(k).wait_recv())
    keep[2].wait()
    first = to_tp(blocks_in, weights_ref.at[tp], weights_send.at[0], weights_recv.at[0], across)
    second = to_tp(blocks_in, weights_ref.at[tp], weights_send.at[1], weights_recv.at[1], sibling)
    third = to_tp(
        weights_ref.at[across], weights_ref.at[across], weights_send.at[2], weights_recv.at[2], sibling
    )
    first.start()
    second.start()
    mine = pltpu.make_async_copy(blocks_in, weights_ref.at[tp], own_sem.at[3])
    mine.start()

    for x in range(2):
        branch_copy(x).wait_send()
    branch_across.wait_recv()
    middle = inputs_ref[...].astype(F32) + branch_out[tp].astype(F32)
    middle = middle + branch_in[near].astype(F32) + branch_in[3].astype(F32)
    middle_ref[...] = middle
    inverse_two = lax.rsqrt(jnp.mean(middle * middle, axis=-1, keepdims=True) + EPSILON)
    normed_two = (middle * inverse_two * tail[EXPERTS + 1 : EXPERTS + 2]).astype(BF16)
    normed_two_ref[...] = normed_two
    logits = nn(normed_two, packed_all_ref[:, :, 512:640].reshape(width, 128))
    logits = jnp.where(member > 0, logits, MASKED)
    grown = jnp.exp(logits - jnp.max(logits, axis=1, keepdims=True)) * member
    gates_ref[...] = grown / jnp.sum(grown, axis=1, keepdims=True)

    def pass_weights():
        first.wait_recv()
        third.start()

    def weights_ready():
        second.wait_recv()
        third.wait_recv()
        mine.wait()
        for copy in (first, second, third):
            copy.wait_send()

    def cot_ready():
        def got(k):
            main_copy(k).wait_recv()
            spare_copy(k).wait_recv()
            main_copy(k).wait_send()

        loop(1, FSDP, got)

    def sent():
        def gone(k):
            packed_copy(k).wait_send()
            outw_copy(k).wait_send()
            blocks_copy(k).wait_send()
            spare_copy(k).wait_send()

        loop(1, FSDP, gone)
        for k in range(3):
            inputs_copy(k).wait_send()
        branch_across.wait_send()

    return pass_weights, weights_ready, cot_ready, sent


def shape(dims, kind):
    return jax.ShapeDtypeStruct(dims, kind)


def dma(count):
    return pltpu.SemaphoreType.DMA((count,))


def to_column(table, count):
    n = table.shape[0]
    spread = jnp.broadcast_to(table[:, None, :], (n, count, 128)).reshape(n * count, 128)
    mine = lanes(spread.shape) == rows_of(spread.shape) % count
    return jnp.sum(jnp.where(mine, spread, 0.0), axis=1, keepdims=True)


def to_table(column, count):
    n = column.shape[0] // count
    spread = jnp.broadcast_to(column, (n * count, 128))
    mine = lanes(spread.shape) == rows_of(spread.shape) % count
    return jnp.sum(jnp.where(mine, spread, 0.0).reshape(n, count, 128), axis=1)


def expert_part(
    pass_weights, weights_ready, cot_ready, start_pairs,
    normed_two_ref, gates_ref, slot_ref, weights_ref, cot_main_ref, cot_spare_ref,
    middle_ref, cot_ref, packed_all_ref,
    out_main_ref, out_spare_ref, grads_ref, grad_middle_ref, router_part_ref, second_ref,
    hot_main_ref, hot_spare_ref,
    gate_mat, up_mat, down_mat, gate_t, row_send, spare_send, row_in, spare_in,
    back_send, back_spare_send, back_in, back_spare_in,
    hidden_ref, dgate_ref, dup_ref, ghidden_ref, sel_ref, gg_ref,
    out_in, out_spare_in,
    row_s, row_r, spare_s, spare_r, back_s, back_r, bspare_s, bspare_r,
    out_s, out_r, out_spare_s, out_spare_r,
):
    me, tp = lax.axis_index("fsdp"), lax.axis_index("tp")
    half = (me // 4) % 2
    rows, width = normed_two_ref.shape
    main = FSDP * 32

    def row_copy(k):
        return to_side(
            row_send.at[k], row_in.at[k], row_s.at[k], row_r.at[k], peer(me, k), side(tp, k)
        )

    def spare_copy(k):
        return to_side(
            spare_send.at[k], spare_in.at[k], spare_s.at[k], spare_r.at[k], peer(me, k), side(tp, k)
        )

    def back_copy(k):
        return to_side(
            back_send.at[k], back_in.at[k], back_s.at[k], back_r.at[k], giver(me, k), side(tp, k)
        )

    def bspare_copy(k):
        return to_side(
            back_spare_send.at[k],
            back_spare_in.at[k],
            bspare_s.at[k],
            bspare_r.at[k],
            giver(me, k),
            side(tp, k),
        )

    def out_copy(k):
        return to_side(
            out_main_ref.at[k], out_in.at[k], out_s.at[k], out_r.at[k], giver(me, k), side(tp, k)
        )

    def out_spare_copy(k):
        return to_side(
            out_spare_ref.at[k],
            out_spare_in.at[k],
            out_spare_s.at[k],
            out_spare_r.at[k],
            giver(me, k),
            side(tp, k),
        )

    gates_low = gates_ref[...].astype(BF16).astype(F32)
    gate_t[...] = jnp.transpose(gates_low)[:EXPERTS]

    def some_rows(i):
        experts = [peer(me, 4 * i + j) for j in range(4)]
        hot = pick(slot_ref, experts, 40)
        out = nn(hot, normed_two_ref[...])
        for j in range(4):
            k = 4 * i + j
            mine = hot[40 * j : 40 * j + 40].astype(F32)
            column = jnp.sum(mine * gate_t[pl.ds(experts[j], 1), :], axis=1, keepdims=True)
            row_send[k] = out[40 * j : 40 * j + 32].astype(BF16)
            spare_send[k, :, :1024] = out[40 * j + 32 : 40 * j + 33]
            spare_send[k, :, 1024:] = to_table(column, 40)
            hot_main_ref[k] = hot[40 * j : 40 * j + 32]
            hot_spare_ref[pl.ds(k, 1), :] = mine[32:33]

        def go(k):
            row_copy(k).start()
            spare_copy(k).start()

        loop(jnp.maximum(4 * i, 1), 4 * i + 4, go)

    loop(0, FSDP // 4, some_rows)
    row_in[0] = row_send[0]
    spare_in[0] = spare_send[0]

    pass_weights()
    weights_ready()

    def side_by_side(i):
        at = pl.ds(pl.multiple_of(128 * i, 128), 128)
        swap = 2 * lax.rem(half + i, 2)
        for j in range(TP):
            cols = slice(128 * j, 128 * j + 128)
            block = weights_ref[lax.rem(j + swap, TP), pl.ds(4 * i, 4)]
            gate_mat[at, cols] = block[:, 0:32].reshape(128, 128)
            up_mat[at, cols] = block[:, 32:64].reshape(128, 128)
            down_mat[at, cols] = block[:, 64:96].reshape(128, 128)

    loop(0, 8, side_by_side)

    cot_ready()

    def hidden_grads(i):
        cot_rows = cot_main_ref[pl.ds(8 * i, 8)].reshape(256, width)
        ghidden_ref[pl.ds(256 * i, 256), :] = nn(cot_rows, down_mat[...])

    loop(0, 4, hidden_grads)
    cot_spare = cot_spare_ref[...].reshape(FSDP, width).astype(BF16)
    ghidden_ref[pl.ds(main, FSDP), :] = nn(cot_spare, down_mat[...])

    def expert_rows(x, gate, where):
        gate_act = nn(x, gate_mat[...])
        up_act = nn(x, up_mat[...])
        grad_hidden = ghidden_ref[where, :]
        sigmoid_gate = 1.0 / (1.0 + jnp.exp(-gate_act))
        silu_gate = gate_act * sigmoid_gate
        both = silu_gate * up_act
        hidden_ref[where, :] = (both * gate).astype(BF16)
        grad_prod = grad_hidden * gate
        dgate = (
            grad_prod * up_act * sigmoid_gate * (1.0 + gate_act * (1.0 - sigmoid_gate))
        ).astype(BF16)
        dup = (grad_prod * silu_gate).astype(BF16)
        dgate_ref[where, :] = dgate
        dup_ref[where, :] = dup
        grad_in = nt(dgate, gate_mat[...]) + nt(dup, up_mat[...])
        return grad_in, jnp.sum(both * grad_hidden, axis=1, keepdims=True)

    def some_experts(i):
        def got(k):
            row_copy(k).wait_recv()
            spare_copy(k).wait_recv()

        loop(jnp.maximum(8 * i, 1), 8 * i + 8, got)
        x = row_in[pl.ds(8 * i, 8)].reshape(256, width)
        gate = to_column(spare_in[pl.ds(8 * i, 8), :, 1024:].reshape(8, 128), 32)
        grad_in, sel = expert_rows(x, gate, pl.ds(256 * i, 256))
        back_send[pl.ds(8 * i, 8)] = grad_in.astype(BF16).reshape(8, 32, width)
        sel_ref[pl.ds(8 * i, 8), :] = to_table(sel, 32)
        loop(jnp.maximum(8 * i, 1), 8 * i + 8, lambda k: back_copy(k).start())

    loop(0, 4, some_experts)
    spare = spare_in[...].reshape(FSDP, 1152)
    spare_gate = spare[:, 1056:1057]
    spare_rows = spare[:, :1024].astype(BF16)
    grad_in, sel = expert_rows(spare_rows, spare_gate, pl.ds(main, FSDP))
    sel_all = jnp.where(lanes((FSDP, 128)) == 32, sel, sel_ref[...])
    for k in range(FSDP):
        back_spare_send[k, :, :1024] = grad_in[k : k + 1]
        back_spare_send[k, :, 1024:] = sel_all[k : k + 1]
    loop(1, FSDP, lambda k: bspare_copy(k).start())
    back_in[0] = back_send[0]
    back_spare_in[0] = back_spare_send[0]

    loop(1, FSDP, lambda k: row_copy(k).wait_send())

    def outputs(i):
        out = nt(hidden_ref[pl.ds(256 * i, 256), :], down_mat[...])
        out_main_ref[pl.ds(8 * i, 8)] = out.astype(BF16).reshape(8, 32, width)
        loop(jnp.maximum(8 * i, 1), 8 * i + 8, lambda k: out_copy(k).start())

    loop(0, 4, outputs)
    out = nt(hidden_ref[pl.ds(main, FSDP), :], down_mat[...])
    for k in range(FSDP):
        out_spare_ref[k] = out[k : k + 1]
    loop(1, FSDP, lambda k: out_spare_copy(k).start())
    out_in[0] = out_main_ref[0]
    out_spare_in[0] = out_spare_ref[0]

    def weight_grads(i):
        at = pl.ds(pl.multiple_of(256 * i, 256), 256)
        x = row_in[:, :, at].reshape(main, 256)
        x_spare = spare_in[:, :, at].reshape(FSDP, 256).astype(BF16)
        c = cot_main_ref[:, :, at].reshape(main, 256)
        c_spare = cot_spare_ref[:, :, at].reshape(FSDP, 256).astype(BF16)
        for m, (a, a_spare, b) in enumerate(
            ((x, x_spare, dgate_ref), (x, x_spare, dup_ref), (c, c_spare, hidden_ref))
        ):
            part = tn(a, b[pl.ds(0, main), :]) + tn(a_spare, b[pl.ds(main, FSDP), :])
            part = part.astype(BF16)
            for j in range(TP):
                for h in range(2):
                    grads_ref[
                        lax.rem(j + 2 * lax.rem(half + h, 2), TP),
                        pl.ds(8 * i + 4 * h, 4),
                        32 * m : 32 * m + 32,
                        :,
                    ] = part[128 * h : 128 * h + 128, 128 * j : 128 * j + 128].reshape(4, 32, 128)

    loop(0, 4, weight_grads)

    start_pairs()

    def back_got(k):
        back_copy(k).wait_recv()
        bspare_copy(k).wait_recv()

    loop(1, FSDP, back_got)
    hot = hot_main_ref[...].reshape(main, rows)
    hot_spare = hot_spare_ref[...]
    back_spare = back_spare_in[...].reshape(FSDP, 1152)
    grad_rows = tn(hot, back_in[...].reshape(main, width)) + tn(
        hot_spare.astype(BF16), back_spare[:, :1024].astype(BF16)
    )
    sel = back_spare[:, 1024:]
    by_slot = jnp.sum(
        (hot.astype(F32) * to_column(sel, 32)).reshape(FSDP, 32, rows), axis=1
    ) + hot_spare * sel[:, 32:33]
    gg_ref[...] = jnp.zeros_like(gg_ref)
    for k in range(FSDP):
        gg_ref[pl.ds(peer(me, k), 1), :] = by_slot[k : k + 1]
    grad_gates = jnp.transpose(gg_ref[...])
    gates = gates_ref[...]
    grad_chosen = gates * (grad_gates - jnp.sum(gates * grad_gates, axis=1, keepdims=True))
    grad_logits = grad_chosen.astype(BF16)
    tail = packed_all_ref[:, :, 512:640].reshape(width, 128)
    gain_two = jnp.transpose(tail.astype(F32))[EXPERTS + 1 : EXPERTS + 2]
    router_part_ref[...] = tn(normed_two_ref[...], grad_logits)
    dy = grad_rows + nt(grad_logits, tail)
    middle = middle_ref[...]
    inverse = lax.rsqrt(jnp.mean(middle * middle, axis=-1, keepdims=True) + EPSILON)
    scaled = dy * gain_two
    second_ref[...] = jnp.sum(dy * middle * inverse, axis=0, keepdims=True)
    grad_middle_ref[...] = (
        cot_ref[...].astype(F32)
        + inverse * scaled
        - middle
        * inverse
        * inverse
        * inverse
        * jnp.mean(scaled * middle, axis=-1, keepdims=True)
    )

    def out_ready():
        def got(k):
            out_copy(k).wait_recv()
            out_spare_copy(k).wait_recv()

        loop(1, FSDP, got)

    def sent():
        def gone(k):
            spare_copy(k).wait_send()
            back_copy(k).wait_send()
            bspare_copy(k).wait_send()
            out_copy(k).wait_send()
            out_spare_copy(k).wait_send()

        loop(1, FSDP, gone)

    return out_ready, sent


def backward_part(
    out_ready, pair_copy,
    grad_middle_ref, packed_all_ref, out_all_ref, heads_ref, normed_all_ref, attended_ref,
    cos_ref, sin_ref,
    seg_ref, grads_ref, middle_ref, hot_main_ref, hot_spare_ref,
    inputs_ref, router_part_ref, second_ref,
    output_ref, grad_inputs_ref, sums_ref, out_sums_ref, dw_in,
    branch_own, branch_all, out_in, out_spare_in, pair_in, across_send, across_in, dw_send,
    normed_send, normed_in, sums_send, sums_in, outs_send, outs_in, small_own, small_in,
    branch_s, branch_r, across_s, across_r,
    dw_s, dw_r, normed_s, normed_r, sums_s, sums_r, outs_s, outs_r, small_s, small_r,
):
    me, tp = lax.axis_index("fsdp"), lax.axis_index("tp")
    rows, width = inputs_ref.shape
    total = seg_ref.shape[1]
    core = lax.rem(tp, 2)
    sibling = tp + 1 - 2 * core
    across = lax.rem(tp + 2, TP)

    def branch_copy(k):
        block, where = ((tp, across), (tp, sibling), (across, sibling))[k]
        src = branch_own if k < 2 else branch_all.at[block]
        return to_tp(src, branch_all.at[block], branch_s.at[k], branch_r.at[k], where)

    across_copy = to_tp(across_send, across_in, across_s.at[0], across_r.at[0], across)

    def dw_copy(k):
        p = peer(me, k)
        return to_side(dw_send.at[p], dw_in.at[me], dw_s.at[k], dw_r.at[k], p, side(tp, k))

    def normed_copy(x):
        return to_tp(
            normed_send.at[2 * x + 1 - core],
            normed_in.at[x],
            normed_s.at[x],
            normed_r.at[x],
            sibling,
        )

    normed_across = to_tp(
        normed_in.at[2], normed_in.at[3], normed_s.at[2], normed_r.at[2], across
    )

    def sums_copy(k):
        p = peer(me, k)
        return to_fsdp(sums_send.at[p], sums_in.at[k], sums_s.at[k], sums_r.at[k], p)

    def outs_copy(k):
        p = peer(me, k)
        return to_fsdp(outs_send.at[p], outs_in.at[k], outs_s.at[k], outs_r.at[k], p)

    def small_copy(k):
        return to_tp(small_own, small_in.at[k], small_s.at[k], small_r.at[k], lax.rem(tp + k, TP))

    grad_middle = grad_middle_ref[...]
    branch_own[...] = grad_middle.astype(BF16)
    branch_copy(0).start()
    branch_copy(1).start()
    branch_all[tp] = branch_own[...]
    branch_copy(0).wait_recv()
    branch_copy(2).start()

    for x in range(2):
        pair_copy(x).wait_recv()
    near = tp // 2
    far = 1 - near
    across_send[...] = (
        grads_ref[2 * far + core].astype(F32) + pair_in[far].astype(F32)
    ).astype(BF16)
    across_copy.start()

    seg_row = jnp.broadcast_to(seg_ref[...].astype(F32), (128, total))
    seg_col = jnp.transpose(seg_row)[:, :1]
    allowed = (
        (seg_col == seg_row[:1]) & (rows_of((total, total)) >= lanes((total, total)))
    ).astype(F32)

    branch_copy(1).wait_recv()
    branch_copy(2).wait_recv()
    branch = branch_all[...].reshape(total, width)
    out_part = tn(branch, attended_ref[...])
    outs_send[...] = out_part.astype(BF16).reshape(FSDP, 32, 256)
    loop(1, FSDP, lambda k: outs_copy(k).start())
    outs_in[0] = outs_send[me]
    grad_attended = nn(branch, out_all_ref[...].reshape(width, 256)).astype(BF16)
    scale = HEAD_SIZE ** (-0.5)
    dq, dk, dv = [], [], []
    for g in range(2):
        key = heads_ref[:, 256 + 64 * g : 320 + 64 * g]
        value = heads_ref[:, 384 + 64 * g : 448 + 64 * g]
        dk_sum, dv_sum = None, None
        for h in (2 * g, 2 * g + 1):
            q = heads_ref[:, 64 * h : 64 * h + 64]
            da = grad_attended[:, 64 * h : 64 * h + 64]
            scores = jnp.where(allowed > 0, nt(q, key) * scale, MASKED)
            top = jnp.max(scores, axis=1, keepdims=True)
            grown = jnp.exp(scores - top)
            whole = grown * (1.0 / jnp.sum(grown, axis=1, keepdims=True))
            grad_shares = nt(da, value)
            inner = jnp.sum(whole * grad_shares, axis=1, keepdims=True)
            grad_scores = (whole * (grad_shares - inner)).astype(BF16)
            dq.append(nn(grad_scores, key) * scale)
            dk_one = tn(grad_scores, q) * scale
            dv_one = tn(whole.astype(BF16), da)
            dk_sum = dk_one if dk_sum is None else dk_sum + dk_one
            dv_sum = dv_one if dv_sum is None else dv_sum + dv_one
        dk.append(dk_sum)
        dv.append(dv_sum)
        if g > 0:
            continue
        across_copy.wait_recv()
        dw_send[...] = (
            grads_ref[tp].astype(F32) + pair_in[near].astype(F32) + across_in[...].astype(F32)
        ).astype(BF16)
        loop(1, FSDP, lambda k: dw_copy(k).start())
        dw_in[me] = dw_send[me]
    turned = jnp.concatenate(dq + dk, axis=1)
    turn = turned * wide_table(cos_ref[...], 384) - half_swap(turned) * wide_table(
        sin_ref[...], 384
    )
    grad_lin = jnp.concatenate([turn] + dv, axis=1).astype(BF16)
    grad_normed = nt(grad_lin, packed_all_ref[:, :, 0:512].reshape(width, 512))
    normed_send[...] = grad_normed.astype(BF16).reshape(TP, rows, width)
    for x in range(2):
        normed_copy(x).start()
    gain_one = jnp.transpose(packed_all_ref[:, :, 512:640].reshape(width, 128).astype(F32))[
        EXPERTS : EXPERTS + 1
    ]
    first = jnp.sum(grad_normed * normed_all_ref[...].astype(F32), axis=0, keepdims=True) / gain_one

    qkv_part = tn(normed_all_ref[...], grad_lin)
    sums_send[:, :, 0:512] = qkv_part.astype(BF16).reshape(FSDP, 32, 512)
    at = rows_of((128, width))
    gains = jnp.where(at == EXPERTS, first, 0.0) + jnp.where(at == EXPERTS + 1, second_ref[...], 0.0)
    small = router_part_ref[...] + jnp.transpose(gains)
    sums_send[:, :, 512:640] = small.astype(BF16).reshape(FSDP, 32, 128)
    loop(1, FSDP, lambda k: sums_copy(k).start())
    sums_in[0] = sums_send[me]

    for x in range(2):
        normed_copy(x).wait_recv()
    normed_in[2] = (
        normed_send[across].astype(F32) + normed_in[far].astype(F32)
    ).astype(BF16)
    normed_across.start()

    normed_across.wait_recv()
    dy = normed_send[tp].astype(F32) + normed_in[near].astype(F32) + normed_in[3].astype(F32)
    wide = inputs_ref[...].astype(F32)
    inverse = lax.rsqrt(jnp.mean(wide * wide, axis=-1, keepdims=True) + EPSILON)
    scaled = dy * gain_one
    grad_inputs_ref[...] = (
        grad_middle
        + inverse * scaled
        - wide
        * inverse
        * inverse
        * inverse
        * jnp.mean(scaled * wide, axis=-1, keepdims=True)
    )

    out_ready()
    hot = hot_main_ref[...].reshape(FSDP * 32, rows)
    output_ref[...] = (
        middle_ref[...]
        + tn(hot, out_in[...].reshape(FSDP * 32, width))
        + tn(hot_spare_ref[...].astype(BF16), out_spare_in[...].reshape(FSDP, width).astype(BF16))
    ).astype(BF16)

    loop(1, FSDP, lambda k: sums_copy(k).wait_recv())
    sums = jnp.sum(sums_in[...].astype(F32), axis=0)
    sums_ref[:, :512] = sums[:, :512]
    small_own[...] = sums[:, 512:]
    for k in (2, 1, 3):
        small_copy(k).start()
    loop(1, FSDP, lambda k: dw_copy(k).wait_recv())
    loop(1, FSDP, lambda k: outs_copy(k).wait_recv())
    out_sums_ref[...] = jnp.sum(outs_in[...].astype(F32), axis=0)
    for k in range(1, TP):
        small_copy(k).wait_recv()
    sums_ref[:, 512:] = small_own[...] + small_in[1] + small_in[2] + small_in[3]

    def gone(k):
        sums_copy(k).wait_send()
        outs_copy(k).wait_send()
        dw_copy(k).wait_send()

    loop(1, FSDP, gone)
    for k in range(3):
        branch_copy(k).wait_send()
        small_copy(k + 1).wait_send()
    for x in range(2):
        normed_copy(x).wait_send()
        pair_copy(x).wait_send()
    normed_across.wait_send()
    across_copy.wait_send()


def layer_kernel(
    query_ref, key_ref, value_ref, out_weight_ref, router_ref, first_gain_ref, second_gain_ref,
    gate_ref, up_ref, down_ref, inputs_ref, seg_ref, routes_ref, cot_ref,
    output_ref, grad_inputs_ref, sums_ref, out_sums_ref, weight_grads_ref,
    middle, normed_two, gates, slot, weights, cot_main, cot_spare, packed_all, out_all,
    heads, normed_all, attended, cosine, sine,
    packed, blocks, inputs_all, blocks_in, rows_out, spare_out, branch_out, branch_in,
    router_part, second_part, hot_main, hot_spare, grad_middle, out_spare,
    gate_mat, up_mat, down_mat, gate_t, row_send, spare_send, row_in, spare_in,
    back_spare_send, back_in, back_spare_in,
    hidden, dgate, dup, ghidden, sel, gate_grads, out_in, out_spare_in,
    branch_own, branch_all, pair_in, across_send, across_in, dw_send, normed_in,
    sums_send, sums_in, outs_send, outs_in, small_own, small_in,
    *sems,
):
    tp = lax.axis_index("tp")
    sems = list(sems)

    def take(count):
        taken = sems[:count]
        del sems[:count]
        return taken

    pass_weights, weights_ready, cot_ready, forward_sent = forward_part(
        query_ref, key_ref, value_ref, out_weight_ref, router_ref, first_gain_ref,
        second_gain_ref, gate_ref, up_ref, down_ref, inputs_ref, seg_ref, routes_ref, cot_ref,
        middle, normed_two, gates, slot, weights, cot_main, cot_spare,
        packed_all, out_all, heads, normed_all, attended, cosine, sine,
        packed, blocks, inputs_all, blocks_in, rows_out, spare_out, branch_out, branch_in,
        *take(17),
    )
    core = lax.rem(tp, 2)
    pair_s, pair_r = take(2)

    def pair_copy(x):
        return to_tp(
            weights.at[2 * x + 1 - core],
            pair_in.at[x],
            pair_s.at[x],
            pair_r.at[x],
            tp + 1 - 2 * core,
        )

    def start_pairs():
        for x in range(2):
            pair_copy(x).start()

    out_ready, expert_sent = expert_part(
        pass_weights, weights_ready, cot_ready, start_pairs,
        normed_two, gates, slot, weights, cot_main, cot_spare, middle, cot_ref,
        packed_all,
        row_send, out_spare, weights, grad_middle, router_part, second_part, hot_main, hot_spare,
        gate_mat, up_mat, down_mat, gate_t, row_send, spare_send, row_in, spare_in,
        rows_out, back_spare_send, back_in, back_spare_in,
        hidden, dgate, dup, ghidden, sel, gate_grads, out_in, out_spare_in,
        *take(12),
    )
    backward_part(
        out_ready, pair_copy,
        grad_middle, packed_all, out_all, heads, normed_all, attended, cosine, sine, seg_ref,
        weights, middle, hot_main, hot_spare, inputs_ref, router_part, second_part,
        output_ref, grad_inputs_ref, sums_ref, out_sums_ref, weight_grads_ref,
        branch_own, branch_all, out_in, out_spare_in, pair_in, across_send, across_in,
        dw_send, branch_out, normed_in, sums_send, sums_in, outs_send, outs_in,
        small_own, small_in,
        *take(14),
    )
    forward_sent()
    expert_sent()


def layer(*operands):
    inputs, seg = operands[10], operands[11]
    rows, width = inputs.shape
    total = seg.shape[1]
    packed_shape, out_shape, blocks_shape = (32, 640), (32, 256), (EXPERTS, 96, 128)
    hidden = 128 * TP
    slots = FSDP * SPARE
    vmem = pl.BlockSpec(memory_space=pltpu.VMEM)
    out = (
        shape((rows, width), BF16),
        shape((rows, width), F32),
        shape(packed_shape, F32),
        shape(out_shape, F32),
        shape(blocks_shape, BF16),
    )
    block = pltpu.VMEM((FSDP, 32, width), BF16)
    spare = pltpu.VMEM((FSDP, 1, width), F32)
    spare_wide = pltpu.VMEM((FSDP, 1, width + 128), F32)
    four = pltpu.VMEM((TP, rows, width), BF16)
    shards = pltpu.VMEM(blocks_shape, BF16)
    packs = pltpu.VMEM((FSDP, *packed_shape), BF16)
    outs = pltpu.VMEM((FSDP, *out_shape), BF16)
    return pl.pallas_call(
        layer_kernel,
        out_shape=out,
        in_specs=[vmem] * len(operands),
        out_specs=[vmem] * len(out),
        scratch_shapes=[
            pltpu.VMEM((rows, width), F32),
            pltpu.VMEM((rows, width), BF16),
            pltpu.VMEM((rows, 128), F32),
            pltpu.VMEM((EXPERTS, rows), F32),
            pltpu.VMEM((TP, *blocks_shape), BF16),
            block,
            spare,
            packs,
            outs,
            pltpu.VMEM((total, 512), BF16),
            pltpu.VMEM((total, width), BF16),
            pltpu.VMEM((total, 256), BF16),
            pltpu.VMEM((total, 128), F32),
            pltpu.VMEM((total, 128), F32),
            pltpu.VMEM(packed_shape, BF16),
            shards,
            four,
            shards,
            block,
            spare,
            four,
            four,
            pltpu.VMEM((width, 128), F32),
            pltpu.VMEM((1, width), F32),
            pltpu.VMEM((FSDP, 32, rows), BF16),
            pltpu.VMEM((FSDP, rows), F32),
            pltpu.VMEM((rows, width), F32),
            spare,
            *[pltpu.VMEM((width, hidden), BF16)] * 3,
            pltpu.VMEM((EXPERTS, rows), F32),
            block,
            spare_wide,
            block,
            spare_wide,
            spare_wide,
            block,
            spare_wide,
            *[pltpu.VMEM((slots, hidden), BF16)] * 3,
            pltpu.VMEM((slots, hidden), F32),
            pltpu.VMEM((FSDP, 128), F32),
            pltpu.VMEM((128, 128), F32),
            block,
            spare,
            pltpu.VMEM((rows, width), BF16),
            four,
            pltpu.VMEM((2, *blocks_shape), BF16),
            *[shards] * 3,
            four,
            packs,
            packs,
            outs,
            outs,
            pltpu.VMEM((32, 128), F32),
            pltpu.VMEM((TP, 32, 128), F32),
            *[dma(FSDP)] * 10,
            *[dma(TP)] * 6,
            dma(5),
            *[dma(2)] * 2,
            *[dma(FSDP)] * 12,
            *[dma(TP)] * 2,
            *[dma(1)] * 2,
            *[dma(FSDP)] * 2,
            *[dma(TP)] * 2,
            *[dma(FSDP)] * 4,
            *[dma(TP)] * 2,
        ],
        compiler_params=pltpu.CompilerParams(
            collective_id=1, has_side_effects=True, vmem_limit_bytes=62 * 2**20
        ),
        name="layer",
    )(*operands)


def finish_kernel(
    output_in, grad_inputs_in, sums_ref, out_sums_ref, weight_grads_ref,
    output_ref, grad_inputs_ref, query_ref, key_ref, value_ref, out_ref, router_ref,
    gains_ref, gate_ref, up_ref, down_ref,
):
    output_ref[...] = output_in[...]
    grad_inputs_ref[...] = grad_inputs_in[...]
    query_ref[...] = sums_ref[:, 0:256]
    key_ref[...] = sums_ref[:, 256:384]
    value_ref[...] = sums_ref[:, 384:512]
    out_ref[...] = out_sums_ref[...]
    router_ref[...] = sums_ref[:, 512:544]
    tail = jnp.concatenate([sums_ref[:, 512:640], jnp.zeros((96, 128), F32)], axis=0)
    gains_ref[...] = jnp.transpose(tail)[EXPERTS : EXPERTS + 8, :32]
    gate_ref[...] = weight_grads_ref[:, 0:32].astype(F32)
    up_ref[...] = weight_grads_ref[:, 32:64].astype(F32)
    down_ref[...] = weight_grads_ref[:, 64:96].astype(F32)


def finish(*operands):
    vmem = pl.BlockSpec(memory_space=pltpu.VMEM)
    shard = shape((EXPERTS, 32, 128), F32)
    out = (
        shape(operands[0].shape, BF16),
        shape(operands[1].shape, F32),
        shape((32, 256), F32),
        shape((32, 128), F32),
        shape((32, 128), F32),
        shape((32, 256), F32),
        shape((32, 32), F32),
        shape((8, 32), F32),
        shard,
        shard,
        shard,
    )
    return pl.pallas_call(
        finish_kernel,
        out_shape=out,
        in_specs=[vmem] * len(operands),
        out_specs=[vmem] * len(out),
        compiler_params=pltpu.CompilerParams(vmem_limit_bytes=32 * 2**20),
        name="finish",
    )(*operands)


def per_device(
    inputs,
    segments,
    routes,
    query_weight,
    key_projection_weight,
    value_projection_weight,
    out_weight,
    router_weight,
    first_gain,
    second_gain,
    gate_weight,
    up_weight,
    down_weight,
    cotangent,
):
    parts = layer(
        query_weight,
        key_projection_weight,
        value_projection_weight,
        out_weight.T,
        router_weight,
        first_gain[None, :],
        second_gain[None, :],
        gate_weight,
        up_weight,
        jnp.transpose(down_weight, (0, 2, 1)),
        inputs,
        segments,
        routes.T,
        cotangent,
    )
    (
        output, grad_inputs, grad_query, grad_key, grad_value, grad_out, grad_router,
        grad_gains, grad_gate, grad_up, grad_down,
    ) = finish(*parts)
    return (
        output,
        grad_inputs,
        grad_query,
        grad_key,
        grad_value,
        grad_out.T,
        grad_router,
        grad_gains[0],
        grad_gains[1],
        grad_gate,
        grad_up,
        jnp.transpose(grad_down, (0, 2, 1)),
    )


def solution(mesh):
    return jax.shard_map(
        per_device,
        mesh=mesh,
        in_specs=(
            P(("fsdp", "tp"), None),
            P("fsdp", None),
            P("fsdp", None),
            P("fsdp", "tp"),
            P("fsdp", "tp"),
            P("fsdp", "tp"),
            P("tp", "fsdp"),
            P("fsdp", None),
            P("fsdp"),
            P("fsdp"),
            P(None, "fsdp", "tp"),
            P(None, "fsdp", "tp"),
            P(None, "tp", "fsdp"),
            P(("fsdp", "tp"), None),
        ),
        out_specs=(
            P(("fsdp", "tp"), None),
            P(("fsdp", "tp"), None),
            P("fsdp", "tp"),
            P("fsdp", "tp"),
            P("fsdp", "tp"),
            P("tp", "fsdp"),
            P("fsdp", None),
            P("fsdp"),
            P("fsdp"),
            P(None, "fsdp", "tp"),
            P(None, "fsdp", "tp"),
            P(None, "tp", "fsdp"),
        ),
        check_vma=False,
    )
```

```python
import math

import jax
import jax.numpy as jnp
from jax import lax
from jax.experimental import pallas as pl
from jax.experimental.pallas import tpu as pltpu
from jax.sharding import PartitionSpec as P

HEAD_SIZE = 64
EXPERTS = 32
TOP = 8


EPSILON = 1e-06
ROPE_BASE = 10000.0
MASKED = -1e30


MESH = pl.DeviceIdType.MESH
FSDP, TP, SPARE = 32, 4, 33
F32, BF16 = jnp.float32, jnp.bfloat16


def offset(k):
    a, b, c = k % 4, (k // 4) % 4, k // 16
    return a, (b + c) % 2, (a + b) % 4


def peer(me, k):
    dz, dx, dy = offset(k)
    z, x, y = me // 8, (me // 4) % 2, me % 4
    return ((z + dz) % 4 * 2 + (x + dx) % 2) * 4 + (y + dy) % 4


def giver(me, k):
    dz, dx, dy = offset(k)
    z, x, y = me // 8, (me // 4) % 2, me % 4
    return ((z + 4 - dz) % 4 * 2 + (x + dx) % 2) * 4 + (y + 4 - dy) % 4


def side(tp, k):
    return lax.rem(tp + 2 * offset(k)[1], TP)


def loop(low, high, step):
    def body(k, carry):
        step(k)
        return carry

    lax.fori_loop(low, high, body, 0)


def greet(me, tp):
    barrier = pltpu.get_barrier_semaphore()

    def signal(k, q):
        pl.semaphore_signal(
            barrier, inc=1, device_id={"fsdp": peer(me, k), "tp": q}, device_id_type=MESH
        )

    loop(1, FSDP, lambda k: signal(k, tp))
    loop(0, 16, lambda n: signal(n + 16 * ((n // 4 + 1) % 2), lax.rem(tp + 2, TP)))
    for k in range(1, TP):
        pl.semaphore_signal(
            barrier, inc=1, device_id={"tp": lax.rem(tp + k, TP)}, device_id_type=MESH
        )
    pl.semaphore_wait(barrier, FSDP - 1 + 16 + TP - 1)


def to_fsdp(src, dst, send, recv, where):
    return pltpu.make_async_remote_copy(
        src_ref=src,
        dst_ref=dst,
        send_sem=send,
        recv_sem=recv,
        device_id={"fsdp": where},
        device_id_type=MESH,
    )


def to_tp(src, dst, send, recv, where):
    return pltpu.make_async_remote_copy(
        src_ref=src,
        dst_ref=dst,
        send_sem=send,
        recv_sem=recv,
        device_id={"tp": where},
        device_id_type=MESH,
    )


def to_side(src, dst, send, recv, where, q):
    return pltpu.make_async_remote_copy(
        src_ref=src,
        dst_ref=dst,
        send_sem=send,
        recv_sem=recv,
        device_id={"fsdp": where, "tp": q},
        device_id_type=MESH,
    )


def nn(a, b):
    return jnp.dot(a, b, preferred_element_type=F32)


def nt(a, b):
    return lax.dot_general(a, b, (((1,), (1,)), ((), ())), preferred_element_type=F32)


def tn(a, b):
    return lax.dot_general(a, b, (((0,), (0,)), ((), ())), preferred_element_type=F32)


def lanes(shape):
    return lax.broadcasted_iota(jnp.int32, shape, len(shape) - 1)


def rows_of(shape):
    return lax.broadcasted_iota(jnp.int32, shape, 0)


def half_swap(v):
    width = v.shape[-1]
    front = lanes(v.shape) % HEAD_SIZE < HEAD_SIZE // 2
    ahead = pltpu.roll(v, width - HEAD_SIZE // 2, 1)
    behind = pltpu.roll(v, HEAD_SIZE // 2, 1)
    return jnp.where(front, -ahead, behind)


def wide_table(table, width):
    return jnp.concatenate([table] * (width // 128), axis=1)


def pick(slot_ref, experts, count):
    parts = []
    for e in experts:
        row = slot_ref[pl.ds(e, 1), :]
        parts.append(jnp.broadcast_to(row, (count, row.shape[1])))
    both = jnp.concatenate(parts, axis=0)
    want = (rows_of(both.shape) % count).astype(F32)
    return (both == want).astype(BF16)


def forward_part(
    query_ref, key_ref, value_ref, out_weight_ref, router_ref, first_gain_ref, second_gain_ref,
    gate_ref, up_ref, down_ref, inputs_ref, seg_ref, routes_ref, cot_ref,
    middle_ref, normed_two_ref, gates_ref, slot_ref, weights_ref, cot_main_ref, cot_spare_ref,
    packed_all_ref, out_all_ref, heads_ref, normed_all_ref, attended_ref, cos_ref, sin_ref,
    packed_ref, blocks_ref, inputs_all, blocks_in, send_main, send_spare, branch_out, branch_in,
    packed_send, packed_recv, outw_send, outw_recv, blocks_send, blocks_recv, main_send, main_recv, spare_send, spare_recv,
    inputs_send, inputs_recv, weights_send, weights_recv, branch_send, branch_recv, own_sem,
):
    me, tp = lax.axis_index("fsdp"), lax.axis_index("tp")
    rows, width = inputs_ref.shape
    total = seg_ref.shape[1]
    packed_ref[...] = jnp.zeros_like(packed_ref)
    packed_ref[:, 0:256] = query_ref[...]
    packed_ref[:, 256:384] = key_ref[...]
    packed_ref[:, 384:512] = value_ref[...]
    packed_ref[:, 512:544] = router_ref[...]
    shard = query_ref.shape[0]
    same_place = rows_of((shard, shard)) == lanes((shard, shard))
    for n, gain_ref in enumerate((first_gain_ref, second_gain_ref)):
        gain = jnp.broadcast_to(gain_ref[...].astype(F32), (shard, shard))
        column = jnp.sum(jnp.where(same_place, gain, 0.0), axis=1, keepdims=True)
        packed_ref[:, 544 + n : 545 + n] = column.astype(BF16)
    greet(me, tp)

    def outw_copy(k):
        return to_fsdp(
            out_weight_ref, out_all_ref.at[me], outw_send.at[k], outw_recv.at[k], peer(me, k)
        )

    def packed_copy(k):
        return to_fsdp(
            packed_ref, packed_all_ref.at[me], packed_send.at[k], packed_recv.at[k], peer(me, k)
        )

    core = lax.rem(tp, 2)
    sibling = tp + 1 - 2 * core
    across = lax.rem(tp + 2, TP)

    def inputs_copy(k):
        block, where = ((tp, across), (tp, sibling), (across, sibling))[k]
        src = inputs_ref if k < 2 else inputs_all.at[block]
        return to_tp(src, inputs_all.at[block], inputs_send.at[k], inputs_recv.at[k], where)

    def blocks_copy(k):
        p = peer(me, k)
        return to_side(
            blocks_ref.at[p], blocks_in.at[me], blocks_send.at[k], blocks_recv.at[k], p, side(tp, k)
        )

    def main_copy(k):
        return to_side(
            send_main.at[k],
            cot_main_ref.at[k],
            main_send.at[k],
            main_recv.at[k],
            peer(me, k),
            side(tp, k),
        )

    def spare_copy(k):
        return to_side(
            send_spare.at[k],
            cot_spare_ref.at[k],
            spare_send.at[k],
            spare_recv.at[k],
            peer(me, k),
            side(tp, k),
        )

    def branch_copy(x):
        return to_tp(
            branch_out.at[2 * x + 1 - core],
            branch_in.at[x],
            branch_send.at[x],
            branch_recv.at[x],
            sibling,
        )

    branch_across = to_tp(
        branch_in.at[2], branch_in.at[3], branch_send.at[2], branch_recv.at[2], across
    )

    inputs_copy(0).start()
    inputs_copy(1).start()
    loop(1, FSDP, lambda k: packed_copy(k).start())
    blocks_ref[:, 0:32, :] = gate_ref[...]
    blocks_ref[:, 32:64, :] = up_ref[...]
    blocks_ref[:, 64:96, :] = down_ref[...]
    loop(1, FSDP, lambda k: outw_copy(k).start())
    loop(1, FSDP, lambda k: blocks_copy(k).start())
    keep = [
        pltpu.make_async_copy(packed_ref, packed_all_ref.at[me], own_sem.at[0]),
        pltpu.make_async_copy(inputs_ref, inputs_all.at[tp], own_sem.at[1]),
        pltpu.make_async_copy(blocks_ref.at[me], blocks_in.at[me], own_sem.at[2]),
        pltpu.make_async_copy(out_weight_ref, out_all_ref.at[me], own_sem.at[4]),
    ]
    for copy in keep:
        copy.start()

    mine = routes_ref[:, pl.ds(pl.multiple_of(tp * rows, rows), rows)]
    at = rows_of((128, rows))
    member_t = jnp.zeros((128, rows), F32)
    for k in range(TOP):
        member_t = member_t + (mine[k : k + 1] == at).astype(F32)
    earlier = (rows_of((rows, rows)) < lanes((rows, rows))).astype(BF16)
    slot = nn(member_t.astype(BF16), earlier)
    slot_ref[...] = jnp.where(member_t > 0, slot, -1.0)[:EXPERTS]
    member = jnp.transpose(member_t)

    def some_rows(i):
        hot = pick(slot_ref, [peer(me, 4 * i + j) for j in range(4)], 40)
        out = nn(hot, cot_ref[...])
        for j in range(4):
            send_main[4 * i + j] = out[40 * j : 40 * j + 32].astype(BF16)
            send_spare[4 * i + j] = out[40 * j + 32 : 40 * j + 33]

        def go(k):
            main_copy(k).start()
            spare_copy(k).start()

        loop(jnp.maximum(4 * i, 1), 4 * i + 4, go)

    loop(0, FSDP // 4, some_rows)
    cot_main_ref[0] = send_main[0]
    cot_spare_ref[0] = send_spare[0]

    seg_row = jnp.broadcast_to(seg_ref[...].astype(F32), (128, total))
    seg_col = jnp.transpose(seg_row)[:, :1]
    same = (seg_col == seg_row[:1]) & (rows_of((total, total)) >= lanes((total, total)))
    allowed = same.astype(F32)
    place = jnp.sum(allowed, axis=1, keepdims=True) - 1.0
    halves = (lanes((1, 128)) % (HEAD_SIZE // 2)).astype(F32)
    rate = jnp.exp(halves * (-2.0 * math.log(ROPE_BASE) / HEAD_SIZE))
    angle = place * rate
    cos_ref[...] = jnp.cos(angle)
    sin_ref[...] = jnp.sin(angle)

    inputs_copy(0).wait_recv()
    inputs_copy(2).start()
    inputs_copy(1).wait_recv()
    inputs_copy(2).wait_recv()
    keep[1].wait()
    wide = inputs_all[...].reshape(total, width).astype(F32)
    inverse = lax.rsqrt(jnp.mean(wide * wide, axis=-1, keepdims=True) + EPSILON)

    loop(1, FSDP, lambda k: packed_copy(k).wait_recv())
    keep[0].wait()
    tail = jnp.transpose(packed_all_ref[:, :, 512:640].reshape(width, 128).astype(F32))
    normed = (wide * inverse * tail[EXPERTS : EXPERTS + 1]).astype(BF16)
    normed_all_ref[...] = normed
    lin = nn(normed, packed_all_ref[:, :, 0:512].reshape(width, 512))
    turn = lin[:, :384]
    turned = turn * wide_table(cos_ref[...], 384) + half_swap(turn) * wide_table(sin_ref[...], 384)
    heads_ref[:, :384] = turned.astype(BF16)
    heads_ref[:, 384:] = lin[:, 384:].astype(BF16)
    outs = []
    for h in range(4):
        g = h // 2
        q = heads_ref[:, 64 * h : 64 * h + 64]
        key = heads_ref[:, 256 + 64 * g : 320 + 64 * g]
        value = heads_ref[:, 384 + 64 * g : 448 + 64 * g]
        scores = jnp.where(allowed > 0, nt(q, key) * HEAD_SIZE ** (-0.5), MASKED)
        top = jnp.max(scores, axis=1, keepdims=True)
        grown = jnp.exp(scores - top)
        shares = (grown * (1.0 / jnp.sum(grown, axis=1, keepdims=True))).astype(BF16)
        outs.append(nn(shares, value))
    attended = jnp.concatenate(outs, axis=1).astype(BF16)
    attended_ref[...] = attended
    loop(1, FSDP, lambda k: outw_copy(k).wait_recv())
    keep[3].wait()
    branch = nt(attended, out_all_ref[...].reshape(width, 256))
    branch_out[...] = branch.astype(BF16).reshape(TP, rows, width)
    for x in range(2):
        branch_copy(x).start()
    for x in range(2):
        branch_copy(x).wait_recv()
    near = tp // 2
    far = 1 - near
    branch_in[2] = (
        branch_out[across].astype(F32) + branch_in[far].astype(F32)
    ).astype(BF16)
    branch_across.start()

    loop(1, FSDP, lambda k: blocks_copy(k).wait_recv())
    keep[2].wait()
    first = to_tp(blocks_in, weights_ref.at[tp], weights_send.at[0], weights_recv.at[0], across)
    second = to_tp(blocks_in, weights_ref.at[tp], weights_send.at[1], weights_recv.at[1], sibling)
    third = to_tp(
        weights_ref.at[across], weights_ref.at[across], weights_send.at[2], weights_recv.at[2], sibling
    )
    first.start()
    second.start()
    mine = pltpu.make_async_copy(blocks_in, weights_ref.at[tp], own_sem.at[3])
    mine.start()

    for x in range(2):
        branch_copy(x).wait_send()
    branch_across.wait_recv()
    middle = inputs_ref[...].astype(F32) + branch_out[tp].astype(F32)
    middle = middle + branch_in[near].astype(F32) + branch_in[3].astype(F32)
    middle_ref[...] = middle
    inverse_two = lax.rsqrt(jnp.mean(middle * middle, axis=-1, keepdims=True) + EPSILON)
    normed_two = (middle * inverse_two * tail[EXPERTS + 1 : EXPERTS + 2]).astype(BF16)
    normed_two_ref[...] = normed_two
    logits = nn(normed_two, packed_all_ref[:, :, 512:640].reshape(width, 128))
    logits = jnp.where(member > 0, logits, MASKED)
    grown = jnp.exp(logits - jnp.max(logits, axis=1, keepdims=True)) * member
    gates_ref[...] = grown / jnp.sum(grown, axis=1, keepdims=True)

    def pass_weights():
        first.wait_recv()
        third.start()

    def weights_ready():
        second.wait_recv()
        third.wait_recv()
        mine.wait()
        for copy in (first, second, third):
            copy.wait_send()

    def cot_ready():
        def got(k):
            main_copy(k).wait_recv()
            spare_copy(k).wait_recv()
            main_copy(k).wait_send()

        loop(1, FSDP, got)

    def sent():
        def gone(k):
            packed_copy(k).wait_send()
            outw_copy(k).wait_send()
            blocks_copy(k).wait_send()
            spare_copy(k).wait_send()

        loop(1, FSDP, gone)
        for k in range(3):
            inputs_copy(k).wait_send()
        branch_across.wait_send()

    return pass_weights, weights_ready, cot_ready, sent


def shape(dims, kind):
    return jax.ShapeDtypeStruct(dims, kind)


def dma(count):
    return pltpu.SemaphoreType.DMA((count,))


def to_column(table, count):
    n = table.shape[0]
    spread = jnp.broadcast_to(table[:, None, :], (n, count, 128)).reshape(n * count, 128)
    mine = lanes(spread.shape) == rows_of(spread.shape) % count
    return jnp.sum(jnp.where(mine, spread, 0.0), axis=1, keepdims=True)


def to_table(column, count):
    n = column.shape[0] // count
    spread = jnp.broadcast_to(column, (n * count, 128))
    mine = lanes(spread.shape) == rows_of(spread.shape) % count
    return jnp.sum(jnp.where(mine, spread, 0.0).reshape(n, count, 128), axis=1)


def expert_part(
    pass_weights, weights_ready, cot_ready, start_pairs,
    normed_two_ref, gates_ref, slot_ref, weights_ref, cot_main_ref, cot_spare_ref,
    middle_ref, cot_ref, packed_all_ref,
    out_main_ref, out_spare_ref, grads_ref, grad_middle_ref, router_part_ref, second_ref,
    hot_main_ref, hot_spare_ref,
    gate_mat, up_mat, down_mat, gate_t, row_send, spare_send, row_in, spare_in,
    back_send, back_spare_send, back_in, back_spare_in,
    hidden_ref, dgate_ref, dup_ref, ghidden_ref, sel_ref, gg_ref,
    out_in, out_spare_in,
    row_s, row_r, spare_s, spare_r, back_s, back_r, bspare_s, bspare_r,
    out_s, out_r, out_spare_s, out_spare_r,
):
    me, tp = lax.axis_index("fsdp"), lax.axis_index("tp")
    half = (me // 4) % 2
    rows, width = normed_two_ref.shape
    main = FSDP * 32

    def row_copy(k):
        return to_side(
            row_send.at[k], row_in.at[k], row_s.at[k], row_r.at[k], peer(me, k), side(tp, k)
        )

    def spare_copy(k):
        return to_side(
            spare_send.at[k], spare_in.at[k], spare_s.at[k], spare_r.at[k], peer(me, k), side(tp, k)
        )

    def back_copy(k):
        return to_side(
            back_send.at[k], back_in.at[k], back_s.at[k], back_r.at[k], giver(me, k), side(tp, k)
        )

    def bspare_copy(k):
        return to_side(
            back_spare_send.at[k],
            back_spare_in.at[k],
            bspare_s.at[k],
            bspare_r.at[k],
            giver(me, k),
            side(tp, k),
        )

    def out_copy(k):
        return to_side(
            out_main_ref.at[k], out_in.at[k], out_s.at[k], out_r.at[k], giver(me, k), side(tp, k)
        )

    def out_spare_copy(k):
        return to_side(
            out_spare_ref.at[k],
            out_spare_in.at[k],
            out_spare_s.at[k],
            out_spare_r.at[k],
            giver(me, k),
            side(tp, k),
        )

    gates_low = gates_ref[...].astype(BF16).astype(F32)
    gate_t[...] = jnp.transpose(gates_low)[:EXPERTS]

    def some_rows(i):
        experts = [peer(me, 4 * i + j) for j in range(4)]
        hot = pick(slot_ref, experts, 40)
        out = nn(hot, normed_two_ref[...])
        for j in range(4):
            k = 4 * i + j
            mine = hot[40 * j : 40 * j + 40].astype(F32)
            column = jnp.sum(mine * gate_t[pl.ds(experts[j], 1), :], axis=1, keepdims=True)
            row_send[k] = out[40 * j : 40 * j + 32].astype(BF16)
            spare_send[k, :, :1024] = out[40 * j + 32 : 40 * j + 33]
            spare_send[k, :, 1024:] = to_table(column, 40)
            hot_main_ref[k] = hot[40 * j : 40 * j + 32]
            hot_spare_ref[pl.ds(k, 1), :] = mine[32:33]

        def go(k):
            row_copy(k).start()
            spare_copy(k).start()

        loop(jnp.maximum(4 * i, 1), 4 * i + 4, go)

    loop(0, FSDP // 4, some_rows)
    row_in[0] = row_send[0]
    spare_in[0] = spare_send[0]

    pass_weights()
    weights_ready()

    def side_by_side(i):
        at = pl.ds(pl.multiple_of(128 * i, 128), 128)
        swap = 2 * lax.rem(half + i, 2)
        for j in range(TP):
            cols = slice(128 * j, 128 * j + 128)
            block = weights_ref[lax.rem(j + swap, TP), pl.ds(4 * i, 4)]
            gate_mat[at, cols] = block[:, 0:32].reshape(128, 128)
            up_mat[at, cols] = block[:, 32:64].reshape(128, 128)
            down_mat[at, cols] = block[:, 64:96].reshape(128, 128)

    loop(0, 8, side_by_side)

    cot_ready()

    def hidden_grads(i):
        cot_rows = cot_main_ref[pl.ds(8 * i, 8)].reshape(256, width)
        ghidden_ref[pl.ds(256 * i, 256), :] = nn(cot_rows, down_mat[...])

    loop(0, 4, hidden_grads)
    cot_spare = cot_spare_ref[...].reshape(FSDP, width).astype(BF16)
    ghidden_ref[pl.ds(main, FSDP), :] = nn(cot_spare, down_mat[...])

    def expert_rows(x, gate, where):
        gate_act = nn(x, gate_mat[...])
        up_act = nn(x, up_mat[...])
        grad_hidden = ghidden_ref[where, :]
        sigmoid_gate = 1.0 / (1.0 + jnp.exp(-gate_act))
        silu_gate = gate_act * sigmoid_gate
        both = silu_gate * up_act
        hidden_ref[where, :] = (both * gate).astype(BF16)
        grad_prod = grad_hidden * gate
        dgate = (
            grad_prod * up_act * sigmoid_gate * (1.0 + gate_act * (1.0 - sigmoid_gate))
        ).astype(BF16)
        dup = (grad_prod * silu_gate).astype(BF16)
        dgate_ref[where, :] = dgate
        dup_ref[where, :] = dup
        grad_in = nt(dgate, gate_mat[...]) + nt(dup, up_mat[...])
        return grad_in, jnp.sum(both * grad_hidden, axis=1, keepdims=True)

    def some_experts(i):
        def got(k):
            row_copy(k).wait_recv()
            spare_copy(k).wait_recv()

        loop(jnp.maximum(8 * i, 1), 8 * i + 8, got)
        x = row_in[pl.ds(8 * i, 8)].reshape(256, width)
        gate = to_column(spare_in[pl.ds(8 * i, 8), :, 1024:].reshape(8, 128), 32)
        grad_in, sel = expert_rows(x, gate, pl.ds(256 * i, 256))
        back_send[pl.ds(8 * i, 8)] = grad_in.astype(BF16).reshape(8, 32, width)
        sel_ref[pl.ds(8 * i, 8), :] = to_table(sel, 32)
        loop(jnp.maximum(8 * i, 1), 8 * i + 8, lambda k: back_copy(k).start())

    loop(0, 4, some_experts)
    spare = spare_in[...].reshape(FSDP, 1152)
    spare_gate = spare[:, 1056:1057]
    spare_rows = spare[:, :1024].astype(BF16)
    grad_in, sel = expert_rows(spare_rows, spare_gate, pl.ds(main, FSDP))
    sel_all = jnp.where(lanes((FSDP, 128)) == 32, sel, sel_ref[...])
    for k in range(FSDP):
        back_spare_send[k, :, :1024] = grad_in[k : k + 1]
        back_spare_send[k, :, 1024:] = sel_all[k : k + 1]
    loop(1, FSDP, lambda k: bspare_copy(k).start())
    back_in[0] = back_send[0]
    back_spare_in[0] = back_spare_send[0]

    loop(1, FSDP, lambda k: row_copy(k).wait_send())

    def outputs(i):
        out = nt(hidden_ref[pl.ds(256 * i, 256), :], down_mat[...])
        out_main_ref[pl.ds(8 * i, 8)] = out.astype(BF16).reshape(8, 32, width)
        loop(jnp.maximum(8 * i, 1), 8 * i + 8, lambda k: out_copy(k).start())

    loop(0, 4, outputs)
    out = nt(hidden_ref[pl.ds(main, FSDP), :], down_mat[...])
    for k in range(FSDP):
        out_spare_ref[k] = out[k : k + 1]
    loop(1, FSDP, lambda k: out_spare_copy(k).start())
    out_in[0] = out_main_ref[0]
    out_spare_in[0] = out_spare_ref[0]

    def weight_grads(i):
        at = pl.ds(pl.multiple_of(256 * i, 256), 256)
        x = row_in[:, :, at].reshape(main, 256)
        x_spare = spare_in[:, :, at].reshape(FSDP, 256).astype(BF16)
        c = cot_main_ref[:, :, at].reshape(main, 256)
        c_spare = cot_spare_ref[:, :, at].reshape(FSDP, 256).astype(BF16)
        for m, (a, a_spare, b) in enumerate(
            ((x, x_spare, dgate_ref), (x, x_spare, dup_ref), (c, c_spare, hidden_ref))
        ):
            part = tn(a, b[pl.ds(0, main), :]) + tn(a_spare, b[pl.ds(main, FSDP), :])
            part = part.astype(BF16)
            for j in range(TP):
                for h in range(2):
                    grads_ref[
                        lax.rem(j + 2 * lax.rem(half + h, 2), TP),
                        pl.ds(8 * i + 4 * h, 4),
                        32 * m : 32 * m + 32,
                        :,
                    ] = part[128 * h : 128 * h + 128, 128 * j : 128 * j + 128].reshape(4, 32, 128)

    loop(0, 4, weight_grads)

    start_pairs()

    def back_got(k):
        back_copy(k).wait_recv()
        bspare_copy(k).wait_recv()

    loop(1, FSDP, back_got)
    hot = hot_main_ref[...].reshape(main, rows)
    hot_spare = hot_spare_ref[...]
    back_spare = back_spare_in[...].reshape(FSDP, 1152)
    grad_rows = tn(hot, back_in[...].reshape(main, width)) + tn(
        hot_spare.astype(BF16), back_spare[:, :1024].astype(BF16)
    )
    sel = back_spare[:, 1024:]
    by_slot = jnp.sum(
        (hot.astype(F32) * to_column(sel, 32)).reshape(FSDP, 32, rows), axis=1
    ) + hot_spare * sel[:, 32:33]
    gg_ref[...] = jnp.zeros_like(gg_ref)
    for k in range(FSDP):
        gg_ref[pl.ds(peer(me, k), 1), :] = by_slot[k : k + 1]
    grad_gates = jnp.transpose(gg_ref[...])
    gates = gates_ref[...]
    grad_chosen = gates * (grad_gates - jnp.sum(gates * grad_gates, axis=1, keepdims=True))
    grad_logits = grad_chosen.astype(BF16)
    tail = packed_all_ref[:, :, 512:640].reshape(width, 128)
    gain_two = jnp.transpose(tail.astype(F32))[EXPERTS + 1 : EXPERTS + 2]
    router_part_ref[...] = tn(normed_two_ref[...], grad_logits)
    dy = grad_rows + nt(grad_logits, tail)
    middle = middle_ref[...]
    inverse = lax.rsqrt(jnp.mean(middle * middle, axis=-1, keepdims=True) + EPSILON)
    scaled = dy * gain_two
    second_ref[...] = jnp.sum(dy * middle * inverse, axis=0, keepdims=True)
    grad_middle_ref[...] = (
        cot_ref[...].astype(F32)
        + inverse * scaled
        - middle
        * inverse
        * inverse
        * inverse
        * jnp.mean(scaled * middle, axis=-1, keepdims=True)
    )

    def out_ready():
        def got(k):
            out_copy(k).wait_recv()
            out_spare_copy(k).wait_recv()

        loop(1, FSDP, got)

    def sent():
        def gone(k):
            spare_copy(k).wait_send()
            back_copy(k).wait_send()
            bspare_copy(k).wait_send()
            out_copy(k).wait_send()
            out_spare_copy(k).wait_send()

        loop(1, FSDP, gone)

    return out_ready, sent


def backward_part(
    out_ready, pair_copy, packed_ref,
    grad_middle_ref, packed_all_ref, out_all_ref, heads_ref, normed_all_ref, attended_ref,
    cos_ref, sin_ref,
    seg_ref, grads_ref, middle_ref, hot_main_ref, hot_spare_ref,
    inputs_ref, router_part_ref, second_ref,
    output_ref, grad_inputs_ref, sums_ref, out_sums_ref, dw_in,
    branch_own, branch_all, out_in, out_spare_in, pair_in, across_send, across_in, dw_send,
    normed_send, normed_in, sums_send, sums_in, outs_send, outs_in, small_own, small_in,
    branch_s, branch_r, across_s, across_r,
    dw_s, dw_r, normed_s, normed_r, sums_s, sums_r, outs_s, outs_r, small_s, small_r,
):
    me, tp = lax.axis_index("fsdp"), lax.axis_index("tp")
    rows, width = inputs_ref.shape
    total = seg_ref.shape[1]
    core = lax.rem(tp, 2)
    sibling = tp + 1 - 2 * core
    across = lax.rem(tp + 2, TP)

    def branch_copy(k):
        block, where = ((tp, across), (tp, sibling), (across, sibling))[k]
        src = branch_own if k < 2 else branch_all.at[block]
        return to_tp(src, branch_all.at[block], branch_s.at[k], branch_r.at[k], where)

    across_copy = to_tp(across_send, across_in, across_s.at[0], across_r.at[0], across)

    def dw_copy(k):
        p = peer(me, k)
        return to_side(dw_send.at[p], dw_in.at[me], dw_s.at[k], dw_r.at[k], p, side(tp, k))

    def normed_copy(x):
        return to_tp(
            normed_send.at[2 * x + 1 - core],
            normed_in.at[x],
            normed_s.at[x],
            normed_r.at[x],
            sibling,
        )

    normed_across = to_tp(
        normed_in.at[2], normed_in.at[3], normed_s.at[2], normed_r.at[2], across
    )

    def sums_copy(k):
        p = peer(me, k)
        return to_fsdp(sums_send.at[p], sums_in.at[k], sums_s.at[k], sums_r.at[k], p)

    def outs_copy(k):
        p = peer(me, k)
        return to_fsdp(outs_send.at[p], outs_in.at[k], outs_s.at[k], outs_r.at[k], p)

    def small_copy(k):
        return to_tp(small_own, small_in.at[k], small_s.at[k], small_r.at[k], lax.rem(tp + k, TP))

    grad_middle = grad_middle_ref[...]
    branch_own[...] = grad_middle.astype(BF16)
    branch_copy(0).start()
    branch_copy(1).start()
    branch_all[tp] = branch_own[...]
    branch_copy(0).wait_recv()
    branch_copy(2).start()

    for x in range(2):
        pair_copy(x).wait_recv()
    near = tp // 2
    far = 1 - near
    across_send[...] = (
        grads_ref[2 * far + core].astype(F32) + pair_in[far].astype(F32)
    ).astype(BF16)
    across_copy.start()

    seg_row = jnp.broadcast_to(seg_ref[...].astype(F32), (128, total))
    seg_col = jnp.transpose(seg_row)[:, :1]
    allowed = (
        (seg_col == seg_row[:1]) & (rows_of((total, total)) >= lanes((total, total)))
    ).astype(F32)

    branch_copy(1).wait_recv()
    branch_copy(2).wait_recv()
    branch = branch_all[...].reshape(total, width)
    out_part = tn(branch, attended_ref[...])
    outs_send[:, :, 0:256] = out_part.astype(BF16).reshape(FSDP, 32, 256)
    second = jnp.where(rows_of((128, width)) == EXPERTS + 1, second_ref[...], 0.0)
    small = router_part_ref[...] + jnp.transpose(second)
    outs_send[:, :, 256:384] = small.astype(BF16).reshape(FSDP, 32, 128)
    loop(1, FSDP, lambda k: outs_copy(k).start())
    outs_in[0] = outs_send[me]
    grad_attended = nn(branch, out_all_ref[...].reshape(width, 256)).astype(BF16)
    scale = HEAD_SIZE ** (-0.5)
    dq, dk, dv = [], [], []
    for g in range(2):
        key = heads_ref[:, 256 + 64 * g : 320 + 64 * g]
        value = heads_ref[:, 384 + 64 * g : 448 + 64 * g]
        dk_sum, dv_sum = None, None
        for h in (2 * g, 2 * g + 1):
            q = heads_ref[:, 64 * h : 64 * h + 64]
            da = grad_attended[:, 64 * h : 64 * h + 64]
            scores = jnp.where(allowed > 0, nt(q, key) * scale, MASKED)
            top = jnp.max(scores, axis=1, keepdims=True)
            grown = jnp.exp(scores - top)
            whole = grown * (1.0 / jnp.sum(grown, axis=1, keepdims=True))
            grad_shares = nt(da, value)
            inner = jnp.sum(whole * grad_shares, axis=1, keepdims=True)
            grad_scores = (whole * (grad_shares - inner)).astype(BF16)
            dq.append(nn(grad_scores, key) * scale)
            dk_one = tn(grad_scores, q) * scale
            dv_one = tn(whole.astype(BF16), da)
            dk_sum = dk_one if dk_sum is None else dk_sum + dk_one
            dv_sum = dv_one if dv_sum is None else dv_sum + dv_one
        dk.append(dk_sum)
        dv.append(dv_sum)
        if g > 0:
            continue
        across_copy.wait_recv()
        dw_send[...] = (
            grads_ref[tp].astype(F32) + pair_in[near].astype(F32) + across_in[...].astype(F32)
        ).astype(BF16)
        loop(1, FSDP, lambda k: dw_copy(k).start())
        dw_in[me] = dw_send[me]
    turned = jnp.concatenate(dq + dk, axis=1)
    turn = turned * wide_table(cos_ref[...], 384) - half_swap(turned) * wide_table(
        sin_ref[...], 384
    )
    grad_lin = jnp.concatenate([turn] + dv, axis=1).astype(BF16)
    qkv_part = tn(normed_all_ref[...], grad_lin)
    sums_send[...] = qkv_part.astype(BF16).reshape(FSDP, 32, 512)
    loop(1, FSDP, lambda k: sums_copy(k).start())
    sums_in[0] = sums_send[me]

    grad_normed = nt(grad_lin, packed_all_ref[:, :, 0:512].reshape(width, 512))
    normed_send[...] = grad_normed.astype(BF16).reshape(TP, rows, width)
    for x in range(2):
        normed_copy(x).start()
    gain_one = jnp.transpose(packed_all_ref[:, :, 512:640].reshape(width, 128).astype(F32))[
        EXPERTS : EXPERTS + 1
    ]
    for x in range(2):
        normed_copy(x).wait_recv()
    normed_in[2] = (
        normed_send[across].astype(F32) + normed_in[far].astype(F32)
    ).astype(BF16)
    normed_across.start()

    normed_across.wait_recv()
    dy = normed_send[tp].astype(F32) + normed_in[near].astype(F32) + normed_in[3].astype(F32)
    wide = inputs_ref[...].astype(F32)
    inverse = lax.rsqrt(jnp.mean(wide * wide, axis=-1, keepdims=True) + EPSILON)
    scaled = dy * gain_one
    grad_inputs_ref[...] = (
        grad_middle
        + inverse * scaled
        - wide
        * inverse
        * inverse
        * inverse
        * jnp.mean(scaled * wide, axis=-1, keepdims=True)
    )

    out_ready()
    hot = hot_main_ref[...].reshape(FSDP * 32, rows)
    output_ref[...] = (
        middle_ref[...]
        + tn(hot, out_in[...].reshape(FSDP * 32, width))
        + tn(hot_spare_ref[...].astype(BF16), out_spare_in[...].reshape(FSDP, width).astype(BF16))
    ).astype(BF16)

    loop(1, FSDP, lambda k: sums_copy(k).wait_recv())
    sums = jnp.sum(sums_in[...].astype(F32), axis=0)
    sums_ref[:, :512] = sums
    loop(1, FSDP, lambda k: outs_copy(k).wait_recv())
    out_sums = jnp.sum(outs_in[...].astype(F32), axis=0)
    out_sums_ref[...] = out_sums[:, :256]
    first = jnp.sum(packed_ref[:, :512].astype(F32) * sums, axis=1, keepdims=True)
    first = first / packed_ref[:, 544:545].astype(F32)
    small_own[...] = out_sums[:, 256:] + jnp.where(lanes((32, 128)) == EXPERTS, first, 0.0)
    for k in (2, 1, 3):
        small_copy(k).start()
    loop(1, FSDP, lambda k: dw_copy(k).wait_recv())
    for k in range(1, TP):
        small_copy(k).wait_recv()
    sums_ref[:, 512:] = small_own[...] + small_in[1] + small_in[2] + small_in[3]

    def gone(k):
        sums_copy(k).wait_send()
        outs_copy(k).wait_send()
        dw_copy(k).wait_send()

    loop(1, FSDP, gone)
    for k in range(3):
        branch_copy(k).wait_send()
        small_copy(k + 1).wait_send()
    for x in range(2):
        normed_copy(x).wait_send()
        pair_copy(x).wait_send()
    normed_across.wait_send()
    across_copy.wait_send()


def layer_kernel(
    query_ref, key_ref, value_ref, out_weight_ref, router_ref, first_gain_ref, second_gain_ref,
    gate_ref, up_ref, down_ref, inputs_ref, seg_ref, routes_ref, cot_ref,
    output_ref, grad_inputs_ref, sums_ref, out_sums_ref, weight_grads_ref,
    middle, normed_two, gates, slot, weights, cot_main, cot_spare, packed_all, out_all,
    heads, normed_all, attended, cosine, sine,
    packed, blocks, inputs_all, blocks_in, rows_out, spare_out, branch_out, branch_in,
    router_part, second_part, hot_main, hot_spare, grad_middle, out_spare,
    gate_mat, up_mat, down_mat, gate_t, row_send, spare_send, row_in, spare_in,
    back_spare_send, back_in, back_spare_in,
    hidden, dgate, dup, ghidden, sel, gate_grads, out_in, out_spare_in,
    branch_own, branch_all, pair_in, across_send, across_in, dw_send, normed_in,
    sums_send, sums_in, outs_send, outs_in, small_own, small_in,
    *sems,
):
    tp = lax.axis_index("tp")
    sems = list(sems)

    def take(count):
        taken = sems[:count]
        del sems[:count]
        return taken

    pass_weights, weights_ready, cot_ready, forward_sent = forward_part(
        query_ref, key_ref, value_ref, out_weight_ref, router_ref, first_gain_ref,
        second_gain_ref, gate_ref, up_ref, down_ref, inputs_ref, seg_ref, routes_ref, cot_ref,
        middle, normed_two, gates, slot, weights, cot_main, cot_spare,
        packed_all, out_all, heads, normed_all, attended, cosine, sine,
        packed, blocks, inputs_all, blocks_in, rows_out, spare_out, branch_out, branch_in,
        *take(17),
    )
    core = lax.rem(tp, 2)
    pair_s, pair_r = take(2)

    def pair_copy(x):
        return to_tp(
            weights.at[2 * x + 1 - core],
            pair_in.at[x],
            pair_s.at[x],
            pair_r.at[x],
            tp + 1 - 2 * core,
        )

    def start_pairs():
        for x in range(2):
            pair_copy(x).start()

    out_ready, expert_sent = expert_part(
        pass_weights, weights_ready, cot_ready, start_pairs,
        normed_two, gates, slot, weights, cot_main, cot_spare, middle, cot_ref,
        packed_all,
        row_send, out_spare, weights, grad_middle, router_part, second_part, hot_main, hot_spare,
        gate_mat, up_mat, down_mat, gate_t, row_send, spare_send, row_in, spare_in,
        rows_out, back_spare_send, back_in, back_spare_in,
        hidden, dgate, dup, ghidden, sel, gate_grads, out_in, out_spare_in,
        *take(12),
    )
    backward_part(
        out_ready, pair_copy, packed,
        grad_middle, packed_all, out_all, heads, normed_all, attended, cosine, sine, seg_ref,
        weights, middle, hot_main, hot_spare, inputs_ref, router_part, second_part,
        output_ref, grad_inputs_ref, sums_ref, out_sums_ref, weight_grads_ref,
        branch_own, branch_all, out_in, out_spare_in, pair_in, across_send, across_in,
        dw_send, branch_out, normed_in, sums_send, sums_in, outs_send, outs_in,
        small_own, small_in,
        *take(14),
    )
    forward_sent()
    expert_sent()


def layer(*operands):
    inputs, seg = operands[10], operands[11]
    rows, width = inputs.shape
    total = seg.shape[1]
    packed_shape, out_shape, blocks_shape = (32, 640), (32, 256), (EXPERTS, 96, 128)
    hidden = 128 * TP
    slots = FSDP * SPARE
    vmem = pl.BlockSpec(memory_space=pltpu.VMEM)
    out = (
        shape((rows, width), BF16),
        shape((rows, width), F32),
        shape(packed_shape, F32),
        shape(out_shape, F32),
        shape(blocks_shape, BF16),
    )
    block = pltpu.VMEM((FSDP, 32, width), BF16)
    spare = pltpu.VMEM((FSDP, 1, width), F32)
    spare_wide = pltpu.VMEM((FSDP, 1, width + 128), F32)
    four = pltpu.VMEM((TP, rows, width), BF16)
    shards = pltpu.VMEM(blocks_shape, BF16)
    packs = pltpu.VMEM((FSDP, *packed_shape), BF16)
    outs = pltpu.VMEM((FSDP, *out_shape), BF16)
    return pl.pallas_call(
        layer_kernel,
        out_shape=out,
        in_specs=[vmem] * len(operands),
        out_specs=[vmem] * len(out),
        scratch_shapes=[
            pltpu.VMEM((rows, width), F32),
            pltpu.VMEM((rows, width), BF16),
            pltpu.VMEM((rows, 128), F32),
            pltpu.VMEM((EXPERTS, rows), F32),
            pltpu.VMEM((TP, *blocks_shape), BF16),
            block,
            spare,
            packs,
            outs,
            pltpu.VMEM((total, 512), BF16),
            pltpu.VMEM((total, width), BF16),
            pltpu.VMEM((total, 256), BF16),
            pltpu.VMEM((total, 128), F32),
            pltpu.VMEM((total, 128), F32),
            pltpu.VMEM(packed_shape, BF16),
            shards,
            four,
            shards,
            block,
            spare,
            four,
            four,
            pltpu.VMEM((width, 128), F32),
            pltpu.VMEM((1, width), F32),
            pltpu.VMEM((FSDP, 32, rows), BF16),
            pltpu.VMEM((FSDP, rows), F32),
            pltpu.VMEM((rows, width), F32),
            spare,
            *[pltpu.VMEM((width, hidden), BF16)] * 3,
            pltpu.VMEM((EXPERTS, rows), F32),
            block,
            spare_wide,
            block,
            spare_wide,
            spare_wide,
            block,
            spare_wide,
            *[pltpu.VMEM((slots, hidden), BF16)] * 3,
            pltpu.VMEM((slots, hidden), F32),
            pltpu.VMEM((FSDP, 128), F32),
            pltpu.VMEM((128, 128), F32),
            block,
            spare,
            pltpu.VMEM((rows, width), BF16),
            four,
            pltpu.VMEM((2, *blocks_shape), BF16),
            *[shards] * 3,
            four,
            *[pltpu.VMEM((FSDP, 32, 512), BF16)] * 2,
            *[pltpu.VMEM((FSDP, 32, 384), BF16)] * 2,
            pltpu.VMEM((32, 128), F32),
            pltpu.VMEM((TP, 32, 128), F32),
            *[dma(FSDP)] * 10,
            *[dma(TP)] * 6,
            dma(5),
            *[dma(2)] * 2,
            *[dma(FSDP)] * 12,
            *[dma(TP)] * 2,
            *[dma(1)] * 2,
            *[dma(FSDP)] * 2,
            *[dma(TP)] * 2,
            *[dma(FSDP)] * 4,
            *[dma(TP)] * 2,
        ],
        compiler_params=pltpu.CompilerParams(
            collective_id=1, has_side_effects=True, vmem_limit_bytes=62 * 2**20
        ),
        name="layer",
    )(*operands)


def finish_kernel(
    output_in, grad_inputs_in, sums_ref, out_sums_ref, weight_grads_ref,
    output_ref, grad_inputs_ref, query_ref, key_ref, value_ref, out_ref, router_ref,
    gains_ref, gate_ref, up_ref, down_ref,
):
    output_ref[...] = output_in[...]
    grad_inputs_ref[...] = grad_inputs_in[...]
    query_ref[...] = sums_ref[:, 0:256]
    key_ref[...] = sums_ref[:, 256:384]
    value_ref[...] = sums_ref[:, 384:512]
    out_ref[...] = out_sums_ref[...]
    router_ref[...] = sums_ref[:, 512:544]
    tail = jnp.concatenate([sums_ref[:, 512:640], jnp.zeros((96, 128), F32)], axis=0)
    gains_ref[...] = jnp.transpose(tail)[EXPERTS : EXPERTS + 8, :32]
    gate_ref[...] = weight_grads_ref[:, 0:32].astype(F32)
    up_ref[...] = weight_grads_ref[:, 32:64].astype(F32)
    down_ref[...] = weight_grads_ref[:, 64:96].astype(F32)


def finish(*operands):
    vmem = pl.BlockSpec(memory_space=pltpu.VMEM)
    shard = shape((EXPERTS, 32, 128), F32)
    out = (
        shape(operands[0].shape, BF16),
        shape(operands[1].shape, F32),
        shape((32, 256), F32),
        shape((32, 128), F32),
        shape((32, 128), F32),
        shape((32, 256), F32),
        shape((32, 32), F32),
        shape((8, 32), F32),
        shard,
        shard,
        shard,
    )
    return pl.pallas_call(
        finish_kernel,
        out_shape=out,
        in_specs=[vmem] * len(operands),
        out_specs=[vmem] * len(out),
        compiler_params=pltpu.CompilerParams(vmem_limit_bytes=60 * 2**20),
        name="finish",
    )(*operands)


def per_device(
    inputs,
    segments,
    routes,
    query_weight,
    key_projection_weight,
    value_projection_weight,
    out_weight,
    router_weight,
    first_gain,
    second_gain,
    gate_weight,
    up_weight,
    down_weight,
    cotangent,
):
    parts = layer(
        query_weight,
        key_projection_weight,
        value_projection_weight,
        out_weight.T,
        router_weight,
        first_gain[None, :],
        second_gain[None, :],
        gate_weight,
        up_weight,
        jnp.transpose(down_weight, (0, 2, 1)),
        inputs,
        segments,
        routes.T,
        cotangent,
    )
    (
        output, grad_inputs, grad_query, grad_key, grad_value, grad_out, grad_router,
        grad_gains, grad_gate, grad_up, grad_down,
    ) = finish(*parts)
    return (
        output,
        grad_inputs,
        grad_query,
        grad_key,
        grad_value,
        grad_out.T,
        grad_router,
        grad_gains[0],
        grad_gains[1],
        grad_gate,
        grad_up,
        jnp.transpose(grad_down, (0, 2, 1)),
    )


def solution(mesh):
    return jax.shard_map(
        per_device,
        mesh=mesh,
        in_specs=(
            P(("fsdp", "tp"), None),
            P("fsdp", None),
            P("fsdp", None),
            P("fsdp", "tp"),
            P("fsdp", "tp"),
            P("fsdp", "tp"),
            P("tp", "fsdp"),
            P("fsdp", None),
            P("fsdp"),
            P("fsdp"),
            P(None, "fsdp", "tp"),
            P(None, "fsdp", "tp"),
            P(None, "tp", "fsdp"),
            P(("fsdp", "tp"), None),
        ),
        out_specs=(
            P(("fsdp", "tp"), None),
            P(("fsdp", "tp"), None),
            P("fsdp", "tp"),
            P("fsdp", "tp"),
            P("fsdp", "tp"),
            P("tp", "fsdp"),
            P("fsdp", None),
            P("fsdp"),
            P("fsdp"),
            P(None, "fsdp", "tp"),
            P(None, "fsdp", "tp"),
            P(None, "tp", "fsdp"),
        ),
        check_vma=False,
    )
```

```python
import math

import jax
import jax.numpy as jnp
from jax import lax
from jax.experimental import pallas as pl
from jax.experimental.pallas import tpu as pltpu
from jax.sharding import PartitionSpec as P

HEAD_SIZE = 64
EXPERTS = 32
TOP = 8


EPSILON = 1e-06
ROPE_BASE = 10000.0
MASKED = -1e30


MESH = pl.DeviceIdType.MESH
FSDP, TP, SPARE = 32, 4, 33
F32, BF16 = jnp.float32, jnp.bfloat16


def offset(k):
    a, b, c = k % 4, (k // 4) % 4, k // 16
    return a, (b + c) % 2, (a + b) % 4


def peer(me, k):
    dz, dx, dy = offset(k)
    z, x, y = me // 8, (me // 4) % 2, me % 4
    return ((z + dz) % 4 * 2 + (x + dx) % 2) * 4 + (y + dy) % 4


def giver(me, k):
    dz, dx, dy = offset(k)
    z, x, y = me // 8, (me // 4) % 2, me % 4
    return ((z + 4 - dz) % 4 * 2 + (x + dx) % 2) * 4 + (y + 4 - dy) % 4


def side(tp, k):
    return lax.rem(tp + 2 * offset(k)[1], TP)


def loop(low, high, step):
    def body(k, carry):
        step(k)
        return carry

    lax.fori_loop(low, high, body, 0)


def greet(me, tp):
    barrier = pltpu.get_barrier_semaphore()

    def signal(k, q):
        pl.semaphore_signal(
            barrier, inc=1, device_id={"fsdp": peer(me, k), "tp": q}, device_id_type=MESH
        )

    loop(1, FSDP, lambda k: signal(k, tp))
    loop(0, 16, lambda n: signal(n + 16 * ((n // 4 + 1) % 2), lax.rem(tp + 2, TP)))
    for k in range(1, TP):
        pl.semaphore_signal(
            barrier, inc=1, device_id={"tp": lax.rem(tp + k, TP)}, device_id_type=MESH
        )
    pl.semaphore_wait(barrier, FSDP - 1 + 16 + TP - 1)


def to_fsdp(src, dst, send, recv, where):
    return pltpu.make_async_remote_copy(
        src_ref=src,
        dst_ref=dst,
        send_sem=send,
        recv_sem=recv,
        device_id={"fsdp": where},
        device_id_type=MESH,
    )


def to_tp(src, dst, send, recv, where):
    return pltpu.make_async_remote_copy(
        src_ref=src,
        dst_ref=dst,
        send_sem=send,
        recv_sem=recv,
        device_id={"tp": where},
        device_id_type=MESH,
    )


def to_side(src, dst, send, recv, where, q):
    return pltpu.make_async_remote_copy(
        src_ref=src,
        dst_ref=dst,
        send_sem=send,
        recv_sem=recv,
        device_id={"fsdp": where, "tp": q},
        device_id_type=MESH,
    )


def nn(a, b):
    return jnp.dot(a, b, preferred_element_type=F32)


def nt(a, b):
    return lax.dot_general(a, b, (((1,), (1,)), ((), ())), preferred_element_type=F32)


def tn(a, b):
    return lax.dot_general(a, b, (((0,), (0,)), ((), ())), preferred_element_type=F32)


def lanes(shape):
    return lax.broadcasted_iota(jnp.int32, shape, len(shape) - 1)


def rows_of(shape):
    return lax.broadcasted_iota(jnp.int32, shape, 0)


def half_swap(v):
    width = v.shape[-1]
    front = lanes(v.shape) % HEAD_SIZE < HEAD_SIZE // 2
    ahead = pltpu.roll(v, width - HEAD_SIZE // 2, 1)
    behind = pltpu.roll(v, HEAD_SIZE // 2, 1)
    return jnp.where(front, -ahead, behind)


def wide_table(table, width):
    return jnp.concatenate([table] * (width // 128), axis=1)


def pick(slot_ref, experts, count):
    parts = []
    for e in experts:
        row = slot_ref[pl.ds(e, 1), :]
        parts.append(jnp.broadcast_to(row, (count, row.shape[1])))
    both = jnp.concatenate(parts, axis=0)
    want = (rows_of(both.shape) % count).astype(F32)
    return (both == want).astype(BF16)


def forward_part(
    query_ref, key_ref, value_ref, out_weight_ref, router_ref, first_gain_ref, second_gain_ref,
    gate_ref, up_ref, down_ref, inputs_ref, seg_ref, routes_ref, cot_ref,
    middle_ref, normed_two_ref, gates_ref, slot_ref, weights_ref, cot_main_ref, cot_spare_ref,
    packed_all_ref, out_all_ref, heads_ref, normed_all_ref, attended_ref, cos_ref, sin_ref,
    packed_ref, blocks_ref, inputs_all, blocks_in, send_main, send_spare, branch_out, branch_in,
    packed_send, packed_recv, outw_send, outw_recv, blocks_send, blocks_recv, main_send, main_recv, spare_send, spare_recv,
    inputs_send, inputs_recv, weights_send, weights_recv, branch_send, branch_recv, own_sem,
):
    me, tp = lax.axis_index("fsdp"), lax.axis_index("tp")
    rows, width = inputs_ref.shape
    total = seg_ref.shape[1]
    packed_ref[...] = jnp.zeros_like(packed_ref)
    packed_ref[:, 0:256] = query_ref[...]
    packed_ref[:, 256:384] = key_ref[...]
    packed_ref[:, 384:512] = value_ref[...]
    packed_ref[:, 512:544] = router_ref[...]
    shard = query_ref.shape[0]
    same_place = rows_of((shard, shard)) == lanes((shard, shard))
    for n, gain_ref in enumerate((first_gain_ref, second_gain_ref)):
        gain = jnp.broadcast_to(gain_ref[...].astype(F32), (shard, shard))
        column = jnp.sum(jnp.where(same_place, gain, 0.0), axis=1, keepdims=True)
        packed_ref[:, 544 + n : 545 + n] = column.astype(BF16)
    greet(me, tp)

    def outw_copy(k):
        return to_fsdp(
            out_weight_ref, out_all_ref.at[me], outw_send.at[k], outw_recv.at[k], peer(me, k)
        )

    def packed_copy(k):
        return to_fsdp(
            packed_ref, packed_all_ref.at[me], packed_send.at[k], packed_recv.at[k], peer(me, k)
        )

    core = lax.rem(tp, 2)
    sibling = tp + 1 - 2 * core
    across = lax.rem(tp + 2, TP)

    def inputs_copy(k):
        block, where = ((tp, across), (tp, sibling), (across, sibling))[k]
        src = inputs_ref if k < 2 else inputs_all.at[block]
        return to_tp(src, inputs_all.at[block], inputs_send.at[k], inputs_recv.at[k], where)

    def blocks_copy(k):
        p = peer(me, k)
        return to_side(
            blocks_ref.at[p], blocks_in.at[me], blocks_send.at[k], blocks_recv.at[k], p, side(tp, k)
        )

    def main_copy(k):
        return to_side(
            send_main.at[k],
            cot_main_ref.at[k],
            main_send.at[k],
            main_recv.at[k],
            peer(me, k),
            side(tp, k),
        )

    def spare_copy(k):
        return to_side(
            send_spare.at[k],
            cot_spare_ref.at[k],
            spare_send.at[k],
            spare_recv.at[k],
            peer(me, k),
            side(tp, k),
        )

    def branch_copy(x):
        return to_tp(
            branch_out.at[2 * x + 1 - core],
            branch_in.at[x],
            branch_send.at[x],
            branch_recv.at[x],
            sibling,
        )

    branch_across = to_tp(
        branch_in.at[2], branch_in.at[3], branch_send.at[2], branch_recv.at[2], across
    )

    inputs_copy(0).start()
    inputs_copy(1).start()
    loop(1, FSDP, lambda k: packed_copy(k).start())
    blocks_ref[:, 0:32, :] = gate_ref[...]
    blocks_ref[:, 32:64, :] = up_ref[...]
    blocks_ref[:, 64:96, :] = down_ref[...]
    loop(1, FSDP, lambda k: outw_copy(k).start())
    loop(1, FSDP, lambda k: blocks_copy(k).start())
    keep = [
        pltpu.make_async_copy(packed_ref, packed_all_ref.at[me], own_sem.at[0]),
        pltpu.make_async_copy(inputs_ref, inputs_all.at[tp], own_sem.at[1]),
        pltpu.make_async_copy(blocks_ref.at[me], blocks_in.at[me], own_sem.at[2]),
        pltpu.make_async_copy(out_weight_ref, out_all_ref.at[me], own_sem.at[4]),
    ]
    for copy in keep:
        copy.start()

    mine = routes_ref[:, pl.ds(pl.multiple_of(tp * rows, rows), rows)]
    at = rows_of((128, rows))
    member_t = jnp.zeros((128, rows), F32)
    for k in range(TOP):
        member_t = member_t + (mine[k : k + 1] == at).astype(F32)
    earlier = (rows_of((rows, rows)) < lanes((rows, rows))).astype(BF16)
    slot = nn(member_t.astype(BF16), earlier)
    slot_ref[...] = jnp.where(member_t > 0, slot, -1.0)[:EXPERTS]
    member = jnp.transpose(member_t)

    def some_rows(i):
        hot = pick(slot_ref, [peer(me, 4 * i + j) for j in range(4)], 40)
        out = nn(hot, cot_ref[...])
        for j in range(4):
            send_main[4 * i + j] = out[40 * j : 40 * j + 32].astype(BF16)
            send_spare[4 * i + j] = out[40 * j + 32 : 40 * j + 33]

        def go(k):
            main_copy(k).start()
            spare_copy(k).start()

        loop(jnp.maximum(4 * i, 1), 4 * i + 4, go)

    loop(0, FSDP // 4, some_rows)
    cot_main_ref[0] = send_main[0]
    cot_spare_ref[0] = send_spare[0]

    seg_row = jnp.broadcast_to(seg_ref[...].astype(F32), (128, total))
    seg_col = jnp.transpose(seg_row)[:, :1]
    same = (seg_col == seg_row[:1]) & (rows_of((total, total)) >= lanes((total, total)))
    allowed = same.astype(F32)
    place = jnp.sum(allowed, axis=1, keepdims=True) - 1.0
    halves = (lanes((1, 128)) % (HEAD_SIZE // 2)).astype(F32)
    rate = jnp.exp(halves * (-2.0 * math.log(ROPE_BASE) / HEAD_SIZE))
    angle = place * rate
    cos_ref[...] = jnp.cos(angle)
    sin_ref[...] = jnp.sin(angle)

    inputs_copy(0).wait_recv()
    inputs_copy(2).start()
    inputs_copy(1).wait_recv()
    inputs_copy(2).wait_recv()
    keep[1].wait()
    wide = inputs_all[...].reshape(total, width).astype(F32)
    inverse = lax.rsqrt(jnp.mean(wide * wide, axis=-1, keepdims=True) + EPSILON)

    loop(1, FSDP, lambda k: packed_copy(k).wait_recv())
    keep[0].wait()
    tail = jnp.transpose(packed_all_ref[:, :, 512:640].reshape(width, 128).astype(F32))
    normed = (wide * inverse * tail[EXPERTS : EXPERTS + 1]).astype(BF16)
    normed_all_ref[...] = normed
    lin = nn(normed, packed_all_ref[:, :, 0:512].reshape(width, 512))
    turn = lin[:, :384]
    turned = turn * wide_table(cos_ref[...], 384) + half_swap(turn) * wide_table(sin_ref[...], 384)
    heads_ref[:, :384] = turned.astype(BF16)
    heads_ref[:, 384:] = lin[:, 384:].astype(BF16)
    outs = []
    for h in range(4):
        g = h // 2
        q = heads_ref[:, 64 * h : 64 * h + 64]
        key = heads_ref[:, 256 + 64 * g : 320 + 64 * g]
        value = heads_ref[:, 384 + 64 * g : 448 + 64 * g]
        scores = jnp.where(allowed > 0, nt(q, key) * HEAD_SIZE ** (-0.5), MASKED)
        top = jnp.max(scores, axis=1, keepdims=True)
        grown = jnp.exp(scores - top)
        shares = (grown * (1.0 / jnp.sum(grown, axis=1, keepdims=True))).astype(BF16)
        outs.append(nn(shares, value))
    attended = jnp.concatenate(outs, axis=1).astype(BF16)
    attended_ref[...] = attended
    loop(1, FSDP, lambda k: outw_copy(k).wait_recv())
    keep[3].wait()
    branch = nt(attended, out_all_ref[...].reshape(width, 256))
    branch_out[...] = branch.astype(BF16).reshape(TP, rows, width)
    for x in range(2):
        branch_copy(x).start()
    for x in range(2):
        branch_copy(x).wait_recv()
    near = tp // 2
    far = 1 - near
    branch_in[2] = (
        branch_out[across].astype(F32) + branch_in[far].astype(F32)
    ).astype(BF16)
    branch_across.start()

    loop(1, FSDP, lambda k: blocks_copy(k).wait_recv())
    keep[2].wait()
    first = to_tp(blocks_in, weights_ref.at[tp], weights_send.at[0], weights_recv.at[0], across)
    second = to_tp(blocks_in, weights_ref.at[tp], weights_send.at[1], weights_recv.at[1], sibling)
    third = to_tp(
        weights_ref.at[across], weights_ref.at[across], weights_send.at[2], weights_recv.at[2], sibling
    )
    first.start()
    second.start()
    mine = pltpu.make_async_copy(blocks_in, weights_ref.at[tp], own_sem.at[3])
    mine.start()

    for x in range(2):
        branch_copy(x).wait_send()
    branch_across.wait_recv()
    middle = inputs_ref[...].astype(F32) + branch_out[tp].astype(F32)
    middle = middle + branch_in[near].astype(F32) + branch_in[3].astype(F32)
    middle_ref[...] = middle
    inverse_two = lax.rsqrt(jnp.mean(middle * middle, axis=-1, keepdims=True) + EPSILON)
    normed_two = (middle * inverse_two * tail[EXPERTS + 1 : EXPERTS + 2]).astype(BF16)
    normed_two_ref[...] = normed_two
    logits = nn(normed_two, packed_all_ref[:, :, 512:640].reshape(width, 128))
    logits = jnp.where(member > 0, logits, MASKED)
    grown = jnp.exp(logits - jnp.max(logits, axis=1, keepdims=True)) * member
    gates_ref[...] = grown / jnp.sum(grown, axis=1, keepdims=True)

    def pass_weights():
        first.wait_recv()
        third.start()

    def weights_ready():
        second.wait_recv()
        third.wait_recv()
        mine.wait()
        for copy in (first, second, third):
            copy.wait_send()

    def cot_ready():
        def got(k):
            main_copy(k).wait_recv()
            spare_copy(k).wait_recv()
            main_copy(k).wait_send()

        loop(1, FSDP, got)

    def sent():
        def gone(k):
            packed_copy(k).wait_send()
            outw_copy(k).wait_send()
            blocks_copy(k).wait_send()
            spare_copy(k).wait_send()

        loop(1, FSDP, gone)
        for k in range(3):
            inputs_copy(k).wait_send()
        branch_across.wait_send()

    return pass_weights, weights_ready, cot_ready, sent


def shape(dims, kind):
    return jax.ShapeDtypeStruct(dims, kind)


def dma(count):
    return pltpu.SemaphoreType.DMA((count,))


def to_column(table, count):
    n = table.shape[0]
    spread = jnp.broadcast_to(table[:, None, :], (n, count, 128)).reshape(n * count, 128)
    mine = lanes(spread.shape) == rows_of(spread.shape) % count
    return jnp.sum(jnp.where(mine, spread, 0.0), axis=1, keepdims=True)


def to_table(column, count):
    n = column.shape[0] // count
    spread = jnp.broadcast_to(column, (n * count, 128))
    mine = lanes(spread.shape) == rows_of(spread.shape) % count
    return jnp.sum(jnp.where(mine, spread, 0.0).reshape(n, count, 128), axis=1)


def expert_part(
    pass_weights, weights_ready, cot_ready, start_pairs,
    normed_two_ref, gates_ref, slot_ref, weights_ref, cot_main_ref, cot_spare_ref,
    middle_ref, cot_ref, packed_all_ref,
    out_main_ref, out_spare_ref, grads_ref, grad_middle_ref, router_part_ref, second_ref,
    hot_main_ref, hot_spare_ref,
    gate_mat, up_mat, down_mat, gate_t, row_send, spare_send, row_in, spare_in,
    back_send, back_spare_send, back_in, back_spare_in,
    hidden_ref, dgate_ref, dup_ref, ghidden_ref, sel_ref, gg_ref,
    out_in, out_spare_in,
    row_s, row_r, spare_s, spare_r, back_s, back_r, bspare_s, bspare_r,
    out_s, out_r, out_spare_s, out_spare_r,
):
    me, tp = lax.axis_index("fsdp"), lax.axis_index("tp")
    half = (me // 4) % 2
    rows, width = normed_two_ref.shape
    main = FSDP * 32

    def row_copy(k):
        return to_side(
            row_send.at[k], row_in.at[k], row_s.at[k], row_r.at[k], peer(me, k), side(tp, k)
        )

    def spare_copy(k):
        return to_side(
            spare_send.at[k], spare_in.at[k], spare_s.at[k], spare_r.at[k], peer(me, k), side(tp, k)
        )

    def back_copy(k):
        return to_side(
            back_send.at[k], back_in.at[k], back_s.at[k], back_r.at[k], giver(me, k), side(tp, k)
        )

    def bspare_copy(k):
        return to_side(
            back_spare_send.at[k],
            back_spare_in.at[k],
            bspare_s.at[k],
            bspare_r.at[k],
            giver(me, k),
            side(tp, k),
        )

    def out_copy(k):
        return to_side(
            out_main_ref.at[k], out_in.at[k], out_s.at[k], out_r.at[k], giver(me, k), side(tp, k)
        )

    def out_spare_copy(k):
        return to_side(
            out_spare_ref.at[k],
            out_spare_in.at[k],
            out_spare_s.at[k],
            out_spare_r.at[k],
            giver(me, k),
            side(tp, k),
        )

    gates_low = gates_ref[...].astype(BF16).astype(F32)
    gate_t[...] = jnp.transpose(gates_low)[:EXPERTS]

    def some_rows(i):
        experts = [peer(me, 4 * i + j) for j in range(4)]
        hot = pick(slot_ref, experts, 40)
        out = nn(hot, normed_two_ref[...])
        for j in range(4):
            k = 4 * i + j
            mine = hot[40 * j : 40 * j + 40].astype(F32)
            column = jnp.sum(mine * gate_t[pl.ds(experts[j], 1), :], axis=1, keepdims=True)
            row_send[k] = out[40 * j : 40 * j + 32].astype(BF16)
            spare_send[k, :, :1024] = out[40 * j + 32 : 40 * j + 33]
            spare_send[k, :, 1024:] = to_table(column, 40)
            hot_main_ref[k] = hot[40 * j : 40 * j + 32]
            hot_spare_ref[pl.ds(k, 1), :] = mine[32:33]

        def go(k):
            row_copy(k).start()
            spare_copy(k).start()

        loop(jnp.maximum(4 * i, 1), 4 * i + 4, go)

    loop(0, FSDP // 4, some_rows)
    row_in[0] = row_send[0]
    spare_in[0] = spare_send[0]

    pass_weights()
    weights_ready()

    def side_by_side(i):
        at = pl.ds(pl.multiple_of(128 * i, 128), 128)
        swap = 2 * lax.rem(half + i, 2)
        for j in range(TP):
            cols = slice(128 * j, 128 * j + 128)
            block = weights_ref[lax.rem(j + swap, TP), pl.ds(4 * i, 4)]
            gate_mat[at, cols] = block[:, 0:32].reshape(128, 128)
            up_mat[at, cols] = block[:, 32:64].reshape(128, 128)
            down_mat[at, cols] = block[:, 64:96].reshape(128, 128)

    loop(0, 8, side_by_side)

    cot_ready()

    def hidden_grads(i):
        cot_rows = cot_main_ref[pl.ds(8 * i, 8)].reshape(256, width)
        ghidden_ref[pl.ds(256 * i, 256), :] = nn(cot_rows, down_mat[...])

    loop(0, 4, hidden_grads)
    cot_spare = cot_spare_ref[...].reshape(FSDP, width).astype(BF16)
    ghidden_ref[pl.ds(main, FSDP), :] = nn(cot_spare, down_mat[...])

    def expert_rows(x, gate, where):
        gate_act = nn(x, gate_mat[...])
        up_act = nn(x, up_mat[...])
        grad_hidden = ghidden_ref[where, :]
        sigmoid_gate = 1.0 / (1.0 + jnp.exp(-gate_act))
        silu_gate = gate_act * sigmoid_gate
        both = silu_gate * up_act
        hidden_ref[where, :] = (both * gate).astype(BF16)
        grad_prod = grad_hidden * gate
        dgate = (
            grad_prod * up_act * sigmoid_gate * (1.0 + gate_act * (1.0 - sigmoid_gate))
        ).astype(BF16)
        dup = (grad_prod * silu_gate).astype(BF16)
        dgate_ref[where, :] = dgate
        dup_ref[where, :] = dup
        grad_in = nt(dgate, gate_mat[...]) + nt(dup, up_mat[...])
        return grad_in, jnp.sum(both * grad_hidden, axis=1, keepdims=True)

    def some_experts(i):
        def got(k):
            row_copy(k).wait_recv()
            spare_copy(k).wait_recv()

        loop(jnp.maximum(8 * i, 1), 8 * i + 8, got)
        x = row_in[pl.ds(8 * i, 8)].reshape(256, width)
        gate = to_column(spare_in[pl.ds(8 * i, 8), :, 1024:].reshape(8, 128), 32)
        grad_in, sel = expert_rows(x, gate, pl.ds(256 * i, 256))
        back_send[pl.ds(8 * i, 8)] = grad_in.astype(BF16).reshape(8, 32, width)
        sel_ref[pl.ds(8 * i, 8), :] = to_table(sel, 32)
        loop(jnp.maximum(8 * i, 1), 8 * i + 8, lambda k: back_copy(k).start())

    loop(0, 4, some_experts)
    spare = spare_in[...].reshape(FSDP, 1152)
    spare_gate = spare[:, 1056:1057]
    spare_rows = spare[:, :1024].astype(BF16)
    grad_in, sel = expert_rows(spare_rows, spare_gate, pl.ds(main, FSDP))
    sel_all = jnp.where(lanes((FSDP, 128)) == 32, sel, sel_ref[...])
    for k in range(FSDP):
        back_spare_send[k, :, :1024] = grad_in[k : k + 1]
        back_spare_send[k, :, 1024:] = sel_all[k : k + 1]
    loop(1, FSDP, lambda k: bspare_copy(k).start())
    back_in[0] = back_send[0]
    back_spare_in[0] = back_spare_send[0]

    loop(1, FSDP, lambda k: row_copy(k).wait_send())

    def outputs(i):
        out = nt(hidden_ref[pl.ds(256 * i, 256), :], down_mat[...])
        out_main_ref[pl.ds(8 * i, 8)] = out.astype(BF16).reshape(8, 32, width)

    loop(0, 4, outputs)
    out = nt(hidden_ref[pl.ds(main, FSDP), :], down_mat[...])
    for k in range(FSDP):
        out_spare_ref[k] = out[k : k + 1]
    out_in[0] = out_main_ref[0]
    out_spare_in[0] = out_spare_ref[0]

    def weight_grads(i):
        at = pl.ds(pl.multiple_of(256 * i, 256), 256)
        x = row_in[:, :, at].reshape(main, 256)
        x_spare = spare_in[:, :, at].reshape(FSDP, 256).astype(BF16)
        c = cot_main_ref[:, :, at].reshape(main, 256)
        c_spare = cot_spare_ref[:, :, at].reshape(FSDP, 256).astype(BF16)
        for m, (a, a_spare, b) in enumerate(
            ((x, x_spare, dgate_ref), (x, x_spare, dup_ref), (c, c_spare, hidden_ref))
        ):
            part = tn(a, b[pl.ds(0, main), :]) + tn(a_spare, b[pl.ds(main, FSDP), :])
            part = part.astype(BF16)
            for j in range(TP):
                for h in range(2):
                    grads_ref[
                        lax.rem(j + 2 * lax.rem(half + h, 2), TP),
                        pl.ds(8 * i + 4 * h, 4),
                        32 * m : 32 * m + 32,
                        :,
                    ] = part[128 * h : 128 * h + 128, 128 * j : 128 * j + 128].reshape(4, 32, 128)

    loop(0, 4, weight_grads)

    start_pairs()

    def back_got(k):
        back_copy(k).wait_recv()
        bspare_copy(k).wait_recv()

    loop(1, FSDP, back_got)

    def out_go(k):
        out_copy(k).start()
        out_spare_copy(k).start()

    loop(1, FSDP, out_go)
    hot = hot_main_ref[...].reshape(main, rows)
    hot_spare = hot_spare_ref[...]
    back_spare = back_spare_in[...].reshape(FSDP, 1152)
    grad_rows = tn(hot, back_in[...].reshape(main, width)) + tn(
        hot_spare.astype(BF16), back_spare[:, :1024].astype(BF16)
    )
    sel = back_spare[:, 1024:]
    by_slot = jnp.sum(
        (hot.astype(F32) * to_column(sel, 32)).reshape(FSDP, 32, rows), axis=1
    ) + hot_spare * sel[:, 32:33]
    gg_ref[...] = jnp.zeros_like(gg_ref)
    for k in range(FSDP):
        gg_ref[pl.ds(peer(me, k), 1), :] = by_slot[k : k + 1]
    grad_gates = jnp.transpose(gg_ref[...])
    gates = gates_ref[...]
    grad_chosen = gates * (grad_gates - jnp.sum(gates * grad_gates, axis=1, keepdims=True))
    grad_logits = grad_chosen.astype(BF16)
    tail = packed_all_ref[:, :, 512:640].reshape(width, 128)
    gain_two = jnp.transpose(tail.astype(F32))[EXPERTS + 1 : EXPERTS + 2]
    router_part_ref[...] = tn(normed_two_ref[...], grad_logits)
    dy = grad_rows + nt(grad_logits, tail)
    middle = middle_ref[...]
    inverse = lax.rsqrt(jnp.mean(middle * middle, axis=-1, keepdims=True) + EPSILON)
    scaled = dy * gain_two
    second_ref[...] = jnp.sum(dy * middle * inverse, axis=0, keepdims=True)
    grad_middle_ref[...] = (
        cot_ref[...].astype(F32)
        + inverse * scaled
        - middle
        * inverse
        * inverse
        * inverse
        * jnp.mean(scaled * middle, axis=-1, keepdims=True)
    )

    def out_ready():
        def got(k):
            out_copy(k).wait_recv()
            out_spare_copy(k).wait_recv()

        loop(1, FSDP, got)

    def sent():
        def gone(k):
            spare_copy(k).wait_send()
            back_copy(k).wait_send()
            bspare_copy(k).wait_send()
            out_copy(k).wait_send()
            out_spare_copy(k).wait_send()

        loop(1, FSDP, gone)

    return out_ready, sent


def backward_part(
    out_ready, pair_copy, packed_ref,
    grad_middle_ref, packed_all_ref, out_all_ref, heads_ref, normed_all_ref, attended_ref,
    cos_ref, sin_ref,
    seg_ref, grads_ref, middle_ref, hot_main_ref, hot_spare_ref,
    inputs_ref, router_part_ref, second_ref,
    output_ref, grad_inputs_ref, sums_ref, out_sums_ref, dw_in,
    branch_own, branch_all, out_in, out_spare_in, pair_in, across_send, across_in, dw_send,
    normed_send, normed_in, sums_send, sums_in, outs_send, outs_in, small_own, small_in,
    branch_s, branch_r, across_s, across_r,
    dw_s, dw_r, normed_s, normed_r, sums_s, sums_r, outs_s, outs_r, small_s, small_r,
):
    me, tp = lax.axis_index("fsdp"), lax.axis_index("tp")
    rows, width = inputs_ref.shape
    total = seg_ref.shape[1]
    core = lax.rem(tp, 2)
    sibling = tp + 1 - 2 * core
    across = lax.rem(tp + 2, TP)

    def branch_copy(k):
        block, where = ((tp, across), (tp, sibling), (across, sibling))[k]
        src = branch_own if k < 2 else branch_all.at[block]
        return to_tp(src, branch_all.at[block], branch_s.at[k], branch_r.at[k], where)

    across_copy = to_tp(across_send, across_in, across_s.at[0], across_r.at[0], across)

    def dw_copy(k):
        p = peer(me, k)
        return to_side(dw_send.at[p], dw_in.at[me], dw_s.at[k], dw_r.at[k], p, side(tp, k))

    def normed_copy(x):
        return to_tp(
            normed_send.at[2 * x + 1 - core],
            normed_in.at[x],
            normed_s.at[x],
            normed_r.at[x],
            sibling,
        )

    normed_across = to_tp(
        normed_in.at[2], normed_in.at[3], normed_s.at[2], normed_r.at[2], across
    )

    def sums_copy(k):
        p = peer(me, k)
        return to_fsdp(sums_send.at[p], sums_in.at[k], sums_s.at[k], sums_r.at[k], p)

    def outs_copy(k):
        p = peer(me, k)
        return to_fsdp(outs_send.at[p], outs_in.at[k], outs_s.at[k], outs_r.at[k], p)

    def small_copy(k):
        return to_tp(small_own, small_in.at[k], small_s.at[k], small_r.at[k], lax.rem(tp + k, TP))

    grad_middle = grad_middle_ref[...]
    branch_own[...] = grad_middle.astype(BF16)
    branch_copy(0).start()
    branch_copy(1).start()
    branch_all[tp] = branch_own[...]
    branch_copy(0).wait_recv()
    branch_copy(2).start()

    for x in range(2):
        pair_copy(x).wait_recv()
    near = tp // 2
    far = 1 - near
    across_send[...] = (
        grads_ref[2 * far + core].astype(F32) + pair_in[far].astype(F32)
    ).astype(BF16)
    across_copy.start()

    seg_row = jnp.broadcast_to(seg_ref[...].astype(F32), (128, total))
    seg_col = jnp.transpose(seg_row)[:, :1]
    allowed = (
        (seg_col == seg_row[:1]) & (rows_of((total, total)) >= lanes((total, total)))
    ).astype(F32)

    branch_copy(1).wait_recv()
    branch_copy(2).wait_recv()
    branch = branch_all[...].reshape(total, width)
    out_part = tn(branch, attended_ref[...])
    outs_send[:, :, 0:256] = out_part.astype(BF16).reshape(FSDP, 32, 256)
    second = jnp.where(rows_of((128, width)) == EXPERTS + 1, second_ref[...], 0.0)
    small = router_part_ref[...] + jnp.transpose(second)
    outs_send[:, :, 256:384] = small.astype(BF16).reshape(FSDP, 32, 128)
    loop(1, FSDP, lambda k: outs_copy(k).start())
    outs_in[0] = outs_send[me]
    grad_attended = nn(branch, out_all_ref[...].reshape(width, 256)).astype(BF16)
    scale = HEAD_SIZE ** (-0.5)
    dq, dk, dv = [], [], []
    for g in range(2):
        key = heads_ref[:, 256 + 64 * g : 320 + 64 * g]
        value = heads_ref[:, 384 + 64 * g : 448 + 64 * g]
        dk_sum, dv_sum = None, None
        for h in (2 * g, 2 * g + 1):
            q = heads_ref[:, 64 * h : 64 * h + 64]
            da = grad_attended[:, 64 * h : 64 * h + 64]
            scores = jnp.where(allowed > 0, nt(q, key) * scale, MASKED)
            top = jnp.max(scores, axis=1, keepdims=True)
            grown = jnp.exp(scores - top)
            whole = grown * (1.0 / jnp.sum(grown, axis=1, keepdims=True))
            grad_shares = nt(da, value)
            inner = jnp.sum(whole * grad_shares, axis=1, keepdims=True)
            grad_scores = (whole * (grad_shares - inner)).astype(BF16)
            dq.append(nn(grad_scores, key) * scale)
            dk_one = tn(grad_scores, q) * scale
            dv_one = tn(whole.astype(BF16), da)
            dk_sum = dk_one if dk_sum is None else dk_sum + dk_one
            dv_sum = dv_one if dv_sum is None else dv_sum + dv_one
        dk.append(dk_sum)
        dv.append(dv_sum)
    turned = jnp.concatenate(dq + dk, axis=1)
    turn = turned * wide_table(cos_ref[...], 384) - half_swap(turned) * wide_table(
        sin_ref[...], 384
    )
    grad_lin = jnp.concatenate([turn] + dv, axis=1).astype(BF16)
    qkv_part = tn(normed_all_ref[...], grad_lin)
    sums_send[...] = qkv_part.astype(BF16).reshape(FSDP, 32, 512)
    loop(1, FSDP, lambda k: sums_copy(k).start())
    sums_in[0] = sums_send[me]

    grad_normed = nt(grad_lin, packed_all_ref[:, :, 0:512].reshape(width, 512))
    normed_send[...] = grad_normed.astype(BF16).reshape(TP, rows, width)
    for x in range(2):
        normed_copy(x).start()
    gain_one = jnp.transpose(packed_all_ref[:, :, 512:640].reshape(width, 128).astype(F32))[
        EXPERTS : EXPERTS + 1
    ]

    across_copy.wait_recv()
    dw_send[...] = (
        grads_ref[tp].astype(F32) + pair_in[near].astype(F32) + across_in[...].astype(F32)
    ).astype(BF16)
    loop(1, FSDP, lambda k: dw_copy(k).start())
    dw_in[me] = dw_send[me]

    for x in range(2):
        normed_copy(x).wait_recv()
    normed_in[2] = (
        normed_send[across].astype(F32) + normed_in[far].astype(F32)
    ).astype(BF16)
    normed_across.start()

    normed_across.wait_recv()
    dy = normed_send[tp].astype(F32) + normed_in[near].astype(F32) + normed_in[3].astype(F32)
    wide = inputs_ref[...].astype(F32)
    inverse = lax.rsqrt(jnp.mean(wide * wide, axis=-1, keepdims=True) + EPSILON)
    scaled = dy * gain_one
    grad_inputs_ref[...] = (
        grad_middle
        + inverse * scaled
        - wide
        * inverse
        * inverse
        * inverse
        * jnp.mean(scaled * wide, axis=-1, keepdims=True)
    )

    out_ready()
    hot = hot_main_ref[...].reshape(FSDP * 32, rows)
    output_ref[...] = (
        middle_ref[...]
        + tn(hot, out_in[...].reshape(FSDP * 32, width))
        + tn(hot_spare_ref[...].astype(BF16), out_spare_in[...].reshape(FSDP, width).astype(BF16))
    ).astype(BF16)

    loop(1, FSDP, lambda k: sums_copy(k).wait_recv())
    sums = jnp.sum(sums_in[...].astype(F32), axis=0)
    sums_ref[:, :512] = sums
    loop(1, FSDP, lambda k: outs_copy(k).wait_recv())
    out_sums = jnp.sum(outs_in[...].astype(F32), axis=0)
    out_sums_ref[...] = out_sums[:, :256]
    first = jnp.sum(packed_ref[:, :512].astype(F32) * sums, axis=1, keepdims=True)
    first = first / packed_ref[:, 544:545].astype(F32)
    small_own[...] = out_sums[:, 256:] + jnp.where(lanes((32, 128)) == EXPERTS, first, 0.0)
    for k in (2, 1, 3):
        small_copy(k).start()
    loop(1, FSDP, lambda k: dw_copy(k).wait_recv())
    for k in range(1, TP):
        small_copy(k).wait_recv()
    sums_ref[:, 512:] = small_own[...] + small_in[1] + small_in[2] + small_in[3]

    def gone(k):
        sums_copy(k).wait_send()
        outs_copy(k).wait_send()
        dw_copy(k).wait_send()

    loop(1, FSDP, gone)
    for k in range(3):
        branch_copy(k).wait_send()
        small_copy(k + 1).wait_send()
    for x in range(2):
        normed_copy(x).wait_send()
        pair_copy(x).wait_send()
    normed_across.wait_send()
    across_copy.wait_send()


def layer_kernel(
    query_ref, key_ref, value_ref, out_weight_ref, router_ref, first_gain_ref, second_gain_ref,
    gate_ref, up_ref, down_ref, inputs_ref, seg_ref, routes_ref, cot_ref,
    output_ref, grad_inputs_ref, sums_ref, out_sums_ref, weight_grads_ref,
    middle, normed_two, gates, slot, weights, cot_main, cot_spare, packed_all, out_all,
    heads, normed_all, attended, cosine, sine,
    packed, blocks, inputs_all, blocks_in, rows_out, spare_out, branch_out, branch_in,
    router_part, second_part, hot_main, hot_spare, grad_middle, out_spare,
    gate_mat, up_mat, down_mat, gate_t, row_send, spare_send, row_in, spare_in,
    back_spare_send, back_in, back_spare_in,
    hidden, dgate, dup, ghidden, sel, gate_grads, out_in, out_spare_in,
    branch_own, branch_all, pair_in, across_send, across_in, dw_send, normed_in,
    sums_send, sums_in, outs_send, outs_in, small_own, small_in,
    *sems,
):
    tp = lax.axis_index("tp")
    sems = list(sems)

    def take(count):
        taken = sems[:count]
        del sems[:count]
        return taken

    pass_weights, weights_ready, cot_ready, forward_sent = forward_part(
        query_ref, key_ref, value_ref, out_weight_ref, router_ref, first_gain_ref,
        second_gain_ref, gate_ref, up_ref, down_ref, inputs_ref, seg_ref, routes_ref, cot_ref,
        middle, normed_two, gates, slot, weights, cot_main, cot_spare,
        packed_all, out_all, heads, normed_all, attended, cosine, sine,
        packed, blocks, inputs_all, blocks_in, rows_out, spare_out, branch_out, branch_in,
        *take(17),
    )
    core = lax.rem(tp, 2)
    pair_s, pair_r = take(2)

    def pair_copy(x):
        return to_tp(
            weights.at[2 * x + 1 - core],
            pair_in.at[x],
            pair_s.at[x],
            pair_r.at[x],
            tp + 1 - 2 * core,
        )

    def start_pairs():
        for x in range(2):
            pair_copy(x).start()

    out_ready, expert_sent = expert_part(
        pass_weights, weights_ready, cot_ready, start_pairs,
        normed_two, gates, slot, weights, cot_main, cot_spare, middle, cot_ref,
        packed_all,
        row_send, out_spare, weights, grad_middle, router_part, second_part, hot_main, hot_spare,
        gate_mat, up_mat, down_mat, gate_t, row_send, spare_send, row_in, spare_in,
        rows_out, back_spare_send, back_in, back_spare_in,
        hidden, dgate, dup, ghidden, sel, gate_grads, out_in, out_spare_in,
        *take(12),
    )
    backward_part(
        out_ready, pair_copy, packed,
        grad_middle, packed_all, out_all, heads, normed_all, attended, cosine, sine, seg_ref,
        weights, middle, hot_main, hot_spare, inputs_ref, router_part, second_part,
        output_ref, grad_inputs_ref, sums_ref, out_sums_ref, weight_grads_ref,
        branch_own, branch_all, out_in, out_spare_in, pair_in, across_send, across_in,
        dw_send, branch_out, normed_in, sums_send, sums_in, outs_send, outs_in,
        small_own, small_in,
        *take(14),
    )
    forward_sent()
    expert_sent()


def layer(*operands):
    inputs, seg = operands[10], operands[11]
    rows, width = inputs.shape
    total = seg.shape[1]
    packed_shape, out_shape, blocks_shape = (32, 640), (32, 256), (EXPERTS, 96, 128)
    hidden = 128 * TP
    slots = FSDP * SPARE
    vmem = pl.BlockSpec(memory_space=pltpu.VMEM)
    out = (
        shape((rows, width), BF16),
        shape((rows, width), F32),
        shape(packed_shape, F32),
        shape(out_shape, F32),
        shape(blocks_shape, BF16),
    )
    block = pltpu.VMEM((FSDP, 32, width), BF16)
    spare = pltpu.VMEM((FSDP, 1, width), F32)
    spare_wide = pltpu.VMEM((FSDP, 1, width + 128), F32)
    four = pltpu.VMEM((TP, rows, width), BF16)
    shards = pltpu.VMEM(blocks_shape, BF16)
    packs = pltpu.VMEM((FSDP, *packed_shape), BF16)
    outs = pltpu.VMEM((FSDP, *out_shape), BF16)
    return pl.pallas_call(
        layer_kernel,
        out_shape=out,
        in_specs=[vmem] * len(operands),
        out_specs=[vmem] * len(out),
        scratch_shapes=[
            pltpu.VMEM((rows, width), F32),
            pltpu.VMEM((rows, width), BF16),
            pltpu.VMEM((rows, 128), F32),
            pltpu.VMEM((EXPERTS, rows), F32),
            pltpu.VMEM((TP, *blocks_shape), BF16),
            block,
            spare,
            packs,
            outs,
            pltpu.VMEM((total, 512), BF16),
            pltpu.VMEM((total, width), BF16),
            pltpu.VMEM((total, 256), BF16),
            pltpu.VMEM((total, 128), F32),
            pltpu.VMEM((total, 128), F32),
            pltpu.VMEM(packed_shape, BF16),
            shards,
            four,
            shards,
            block,
            spare,
            four,
            four,
            pltpu.VMEM((width, 128), F32),
            pltpu.VMEM((1, width), F32),
            pltpu.VMEM((FSDP, 32, rows), BF16),
            pltpu.VMEM((FSDP, rows), F32),
            pltpu.VMEM((rows, width), F32),
            spare,
            *[pltpu.VMEM((width, hidden), BF16)] * 3,
            pltpu.VMEM((EXPERTS, rows), F32),
            block,
            spare_wide,
            block,
            spare_wide,
            spare_wide,
            block,
            spare_wide,
            *[pltpu.VMEM((slots, hidden), BF16)] * 3,
            pltpu.VMEM((slots, hidden), F32),
            pltpu.VMEM((FSDP, 128), F32),
            pltpu.VMEM((128, 128), F32),
            block,
            spare,
            pltpu.VMEM((rows, width), BF16),
            four,
            pltpu.VMEM((2, *blocks_shape), BF16),
            *[shards] * 3,
            four,
            *[pltpu.VMEM((FSDP, 32, 512), BF16)] * 2,
            *[pltpu.VMEM((FSDP, 32, 384), BF16)] * 2,
            pltpu.VMEM((32, 128), F32),
            pltpu.VMEM((TP, 32, 128), F32),
            *[dma(FSDP)] * 10,
            *[dma(TP)] * 6,
            dma(5),
            *[dma(2)] * 2,
            *[dma(FSDP)] * 12,
            *[dma(TP)] * 2,
            *[dma(1)] * 2,
            *[dma(FSDP)] * 2,
            *[dma(TP)] * 2,
            *[dma(FSDP)] * 4,
            *[dma(TP)] * 2,
        ],
        compiler_params=pltpu.CompilerParams(
            collective_id=1, has_side_effects=True, vmem_limit_bytes=62 * 2**20
        ),
        name="layer",
    )(*operands)


def finish_kernel(
    output_in, grad_inputs_in, sums_ref, out_sums_ref, weight_grads_ref,
    output_ref, grad_inputs_ref, query_ref, key_ref, value_ref, out_ref, router_ref,
    gains_ref, gate_ref, up_ref, down_ref,
):
    output_ref[...] = output_in[...]
    grad_inputs_ref[...] = grad_inputs_in[...]
    query_ref[...] = sums_ref[:, 0:256]
    key_ref[...] = sums_ref[:, 256:384]
    value_ref[...] = sums_ref[:, 384:512]
    out_ref[...] = out_sums_ref[...]
    router_ref[...] = sums_ref[:, 512:544]
    tail = jnp.concatenate([sums_ref[:, 512:640], jnp.zeros((96, 128), F32)], axis=0)
    gains_ref[...] = jnp.transpose(tail)[EXPERTS : EXPERTS + 8, :32]
    gate_ref[...] = weight_grads_ref[:, 0:32].astype(F32)
    up_ref[...] = weight_grads_ref[:, 32:64].astype(F32)
    down_ref[...] = weight_grads_ref[:, 64:96].astype(F32)


def finish(*operands):
    vmem = pl.BlockSpec(memory_space=pltpu.VMEM)
    shard = shape((EXPERTS, 32, 128), F32)
    out = (
        shape(operands[0].shape, BF16),
        shape(operands[1].shape, F32),
        shape((32, 256), F32),
        shape((32, 128), F32),
        shape((32, 128), F32),
        shape((32, 256), F32),
        shape((32, 32), F32),
        shape((8, 32), F32),
        shard,
        shard,
        shard,
    )
    return pl.pallas_call(
        finish_kernel,
        out_shape=out,
        in_specs=[vmem] * len(operands),
        out_specs=[vmem] * len(out),
        compiler_params=pltpu.CompilerParams(vmem_limit_bytes=60 * 2**20),
        name="finish",
    )(*operands)


def per_device(
    inputs,
    segments,
    routes,
    query_weight,
    key_projection_weight,
    value_projection_weight,
    out_weight,
    router_weight,
    first_gain,
    second_gain,
    gate_weight,
    up_weight,
    down_weight,
    cotangent,
):
    parts = layer(
        query_weight,
        key_projection_weight,
        value_projection_weight,
        out_weight.T,
        router_weight,
        first_gain[None, :],
        second_gain[None, :],
        gate_weight,
        up_weight,
        jnp.transpose(down_weight, (0, 2, 1)),
        inputs,
        segments,
        routes.T,
        cotangent,
    )
    (
        output, grad_inputs, grad_query, grad_key, grad_value, grad_out, grad_router,
        grad_gains, grad_gate, grad_up, grad_down,
    ) = finish(*parts)
    return (
        output,
        grad_inputs,
        grad_query,
        grad_key,
        grad_value,
        grad_out.T,
        grad_router,
        grad_gains[0],
        grad_gains[1],
        grad_gate,
        grad_up,
        jnp.transpose(grad_down, (0, 2, 1)),
    )


def solution(mesh):
    return jax.shard_map(
        per_device,
        mesh=mesh,
        in_specs=(
            P(("fsdp", "tp"), None),
            P("fsdp", None),
            P("fsdp", None),
            P("fsdp", "tp"),
            P("fsdp", "tp"),
            P("fsdp", "tp"),
            P("tp", "fsdp"),
            P("fsdp", None),
            P("fsdp"),
            P("fsdp"),
            P(None, "fsdp", "tp"),
            P(None, "fsdp", "tp"),
            P(None, "tp", "fsdp"),
            P(("fsdp", "tp"), None),
        ),
        out_specs=(
            P(("fsdp", "tp"), None),
            P(("fsdp", "tp"), None),
            P("fsdp", "tp"),
            P("fsdp", "tp"),
            P("fsdp", "tp"),
            P("tp", "fsdp"),
            P("fsdp", None),
            P("fsdp"),
            P("fsdp"),
            P(None, "fsdp", "tp"),
            P(None, "fsdp", "tp"),
            P(None, "tp", "fsdp"),
        ),
        check_vma=False,
    )
```
